32 devices in a mesh: dx: 4 (over z), dy: 8 (over y, x, core).
Axes of the slice: x: 2, y: 2, z: 4, core: 2. Of those that a mesh axis runs over, the one named last changes fastest.
Arguments:
- orbitals: bfloat16 [56, 112, 13, 256], P('dx', 'dy'), may hold values from -6 to 6
- elem_mats: bfloat16 [8, 16, 2, 512, 512], P('dx', 'dy'), as said below
- conn: int32 [8, 16, 2, 512], P('dx', 'dy'), may hold values from 0 to 3374, as said below
Outputs:
- filtered: float32 [56, 112, 13, 256], P('dx', 'dy')
The draws below stay inside these ranges and needn't reach their ends.
Inputs may be any that keep to these rules, and one draw needn't show every extreme that they name: conn[e1, e2, e3, k] is ((7 (e1 mod 2) + a) (15) + 7 (e2 mod 2) + b) * 15 + 7 e3 + c for a node (a, b, c) of the element, 0 <= a, b, c <= 7, and each of the element's 512 nodes appears exactly once. `elem_mats`: each element's matrix is symmetric.
All inputs are finite; a program needn't handle non-finite values.
Results may differ from the reference program's by a relative error of at most 0.0059.
Values may be sent and summed in bfloat16 or wider, within the bound.
No kernel may reach another device: no remote copies, remote signals or barrier semaphores. Data moves between devices by JAX's collectives and lax.ppermute only.
A program may use at most 128 MiB of HBM per device.

```python
import math
import jax
import jax.numpy as jnp
from jax import lax

BANDS = 256
DEG = 7
ESIDE = 2
EZ = 2
NPE = 512
NZO = 13
NZE = 15
NEX = 8
NEY = 16
NX = 56
NY = 112
N_DX = 4
N_DY = 8


def draw_conn(key, part):
    count = NEX * NEY * EZ
    keys = jax.random.split(jax.random.fold_in(key, 11), count)
    orders = jax.vmap(lambda single: jax.random.permutation(single, NPE))(keys).reshape(NEX, NEY, EZ, NPE)
    side = DEG + 1
    node_ids = jnp.arange(NPE, dtype=jnp.int32)
    first = node_ids // (side * side)
    second = node_ids // side % side
    third = node_ids % side
    along_x = (jnp.arange(NEX, dtype=jnp.int32) % ESIDE)[:, None, None, None]
    along_y = (jnp.arange(NEY, dtype=jnp.int32) % ESIDE)[None, :, None, None]
    along_z = jnp.arange(EZ, dtype=jnp.int32)[None, None, :, None]
    width = ESIDE * DEG + 1
    base = ((DEG * along_x + first) * width + DEG * along_y + second) * NZE + DEG * along_z + third
    base = jnp.broadcast_to(base, (NEX, NEY, EZ, NPE))
    return jnp.take_along_axis(base, orders.astype(jnp.int32), axis=3).astype(jnp.int32)


def draw_elem_mats(key, part):
    keys = jax.random.split(jax.random.fold_in(key, 5), NEX)

    def slab(single):
        noise_key, diag_key = jax.random.split(single, 2)
        noise = jax.random.normal(noise_key, (NEY, EZ, NPE, NPE), jnp.float32)
        matrix = (noise + jnp.swapaxes(noise, 2, 3)) * (1.0 / math.sqrt(2.0 * NPE))
        diagonal = jax.random.uniform(diag_key, (NEY, EZ, NPE), jnp.float32, 0.5, 2.5)
        matrix = matrix + diagonal[..., None] * jnp.eye(NPE, dtype=jnp.float32)
        return matrix.astype(jnp.bfloat16)
    return lax.map(slab, keys)


def steps_of(stream_key, dims, pieces, smallest, high):
    def one(axis_at, blocks):
        draws = jax.random.uniform(jax.random.fold_in(jax.random.fold_in(stream_key, 6), axis_at), (blocks,), jnp.float32, smallest / len(pieces), high / len(pieces))
        return jnp.repeat(jnp.exp(draws), dims[axis_at] // blocks).reshape((-1,) + (1,) * (len(dims) - axis_at - 1))

    gain = one(*pieces[0])
    for cut in pieces[1:]:
        gain = gain * one(*cut)
    return gain


def gaussian(key, shape, spread, most, cuts=(), kind=jnp.bfloat16):
    result = jax.random.normal(key, shape, jnp.float32) * spread
    if len(cuts) > 0:
        result = steps_of(key, shape, cuts, -0.22, 0.18) * result
    return jnp.clip(result, min=-most, max=most).astype(kind)


def setup_inputs(seed: int = 0) -> dict:
    streams_of = jax.random.split(jax.random.key(seed), 4)
    orbitals = gaussian(streams_of[0], (NX, NY, NZO, BANDS), 1.0, 6.0, ((0, 4), (1, 8)))
    elem_mats = draw_elem_mats(jax.random.fold_in(streams_of[3], 71), 0)
    conn = draw_conn(jax.random.fold_in(streams_of[3], 71), 0)
    return {"orbitals": orbitals, "elem_mats": elem_mats, "conn": conn}


filter_center = 1.5
filter_half = 4.0

def local_apply(block, mats_dev, conn_dev):
    rows = block[conn_dev]
    product = jnp.einsum('eij,ejb->eib', mats_dev.astype(jnp.float32), rows.astype(jnp.float32))
    summed = jnp.zeros((block.shape[0], block.shape[1]), jnp.float32)
    return summed.at[conn_dev.reshape(-1)].add(product.reshape(-1, block.shape[1]))

def apply_operator(field, elem_mats, conn):
    edge = ESIDE * DEG
    width = edge + 1
    padded = jnp.pad(field, ((1, 0), (1, 0), (1, 1), (0, 0)))
    start_sum = jnp.zeros(padded.shape, jnp.float32)

    def visit(index, summed):
        row = (index // N_DY).astype(jnp.int32)
        col = (index % N_DY).astype(jnp.int32)
        zero = jnp.zeros((), jnp.int32)
        start = (row * edge, col * edge, zero, zero)
        block = lax.dynamic_slice(padded, start, (width, width, NZE, BANDS)).reshape(-1, BANDS)
        mats_dev = lax.dynamic_slice(elem_mats, (row * ESIDE, col * ESIDE, zero, zero, zero), (ESIDE, ESIDE, EZ, NPE, NPE)).reshape(-1, NPE, NPE)
        conn_dev = lax.dynamic_slice(conn, (row * ESIDE, col * ESIDE, zero, zero), (ESIDE, ESIDE, EZ, NPE)).reshape(-1, NPE).astype(jnp.int32)
        piece = local_apply(block, mats_dev, conn_dev).reshape(width, width, NZE, BANDS)
        current = lax.dynamic_slice(summed, start, (width, width, NZE, BANDS))
        return lax.dynamic_update_slice(summed, current + piece, start)
    summed = lax.fori_loop(0, N_DX * N_DY, visit, start_sum)
    return summed[1:, 1:, 1:-1]

def reference(orbitals, elem_mats, conn):
    previous = orbitals.astype(jnp.float32)
    image = apply_operator(orbitals, elem_mats, conn)
    current = (image - filter_center * previous) / filter_half
    for turn in range(2):
        field = lax.optimization_barrier(current.astype(jnp.bfloat16))
        image = apply_operator(field, elem_mats, conn)
        following = 2.0 * (image - filter_center * current) / filter_half - previous
        previous, current = (current, following)
    matrix = current.reshape(-1, BANDS)
    basis, upper = jnp.linalg.qr(matrix)
    basis = basis * jnp.sign(jnp.diagonal(upper))[None, :]
    scale = math.sqrt(matrix.shape[0])
    return (basis * scale).reshape(current.shape)
```

```python
import functools
import math

import jax
import jax.numpy as jnp
from jax import lax
from jax.experimental import pallas as pl
from jax.experimental.pallas import tpu as pltpu
from jax.sharding import PartitionSpec as P

filter_center = 1.5
filter_half = 4.0
AXES = ("dx", "dy")
VMEM = pl.BlockSpec(memory_space=pltpu.VMEM)
LIMIT = 48 * 1024 * 1024
LANES = 128


def partner(index, size, pairing):
    if pairing == "-":
        return index
    other = index ^ 1 if pairing == "A" else index - 1 if index % 2 == 0 else index + 1
    return other if 0 <= other < size else index


def pair_swap(value, along_x, along_y):
    size_x, size_y = lax.axis_size("dx"), lax.axis_size("dy")
    route = [
        (p * size_y + q, partner(p, size_x, along_x) * size_y + partner(q, size_y, along_y))
        for p in range(size_x)
        for q in range(size_y)
    ]
    return lax.ppermute(value, AXES, route)


def offset(value, step_x, step_y):
    size_x, size_y = lax.axis_size("dx"), lax.axis_size("dy")
    route = [
        (p * size_y + q, (p + step_x) * size_y + q + step_y)
        for p in range(size_x)
        for q in range(size_y)
        if 0 <= p + step_x < size_x and 0 <= q + step_y < size_y
    ]
    return lax.ppermute(value, AXES, route)


def xor_swap(value, axis, bits):
    return lax.ppermute(value, axis, [(i, i ^ bits) for i in range(lax.axis_size(axis))])


def total(gram):
    sizes = [lax.axis_size(axis) for axis in AXES]
    if any(size & (size - 1) or size < 2 for size in sizes):
        return lax.psum(gram, AXES)
    half = gram.shape[0] // 2
    odd = lax.axis_index("dy") % 2
    kept = lax.dynamic_slice_in_dim(gram, odd * half, half, 0)
    sent = lax.dynamic_slice_in_dim(gram, (1 - odd) * half, half, 0)
    part = kept + xor_swap(sent, "dy", 1)
    for axis, first in (("dx", 1), ("dy", 2)):
        bit = first
        while bit < lax.axis_size(axis):
            if 2 * bit < lax.axis_size(axis):
                one, two, three = [xor_swap(part, axis, bit * k) for k in (1, 2, 3)]
                part = (part + one) + (two + three)
                bit *= 4
            else:
                part = part + xor_swap(part, axis, bit)
                bit *= 2
    other = xor_swap(part, "dy", 1)
    low = jnp.where(odd == 0, part, other)
    high = jnp.where(odd == 0, other, part)
    return jnp.concatenate([low, high], axis=0)


def renumber_kernel(conn_ref, mats_ref, out_ref, *, side, width, depth, layers):
    e1, e2, e3 = (pl.program_id(k) for k in range(3))
    deg = side - 1
    rows = conn_ref[0, 0]
    node = rows[0:1]
    for k in range(1, layers):
        node = jnp.where(e3 == k, rows[k : k + 1], node)
    node = node.astype(jnp.float32)
    plane = jnp.floor((node + 0.5) * (1.0 / depth))
    first = jnp.floor((plane + 0.5) * (1.0 / width))
    c = (node - plane * depth).astype(jnp.int32) - deg * e3
    b = (plane - first * width).astype(jnp.int32) - deg * e2
    a = first.astype(jnp.int32) - deg * e1
    place = (a * side + c) * side + b
    a = jnp.where((e1 == 0) & (lax.axis_index("dx") == 0), a, 1)
    b = jnp.where((e2 == 0) & (lax.axis_index("dy") == 0), b, 1)
    c_low = jnp.where(e3 == 0, c, 1)
    c_high = jnp.where(e3 == layers - 1, c, 1)
    held = (a == 0) | (b == 0) | (c_low == 0) | (c_high == deg)
    place = jnp.where(held, -1, place)
    count = mats_ref.shape[-1]
    order = lax.broadcasted_iota(jnp.int32, (count, count), 0) == place
    order = jnp.where(order, 1.0, 0.0).astype(jnp.bfloat16)
    half = jnp.dot(order, mats_ref[0, 0, 0], preferred_element_type=jnp.float32)
    whole = lax.dot_general(
        half.astype(jnp.bfloat16),
        order,
        (((1,), (1,)), ((), ())),
        preferred_element_type=jnp.float32,
    )
    out_ref[0, 0, 0] = whole.astype(jnp.bfloat16)


def renumber(conn, elem_mats, side, width, depth):
    ex, ey, layers, count, _ = elem_mats.shape
    spot = pl.BlockSpec((1, 1, 1, count, count), lambda i, j, k: (i, j, k, 0, 0))
    return pl.pallas_call(
        functools.partial(renumber_kernel, side=side, width=width, depth=depth, layers=layers),
        out_shape=jax.ShapeDtypeStruct(elem_mats.shape, jnp.bfloat16),
        grid=(ex, ey, layers),
        in_specs=[pl.BlockSpec((1, 1, layers, count), lambda i, j, k: (i, j, 0, 0)), spot],
        out_specs=spot,
        compiler_params=pltpu.CompilerParams(vmem_limit_bytes=LIMIT),
        cost_estimate=pl.CostEstimate(
            flops=4 * ex * ey * layers * count**3,
            bytes_accessed=4 * elem_mats.size,
            transcendentals=0,
        ),
        name="renumber",
    )(conn, elem_mats)


class Grid:
    def __init__(self, elem_mats, side):
        self.ex, self.ey, self.ez = elem_mats.shape[:3]
        self.count = elem_mats.shape[3]
        self.side = side
        self.deg = side - 1
        self.nz = self.ez * self.deg - 1
        self.elements = self.ex * self.ey * self.ez

    def at(self, e1, e2, e3):
        return (e1 * self.ey + e2) * self.ez + e3

    def rows(self, a, c, number):
        start = (a * self.side + c) * self.side
        return slice(start, start + number * self.side)

    def layers(self, e3):
        low = 1 if e3 == 0 else 0
        high = self.deg - 1 if e3 == self.ez - 1 else self.deg
        return low, high - low + 1, e3 * self.deg + low - 1

    def side_rows(self, b):
        return pl.ds(b, self.side * self.side, stride=self.side)

    def line_rows(self, a, b):
        return pl.ds(a * self.side * self.side + b, self.side, stride=self.side)


def lanes(h):
    return slice(h * LANES, (h + 1) * LANES)


def multiply(g, mats_ref, field_of, w_ref):
    side, deg = g.side, g.deg
    halves = range(w_ref.shape[1])
    for e in range(g.elements):
        product = jnp.dot(mats_ref[e], field_of(e), preferred_element_type=jnp.float32)
        for h in halves:
            w_ref[e, h] = product[:, lanes(h)]

    def join(one, top, two, bottom):
        for h in halves:
            both = w_ref[one, h, top] + w_ref[two, h, bottom]
            w_ref[one, h, top] = both
            w_ref[two, h, bottom] = both

    for e1 in range(g.ex):
        for e2 in range(g.ey):
            for e3 in range(g.ez - 1):
                for a in range(side):
                    one, two = g.at(e1, e2, e3), g.at(e1, e2, e3 + 1)
                    join(one, g.rows(a, deg, 1), two, g.rows(a, 0, 1))
    for e1 in range(g.ex - 1):
        for e2 in range(g.ey):
            for e3 in range(g.ez):
                one, two = g.at(e1, e2, e3), g.at(e1 + 1, e2, e3)
                join(one, g.rows(deg, 0, side), two, g.rows(0, 0, side))
    for e1 in range(g.ex):
        for e2 in range(g.ey - 1):
            for e3 in range(g.ez):
                one, two = g.at(e1, e2, e3), g.at(e1, e2 + 1, e3)
                join(one, g.side_rows(deg), two, g.side_rows(0))


def put_x_face(g, w_ref, put):
    for h in range(w_ref.shape[1]):
        for e2 in range(g.ey):
            for e3 in range(g.ez):
                low, number, start = g.layers(e3)
                if e3 > 0:
                    low, number, start = low + 1, number - 1, start + 1
                one = w_ref[g.at(0, e2, e3), h, g.rows(0, low, number)]
                two = w_ref[g.at(g.ex - 1, e2, e3), h, g.rows(g.deg, low, number)]
                where = (
                    slice(start, start + number),
                    slice(e2 * g.side, (e2 + 1) * g.side),
                    lanes(h),
                )
                shape = (number, g.side, LANES)
                put(where, one.reshape(shape), two.reshape(shape))


def put_y_face(g, w_ref, put):
    for h in range(w_ref.shape[1]):
        for e1 in range(g.ex):
            for e3 in range(g.ez):
                one = w_ref[g.at(e1, 0, e3), h, g.side_rows(0)]
                two = w_ref[g.at(e1, g.ey - 1, e3), h, g.side_rows(g.deg)]
                put((e1 * g.ez + e3, slice(None), lanes(h)), one, two)


def line(g, w_ref, high_x, high_y, e3, h):
    e1, a = (g.ex - 1, g.deg) if high_x else (0, 0)
    e2, b = (g.ey - 1, g.deg) if high_y else (0, 0)
    return w_ref[g.at(e1, e2, e3), h, g.line_rows(a, b)]


def add_x_face(g, out_ref, high, received, factor):
    e1, a = (g.ex - 1, g.deg) if high else (0, 0)
    for h in range(out_ref.shape[1]):
        for e2 in range(g.ey):
            for e3 in range(g.ez):
                low, number, start = g.layers(e3)
                columns = slice(e2 * g.side, (e2 + 1) * g.side)
                part = received((slice(start, start + number), columns, lanes(h)))
                rows = g.rows(a, low, number)
                part = part.reshape(number * g.side, LANES)
                out_ref[g.at(e1, e2, e3), h, rows] += factor * part


def add_y_face(g, out_ref, high, received, factor):
    e2, b = (g.ey - 1, g.deg) if high else (0, 0)
    for h in range(out_ref.shape[1]):
        for e1 in range(g.ex):
            for e3 in range(g.ez):
                part = received((e1 * g.ez + e3, slice(None), lanes(h)))
                out_ref[g.at(e1, e2, e3), h, g.side_rows(b)] += factor * part


def add_line(g, out_ref, high_x, high_y, received, factor):
    e1, a = (g.ex - 1, g.deg) if high_x else (0, 0)
    e2, b = (g.ey - 1, g.deg) if high_y else (0, 0)
    for h in range(out_ref.shape[1]):
        for e3 in range(g.ez):
            part = received((slice(e3 * g.side, (e3 + 1) * g.side), lanes(h)))
            out_ref[g.at(e1, e2, e3), h, g.line_rows(a, b)] += factor * part


def send_all(g, w_ref, sends):
    even_x = lax.axis_index("dx") % 2 == 0
    even_y = lax.axis_index("dy") % 2 == 0

    def by_pair(even, one_ref, two_ref):
        def put(where, low, high):
            one_ref[where] = jnp.where(even, high, low)
            two_ref[where] = jnp.where(even, low, high)

        return put

    put_x_face(g, w_ref, by_pair(even_x, sends[0], sends[1]))
    put_y_face(g, w_ref, by_pair(even_y, sends[2], sends[3]))
    for h in range(w_ref.shape[1]):
        for e3 in range(g.ez):
            where = (slice(e3 * g.side, (e3 + 1) * g.side), lanes(h))
            at_x = [[line(g, w_ref, hx, hy, e3, h) for hy in (0, 1)] for hx in (0, 1)]
            for my in (0, 1):
                low, high = [jnp.where(even_y, at_x[hx][1 - my], at_x[hx][my]) for hx in (0, 1)]
                by_pair(even_x, sends[4 + my], sends[6 + my])(where, low, high)


def add_all(g, out_ref, received, factor):
    p, q = lax.axis_index("dx"), lax.axis_index("dy")
    even_x, even_y = p % 2 == 0, q % 2 == 0
    has_x = (p > 0, p < lax.axis_size("dx") - 1)
    has_y = (q > 0, q < lax.axis_size("dy") - 1)

    def from_pair(even, high, one, two, exists):
        value = jnp.where(even, one, two) if high else jnp.where(even, two, one)
        return jnp.where(exists, value, 0.0)

    for high in (0, 1):

        def across_x(where):
            return from_pair(even_x, high, received[0][where], received[1][where], has_x[high])

        def across_y(where):
            return from_pair(even_y, high, received[2][where], received[3][where], has_y[high])

        add_x_face(g, out_ref, high, across_x, factor)
        add_y_face(g, out_ref, high, across_y, factor)
    for hx in (0, 1):
        for hy in (0, 1):

            def diagonal(where):
                one = from_pair(even_y, hy, received[4][where], received[5][where], has_y[hy])
                two = from_pair(even_y, hy, received[6][where], received[7][where], has_y[hy])
                return from_pair(even_x, hx, one, two, has_x[hx])

            add_line(g, out_ref, hx, hy, diagonal, factor)


def field_of(y_ref, e):
    parts = [y_ref[e, h].astype(jnp.bfloat16) for h in range(y_ref.shape[1])]
    return jnp.concatenate(parts, axis=-1)


def first_kernel(*refs, g):
    orb_ref, below_x, below_y, below_xy, mats_ref, y_ref, w_ref, *sends = refs
    side = g.side
    halves = range(y_ref.shape[1])
    sub = lax.broadcasted_iota(jnp.int32, (side, LANES), 0)
    nothing = jnp.zeros((side, LANES), jnp.float32)
    rest = orb_ref.shape[2] - side
    for e1 in range(g.ex):
        for e2 in range(g.ey):
            for a in range(side):
                for h in halves:
                    y_ref[g.at(e1, e2, 0), h, g.rows(a, 0, 1)] = nothing
                    y_ref[g.at(e1, e2, g.ez - 1), h, g.rows(a, g.deg, 1)] = nothing

    def place(i, k, column, edge):
        for h in halves:
            part = column[:, lanes(h)].astype(jnp.float32)
            t0 = part[:side]
            t1 = jnp.concatenate([part[side:], nothing[: side - rest]], axis=0)
            first = jnp.broadcast_to(edge[:, lanes(h)].astype(jnp.float32), (side, LANES))
            d0 = jnp.where(sub == 0, first, pltpu.roll(t0, 1, 0))
            d1 = jnp.where(sub < 2, pltpu.roll(t0, 2, 0), pltpu.roll(t1, 2, 0))
            for e1 in range(g.ex):
                a = i - e1 * g.deg
                for e3 in range(g.ez):
                    c = k + 1 - e3 * g.deg
                    if 0 <= a <= g.deg and 0 <= c <= g.deg:
                        y_ref[g.at(e1, 0, e3), h, g.rows(a, c, 1)] = d0
                        y_ref[g.at(e1, 1, e3), h, g.rows(a, c, 1)] = d1

    for k in range(g.nz):
        place(0, k, below_x[k], below_xy[k : k + 1])
        for i in range(orb_ref.shape[0]):
            place(i + 1, k, orb_ref[i, k], below_y[i, k : k + 1])
    multiply(g, mats_ref, functools.partial(field_of, y_ref), w_ref)
    send_all(g, w_ref, sends)


def middle_kernel(*refs, g, first):
    w_old, *refs = refs
    received, refs = refs[:8], refs[8:]
    if first:
        now_ref, mats_ref, y_ref, w_ref, *sends = refs
    else:
        now_ref, older_ref, mats_ref, y_ref, w_ref, *sends = refs
    gain = (1.0 if first else 2.0) / filter_half
    for e in range(g.elements):
        for h in range(y_ref.shape[1]):
            value = gain * (w_old[e, h] - filter_center * now_ref[e, h])
            y_ref[e, h] = value if first else value - older_ref[e, h]
    add_all(g, y_ref, received, gain)
    multiply(g, mats_ref, functools.partial(field_of, y_ref), w_ref)
    if first:
        send_all(g, w_ref, sends)
        return

    def put_low(ref):
        def put(where, low, high):
            ref[where] = low

        return put

    put_x_face(g, w_ref, put_low(sends[0]))
    put_y_face(g, w_ref, put_low(sends[1]))
    for h in range(w_ref.shape[1]):
        for e3 in range(g.ez):
            rows = slice(e3 * g.side, (e3 + 1) * g.side)
            sends[2][rows, lanes(h)] = line(g, w_ref, 0, 0, e3, h)


def last_kernel(w_old, from_x, from_y, from_xy, now_ref, older_ref, out_ref, y_ref, *, g):
    side = g.side
    gain = 2.0 / filter_half
    for e in range(g.elements):
        for h in range(y_ref.shape[1]):
            value = gain * (w_old[e, h] - filter_center * now_ref[e, h])
            y_ref[e, h] = value - older_ref[e, h]
    p, q = lax.axis_index("dx"), lax.axis_index("dy")
    has_x, has_y = p < lax.axis_size("dx") - 1, q < lax.axis_size("dy") - 1
    add_x_face(g, y_ref, True, lambda w: jnp.where(has_x, from_x[w], 0.0), gain)
    add_y_face(g, y_ref, True, lambda w: jnp.where(has_y, from_y[w], 0.0), gain)
    add_line(g, y_ref, 1, 1, lambda w: jnp.where(has_x & has_y, from_xy[w], 0.0), gain)
    sub = lax.broadcasted_iota(jnp.int32, (side, LANES), 0)
    rest = 2 * g.deg - side
    for i in range(g.ex * g.deg):
        e1 = i // g.deg
        a = i + 1 - e1 * g.deg
        for k in range(g.nz):
            e3 = k // g.deg
            rows = g.rows(a, k + 1 - e3 * g.deg, 1)
            for h in range(y_ref.shape[1]):
                d0 = pltpu.roll(y_ref[g.at(e1, 0, e3), h, rows], side - 1, 0)
                d1 = pltpu.roll(y_ref[g.at(e1, 1, e3), h, rows], side - 2, 0)
                out_ref[i, k, :side, lanes(h)] = jnp.where(sub < g.deg, d0, d1)
                out_ref[i, k, side:, lanes(h)] = jnp.where(sub < rest, d1, 0.0)


def call(kernel, outs, scratch, operands, flops):
    size = sum(x.size * x.dtype.itemsize for x in (*operands, *outs))
    return pl.pallas_call(
        kernel,
        out_shape=outs,
        in_specs=[VMEM] * len(operands),
        out_specs=[VMEM] * len(outs),
        scratch_shapes=scratch,
        compiler_params=pltpu.CompilerParams(vmem_limit_bytes=LIMIT),
        cost_estimate=pl.CostEstimate(flops=flops, bytes_accessed=size, transcendentals=0),
    )(*operands)


def shards(orbitals, elem_mats, conn):
    nx, ny, nz, bands = orbitals.shape
    side = round(elem_mats.shape[-1] ** (1 / 3))
    g = Grid(elem_mats, side)
    f32 = jnp.float32
    orb = jnp.transpose(orbitals, (0, 2, 1, 3))
    below_x = offset(orb[-1], 1, 0)
    below_y = offset(orb[:, :, -1], 0, 1)
    below_xy = offset(orb[-1, :, -1], 1, 1)
    mats = renumber(conn, elem_mats, side, ny + 1, nz + 2)
    mats = mats.reshape(g.elements, g.count, g.count)

    nodes = (g.elements, bands // LANES, g.count, LANES)
    shape = jax.ShapeDtypeStruct
    x_shape = shape((nz, g.ey * side, bands), f32)
    y_shape = shape((g.ex * g.ez, side * side, bands), f32)
    line_shape = shape((g.ez * side, bands), f32)
    send_shapes = [x_shape] * 2 + [y_shape] * 2 + [line_shape] * 4
    pairings = [("A", "-"), ("B", "-"), ("-", "A"), ("-", "B")]
    pairings += [("A", "A"), ("A", "B"), ("B", "A"), ("B", "B")]
    flops = 2 * g.elements * g.count**2 * bands

    y0, w1, *sends = call(
        functools.partial(first_kernel, g=g),
        [shape(nodes, f32), shape(nodes, f32), *send_shapes],
        [],
        (orb, below_x, below_y, below_xy, mats),
        flops,
    )
    received = [pair_swap(s, *pair) for s, pair in zip(sends, pairings)]
    y1, w2, *sends = call(
        functools.partial(middle_kernel, g=g, first=True),
        [shape(nodes, f32), shape(nodes, f32), *send_shapes],
        [],
        (w1, *received, y0, mats),
        flops,
    )
    received = [pair_swap(s, *pair) for s, pair in zip(sends, pairings)]
    y2, w3, *sends = call(
        functools.partial(middle_kernel, g=g, first=False),
        [shape(nodes, f32), shape(nodes, f32), x_shape, y_shape, line_shape],
        [],
        (w2, *received, y1, y0, mats),
        flops,
    )
    received = [offset(s, *step) for s, step in zip(sends, ((-1, 0), (0, -1), (-1, -1)))]
    (y3,) = call(
        functools.partial(last_kernel, g=g),
        [shape((nx, nz, 2 * side, bands), f32)],
        [pltpu.VMEM(nodes, f32)],
        (w3, *received, y2, y1),
        flops // 100,
    )

    columns = y3.reshape(-1, bands)
    gram = jnp.einsum("rb,rc->bc", columns, columns, precision=lax.Precision.HIGHEST)
    gram = total(gram)
    lower = jnp.linalg.cholesky(gram)
    identity = jnp.eye(bands, dtype=f32)
    inverse_lower = lax.linalg.triangular_solve(lower, identity, left_side=True, lower=True)
    basis = jnp.einsum("rb,cb->rc", columns, inverse_lower, precision=lax.Precision.HIGHEST)
    scale = math.sqrt(nx * ny * nz * lax.axis_size(AXES))
    basis = (basis * scale).reshape(nx, nz, 2 * side, bands)[:, :, :ny]
    return jnp.transpose(basis, (0, 2, 1, 3))


def solution(mesh):
    in_specs = (
        P("dx", "dy", None, None),
        P("dx", "dy", None, None, None),
        P("dx", "dy", None, None),
    )
    out_specs = P("dx", "dy", None, None)
    return jax.shard_map(shards, mesh=mesh, in_specs=in_specs, out_specs=out_specs, check_vma=False)
```

```python
import functools
import math

import jax
import jax.numpy as jnp
from jax import lax
from jax.experimental import pallas as pl
from jax.experimental.pallas import tpu as pltpu
from jax.sharding import PartitionSpec as P

filter_center = 1.5
filter_half = 4.0
FIRST = 1.0 / filter_half
LATER = 2.0 / filter_half
AXES = ("dx", "dy")
VMEM = pl.BlockSpec(memory_space=pltpu.VMEM)
LIMIT = 12 * 1024 * 1024
LANES = 128
ROWS = 8


def partner(index, size, pairing):
    if pairing == "-":
        return index
    other = index ^ 1 if pairing == "A" else index - 1 if index % 2 == 0 else index + 1
    return other if 0 <= other < size else index


def pair_swap(value, along_x, along_y):
    size_x, size_y = lax.axis_size("dx"), lax.axis_size("dy")
    route = [
        (p * size_y + q, partner(p, size_x, along_x) * size_y + partner(q, size_y, along_y))
        for p in range(size_x)
        for q in range(size_y)
    ]
    return lax.ppermute(value, AXES, route)


def ring(value, step_x, step_y):
    size_x, size_y = lax.axis_size("dx"), lax.axis_size("dy")
    route = [
        (p * size_y + q, (p + step_x) % size_x * size_y + (q + step_y) % size_y)
        for p in range(size_x)
        for q in range(size_y)
    ]
    return lax.ppermute(value, AXES, route)


def xor_swap(value, axis, bits):
    return lax.ppermute(value, axis, [(i, i ^ bits) for i in range(lax.axis_size(axis))])


def total(gram):
    sizes = [lax.axis_size(axis) for axis in AXES]
    if any(size & (size - 1) or size < 2 for size in sizes):
        return lax.psum(gram, AXES)
    half = gram.shape[0] // 2
    odd = lax.axis_index("dy") % 2
    kept = lax.dynamic_slice_in_dim(gram, odd * half, half, 0)
    sent = lax.dynamic_slice_in_dim(gram, (1 - odd) * half, half, 0)
    part = kept + xor_swap(sent, "dy", 1)
    for axis, first in (("dx", 1), ("dy", 2)):
        bit = first
        while bit < lax.axis_size(axis):
            if 2 * bit < lax.axis_size(axis):
                one, two, three = [xor_swap(part, axis, bit * k) for k in (1, 2, 3)]
                part = (part + one) + (two + three)
                bit *= 4
            else:
                part = part + xor_swap(part, axis, bit)
                bit *= 2
    other = xor_swap(part, "dy", 1)
    low = jnp.where(odd == 0, part, other)
    high = jnp.where(odd == 0, other, part)
    return jnp.concatenate([low, high], axis=0)


def renumber_kernel(conn_ref, mats_ref, out_ref, *, side, width, depth, layers):
    e1, e2, e3 = (pl.program_id(k) for k in range(3))
    deg = side - 1
    rows = conn_ref[0, 0]
    node = rows[0:1]
    for k in range(1, layers):
        node = jnp.where(e3 == k, rows[k : k + 1], node)
    node = node.astype(jnp.float32)
    plane = jnp.floor((node + 0.5) * (1.0 / depth))
    first = jnp.floor((plane + 0.5) * (1.0 / width))
    c = (node - plane * depth).astype(jnp.int32) - deg * e3
    b = (plane - first * width).astype(jnp.int32) - deg * e2
    a = first.astype(jnp.int32) - deg * e1
    place = (a * side + c) * side + b
    a = jnp.where((e1 == 0) & (lax.axis_index("dx") == 0), a, 1)
    b = jnp.where((e2 == 0) & (lax.axis_index("dy") == 0), b, 1)
    c_low = jnp.where(e3 == 0, c, 1)
    c_high = jnp.where(e3 == layers - 1, c, 1)
    held = (a == 0) | (b == 0) | (c_low == 0) | (c_high == deg)
    place = jnp.where(held, -1, place)
    count = mats_ref.shape[-1]
    order = lax.broadcasted_iota(jnp.int32, (count, count), 0) == place
    order = jnp.where(order, 1.0, 0.0).astype(jnp.bfloat16)
    half = jnp.dot(order, mats_ref[0, 0, 0], preferred_element_type=jnp.float32)
    whole = lax.dot_general(
        half.astype(jnp.bfloat16),
        order,
        (((1,), (1,)), ((), ())),
        preferred_element_type=jnp.float32,
    )
    out_ref[0, 0, 0] = whole.astype(jnp.bfloat16)


def renumber(conn, elem_mats, side, width, depth):
    ex, ey, layers, count, _ = elem_mats.shape
    spot = pl.BlockSpec((1, 1, 1, count, count), lambda i, j, k: (i, j, k, 0, 0))
    return pl.pallas_call(
        functools.partial(renumber_kernel, side=side, width=width, depth=depth, layers=layers),
        out_shape=jax.ShapeDtypeStruct(elem_mats.shape, jnp.bfloat16),
        grid=(ex, ey, layers),
        in_specs=[pl.BlockSpec((1, 1, layers, count), lambda i, j, k: (i, j, 0, 0)), spot],
        out_specs=spot,
        compiler_params=pltpu.CompilerParams(vmem_limit_bytes=LIMIT),
        cost_estimate=pl.CostEstimate(
            flops=4 * ex * ey * layers * count**3,
            bytes_accessed=4 * elem_mats.size,
            transcendentals=0,
        ),
        name="renumber",
    )(conn, elem_mats)


class Grid:
    def __init__(self, elem_mats, side):
        self.ex, self.ey, self.ez = elem_mats.shape[:3]
        self.count = elem_mats.shape[3]
        self.side = side
        self.deg = side - 1
        self.nz = self.ez * self.deg - 1
        self.elements = self.ex * self.ey * self.ez

    def at(self, e1, e2, e3):
        return (e1 * self.ey + e2) * self.ez + e3

    def rows(self, a, c, number):
        start = (a * self.side + c) * self.side
        return slice(start, start + number * self.side)

    def layers(self, e3):
        low = 1 if e3 == 0 else 0
        high = self.deg - 1 if e3 == self.ez - 1 else self.deg
        return low, high - low + 1, e3 * self.deg + low - 1

    def side_rows(self, b):
        return pl.ds(b, self.side * self.side, stride=self.side)

    def line_rows(self, a, b):
        return pl.ds(a * self.side * self.side + b, self.side, stride=self.side)


def lanes(h):
    return slice(h * LANES, (h + 1) * LANES)


def multiply(g, mats_ref, field_of, w_ref):
    side, deg = g.side, g.deg
    halves = range(w_ref.shape[1])
    for e in range(g.elements):
        product = jnp.dot(mats_ref[e], field_of(e), preferred_element_type=jnp.float32)
        for h in halves:
            w_ref[e, h] = product[:, lanes(h)]

    def join(one, top, two, bottom):
        for h in halves:
            both = w_ref[one, h, top] + w_ref[two, h, bottom]
            w_ref[one, h, top] = both
            w_ref[two, h, bottom] = both

    for e1 in range(g.ex):
        for e2 in range(g.ey):
            for e3 in range(g.ez - 1):
                for a in range(side):
                    one, two = g.at(e1, e2, e3), g.at(e1, e2, e3 + 1)
                    join(one, g.rows(a, deg, 1), two, g.rows(a, 0, 1))
    for e1 in range(g.ex - 1):
        for e2 in range(g.ey):
            for e3 in range(g.ez):
                one, two = g.at(e1, e2, e3), g.at(e1 + 1, e2, e3)
                join(one, g.rows(deg, 0, side), two, g.rows(0, 0, side))
    for e1 in range(g.ex):
        for e2 in range(g.ey - 1):
            for e3 in range(g.ez):
                one, two = g.at(e1, e2, e3), g.at(e1, e2 + 1, e3)
                join(one, g.side_rows(deg), two, g.side_rows(0))


def put_x_face(g, w_ref, put):
    for h in range(w_ref.shape[1]):
        for e2 in range(g.ey):
            for e3 in range(g.ez):
                low, number, start = g.layers(e3)
                if e3 > 0:
                    low, number, start = low + 1, number - 1, start + 1
                one = w_ref[g.at(0, e2, e3), h, g.rows(0, low, number)]
                two = w_ref[g.at(g.ex - 1, e2, e3), h, g.rows(g.deg, low, number)]
                where = (
                    slice(start, start + number),
                    slice(e2 * g.side, (e2 + 1) * g.side),
                    lanes(h),
                )
                shape = (number, g.side, LANES)
                put(where, one.reshape(shape), two.reshape(shape))


def put_y_face(g, w_ref, put):
    for h in range(w_ref.shape[1]):
        for e1 in range(g.ex):
            for e3 in range(g.ez):
                one = w_ref[g.at(e1, 0, e3), h, g.side_rows(0)]
                two = w_ref[g.at(e1, g.ey - 1, e3), h, g.side_rows(g.deg)]
                put((e1 * g.ez + e3, slice(None), lanes(h)), one, two)


def line(g, w_ref, high_x, high_y, e3, h):
    e1, a = (g.ex - 1, g.deg) if high_x else (0, 0)
    e2, b = (g.ey - 1, g.deg) if high_y else (0, 0)
    return w_ref[g.at(e1, e2, e3), h, g.line_rows(a, b)]


def add_x_face(g, out_ref, high, received, factor):
    e1, a = (g.ex - 1, g.deg) if high else (0, 0)
    for h in range(out_ref.shape[1]):
        for e2 in range(g.ey):
            for e3 in range(g.ez):
                low, number, start = g.layers(e3)
                columns = slice(e2 * g.side, (e2 + 1) * g.side)
                part = received((slice(start, start + number), columns, lanes(h)))
                rows = g.rows(a, low, number)
                part = part.reshape(number * g.side, LANES)
                out_ref[g.at(e1, e2, e3), h, rows] += factor * part


def add_y_face(g, out_ref, high, received, factor):
    e2, b = (g.ey - 1, g.deg) if high else (0, 0)
    for h in range(out_ref.shape[1]):
        for e1 in range(g.ex):
            for e3 in range(g.ez):
                part = received((e1 * g.ez + e3, slice(None), lanes(h)))
                out_ref[g.at(e1, e2, e3), h, g.side_rows(b)] += factor * part


def add_line(g, out_ref, high_x, high_y, received, factor):
    e1, a = (g.ex - 1, g.deg) if high_x else (0, 0)
    e2, b = (g.ey - 1, g.deg) if high_y else (0, 0)
    for h in range(out_ref.shape[1]):
        for e3 in range(g.ez):
            part = received((slice(e3 * g.side, (e3 + 1) * g.side), lanes(h)))
            out_ref[g.at(e1, e2, e3), h, g.line_rows(a, b)] += factor * part


def send_all(g, w_ref, sends):
    even_x = lax.axis_index("dx") % 2 == 0
    even_y = lax.axis_index("dy") % 2 == 0

    def by_pair(even, one_ref, two_ref):
        def put(where, low, high):
            one_ref[where] = jnp.where(even, high, low)
            two_ref[where] = jnp.where(even, low, high)

        return put

    put_x_face(g, w_ref, by_pair(even_x, sends[0], sends[1]))
    put_y_face(g, w_ref, by_pair(even_y, sends[2], sends[3]))
    for h in range(w_ref.shape[1]):
        for e3 in range(g.ez):
            where = (slice(e3 * g.side, (e3 + 1) * g.side), lanes(h))
            at_x = [[line(g, w_ref, hx, hy, e3, h) for hy in (0, 1)] for hx in (0, 1)]
            for my in (0, 1):
                low, high = [jnp.where(even_y, at_x[hx][1 - my], at_x[hx][my]) for hx in (0, 1)]
                by_pair(even_x, sends[4 + my], sends[6 + my])(where, low, high)


def add_all(g, out_ref, received, factor):
    p, q = lax.axis_index("dx"), lax.axis_index("dy")
    even_x, even_y = p % 2 == 0, q % 2 == 0
    has_x = (p > 0, p < lax.axis_size("dx") - 1)
    has_y = (q > 0, q < lax.axis_size("dy") - 1)

    def from_pair(even, high, one, two, exists):
        value = jnp.where(even, one, two) if high else jnp.where(even, two, one)
        return jnp.where(exists, value, 0.0)

    for high in (0, 1):

        def across_x(where):
            return from_pair(even_x, high, received[0][where], received[1][where], has_x[high])

        def across_y(where):
            return from_pair(even_y, high, received[2][where], received[3][where], has_y[high])

        add_x_face(g, out_ref, high, across_x, factor)
        add_y_face(g, out_ref, high, across_y, factor)
    for hx in (0, 1):
        for hy in (0, 1):

            def diagonal(where):
                one = from_pair(even_y, hy, received[4][where], received[5][where], has_y[hy])
                two = from_pair(even_y, hy, received[6][where], received[7][where], has_y[hy])
                return from_pair(even_x, hx, one, two, has_x[hx])

            add_line(g, out_ref, hx, hy, diagonal, factor)


def field_of(y_ref, e):
    parts = [y_ref[e, h].astype(jnp.bfloat16) for h in range(y_ref.shape[1])]
    return jnp.concatenate(parts, axis=-1)


def first_kernel(*refs, g):
    orb_ref, below_x, below_y, below_xy, mats_ref, y_ref, next_ref, *sends = refs
    side = g.side
    halves = range(y_ref.shape[1])
    sub = lax.broadcasted_iota(jnp.int32, (side, LANES), 0)
    nothing = jnp.zeros((side, LANES), jnp.float32)
    rest = orb_ref.shape[2] - side
    for e1 in range(g.ex):
        for e2 in range(g.ey):
            for a in range(side):
                for h in halves:
                    y_ref[g.at(e1, e2, 0), h, g.rows(a, 0, 1)] = nothing
                    y_ref[g.at(e1, e2, g.ez - 1), h, g.rows(a, g.deg, 1)] = nothing

    def place(i, k, column, edge):
        for h in halves:
            part = column[:, lanes(h)].astype(jnp.float32)
            t0 = part[:side]
            t1 = jnp.concatenate([part[side:], nothing[: side - rest]], axis=0)
            first = jnp.broadcast_to(edge[:, lanes(h)].astype(jnp.float32), (side, LANES))
            d0 = jnp.where(sub == 0, first, pltpu.roll(t0, 1, 0))
            d1 = jnp.where(sub < 2, pltpu.roll(t0, 2, 0), pltpu.roll(t1, 2, 0))
            for e1 in range(g.ex):
                a = i - e1 * g.deg
                for e3 in range(g.ez):
                    c = k + 1 - e3 * g.deg
                    if 0 <= a <= g.deg and 0 <= c <= g.deg:
                        y_ref[g.at(e1, 0, e3), h, g.rows(a, c, 1)] = d0
                        y_ref[g.at(e1, 1, e3), h, g.rows(a, c, 1)] = d1

    for k in range(g.nz):
        place(0, k, below_x[k], below_xy[k : k + 1])
        for i in range(orb_ref.shape[0]):
            place(i + 1, k, orb_ref[i, k], below_y[i, k : k + 1])
    multiply(g, mats_ref, functools.partial(field_of, y_ref), next_ref)
    send_all(g, next_ref, sends)
    advance(next_ref, y_ref, None, FIRST)


def advance(next_ref, now_ref, older_ref, gain):
    for e in range(next_ref.shape[0]):
        for h in range(next_ref.shape[1]):
            value = gain * (next_ref[e, h] - filter_center * now_ref[e, h])
            next_ref[e, h] = value if older_ref is None else value - older_ref[e, h]


def middle_kernel(*refs, g):
    part_ref, *refs = refs
    received, refs = refs[:8], refs[8:]
    older_ref, mats_ref, y_ref, next_ref, *sends = refs
    y_ref[...] = part_ref[...]
    add_all(g, y_ref, received, FIRST)
    multiply(g, mats_ref, functools.partial(field_of, y_ref), next_ref)
    send_all(g, next_ref, sends)
    advance(next_ref, y_ref, older_ref, LATER)


def late_kernel(*refs, g):
    part_ref, *refs = refs
    received, refs = refs[:8], refs[8:]
    older_ref, mats_ref, next_ref, *sends, y_ref = refs
    y_ref[...] = part_ref[...]
    add_all(g, y_ref, received, LATER)
    multiply(g, mats_ref, functools.partial(field_of, y_ref), next_ref)

    def put_low(ref):
        def put(where, low, high):
            ref[where] = low

        return put

    put_x_face(g, next_ref, put_low(sends[0]))
    put_y_face(g, next_ref, put_low(sends[1]))
    for h in range(next_ref.shape[1]):
        for e3 in range(g.ez):
            rows = slice(e3 * g.side, (e3 + 1) * g.side)
            sends[2][rows, lanes(h)] = line(g, next_ref, 0, 0, e3, h)
    advance(next_ref, y_ref, older_ref, LATER)


def last_kernel(part_ref, from_x, from_y, from_xy, out_ref, y_ref, *, g):
    side = g.side
    y_ref[...] = part_ref[...]
    p, q = lax.axis_index("dx"), lax.axis_index("dy")
    has_x, has_y = p < lax.axis_size("dx") - 1, q < lax.axis_size("dy") - 1
    add_x_face(g, y_ref, True, lambda w: jnp.where(has_x, from_x[w], 0.0), LATER)
    add_y_face(g, y_ref, True, lambda w: jnp.where(has_y, from_y[w], 0.0), LATER)
    add_line(g, y_ref, 1, 1, lambda w: jnp.where(has_x & has_y, from_xy[w], 0.0), LATER)
    sub = lax.broadcasted_iota(jnp.int32, (side, LANES), 0)
    rest = 2 * g.deg - side
    for i in range(g.ex * g.deg):
        e1 = i // g.deg
        a = i + 1 - e1 * g.deg
        for k in range(g.nz):
            e3 = k // g.deg
            rows = g.rows(a, k + 1 - e3 * g.deg, 1)
            for h in range(y_ref.shape[1]):
                d0 = pltpu.roll(y_ref[g.at(e1, 0, e3), h, rows], side - 1, 0)
                d1 = pltpu.roll(y_ref[g.at(e1, 1, e3), h, rows], side - 2, 0)
                out_ref[i, k, :side, lanes(h)] = jnp.where(sub < g.deg, d0, d1)
                out_ref[i, k, side:, lanes(h)] = jnp.where(sub < rest, d1, 0.0)


def invert_block(block):
    size = block.shape[0]
    groups = size // ROWS
    sub = lax.broadcasted_iota(jnp.int32, (ROWS, size), 0)
    lane = lax.broadcasted_iota(jnp.int32, (ROWS, size), 1)
    left = [block[ROWS * j : ROWS * (j + 1)] for j in range(groups)]
    right = [jnp.where(lane == sub + ROWS * j, 1.0, 0.0) for j in range(groups)]
    spread = lambda row: jnp.broadcast_to(row, (ROWS, size))
    result = []
    for k in range(groups):
        tile = left[k]
        cols = [spread(tile[:, ROWS * k + c : ROWS * k + c + 1]) for c in range(ROWS)]
        s = [[spread(cols[c][r : r + 1]) if c <= r else None for c in range(ROWS)] for r in range(ROWS)]
        inv, mult = [], [[None] * ROWS for _ in range(ROWS)]
        root = []
        for j in range(ROWS):
            inv.append(1.0 / s[j][j])
            root.append(lax.rsqrt(s[j][j]))
            for r in range(j + 1, ROWS):
                mult[r][j] = s[r][j] * inv[j]
            for r in range(j + 1, ROWS):
                for c in range(j + 1, r + 1):
                    s[r][c] = s[r][c] - mult[r][j] * s[c][j]
        last = k == groups - 1
        solved = []
        for source, wanted in ((right[k], True), (tile, False)):
            if last and not wanted:
                continue
            rows = [spread(source[r : r + 1]) for r in range(ROWS)]
            for j in range(ROWS):
                for r in range(j + 1, ROWS):
                    rows[r] = rows[r] - mult[r][j] * rows[j]
            if wanted:
                done = rows[0] * root[0]
                for r in range(1, ROWS):
                    done = jnp.where(sub == r, rows[r] * root[r], done)
                result.append(done)
            if last:
                continue
            rows = [row * d for row, d in zip(rows, inv)]
            for j in reversed(range(ROWS)):
                for r in range(j):
                    rows[r] = rows[r] - mult[j][r] * rows[j]
            solved.append(rows)
        for j in range(k + 1, groups):
            cols = [spread(left[j][:, ROWS * k + c : ROWS * k + c + 1]) for c in range(ROWS)]
            for c in range(ROWS):
                right[j] = right[j] - cols[c] * solved[0][c]
                left[j] = left[j] - cols[c] * solved[1][c]
    return jnp.concatenate(result, axis=0)


def dot(one, two, axis_one=1, axis_two=0):
    return lax.dot_general(
        one,
        two,
        (((axis_one,), (axis_two,)), ((), ())),
        precision=lax.Precision.HIGHEST,
        preferred_element_type=jnp.float32,
    )


def inverse_factor(block_of, count):
    low, inv = {}, {}
    for i in range(count):
        diag = block_of(i, i)
        for j in range(i):
            part = block_of(i, j)
            for k in range(j):
                part = part - dot(low[i, k], low[j, k], 1, 1)
            low[i, j] = dot(part, inv[j, j], 1, 1)
            diag = diag - dot(low[i, j], low[i, j], 1, 1)
        sums = []
        for j in range(i):
            part = dot(low[i, j], inv[j, j])
            for k in range(j + 1, i):
                part = part + dot(low[i, k], inv[k, j])
            sums.append(part)
        inv[i, i] = invert_block(diag)
        for j in range(i):
            inv[i, j] = -dot(inv[i, i], sums[j])
    return inv

def factor_kernel(gram_ref, out_ref):
    count = gram_ref.shape[0] // LANES
    inverse = inverse_factor(lambda i, j: gram_ref[lanes(i), lanes(j)], count)
    for i in range(count):
        for j in range(count):
            block = inverse[i, j] if j <= i else jnp.zeros((LANES, LANES), jnp.float32)
            out_ref[lanes(i), lanes(j)] = block


def call(kernel, outs, scratch, operands, flops):
    size = sum(x.size * x.dtype.itemsize for x in (*operands, *outs))
    return pl.pallas_call(
        kernel,
        out_shape=outs,
        in_specs=[VMEM] * len(operands),
        out_specs=[VMEM] * len(outs),
        scratch_shapes=scratch,
        compiler_params=pltpu.CompilerParams(vmem_limit_bytes=LIMIT),
        cost_estimate=pl.CostEstimate(flops=flops, bytes_accessed=size, transcendentals=0),
    )(*operands)


def shards(orbitals, elem_mats, conn):
    nx, ny, nz, bands = orbitals.shape
    side = round(elem_mats.shape[-1] ** (1 / 3))
    g = Grid(elem_mats, side)
    f32 = jnp.float32
    orb = jnp.transpose(orbitals, (0, 2, 1, 3))
    below_x = ring(orb[-1], 1, 0)
    below_y = ring(orb[:, :, -1], 0, 1)
    below_xy = ring(orb[-1, :, -1], 1, 1)
    mats = renumber(conn, elem_mats, side, ny + 1, nz + 2)
    mats = mats.reshape(g.elements, g.count, g.count)

    nodes = (g.elements, bands // LANES, g.count, LANES)
    shape = jax.ShapeDtypeStruct
    x_shape = shape((nz, g.ey * side, bands), f32)
    y_shape = shape((g.ex * g.ez, side * side, bands), f32)
    line_shape = shape((g.ez * side, bands), f32)
    send_shapes = [x_shape] * 2 + [y_shape] * 2 + [line_shape] * 4
    pairings = [("A", "-"), ("B", "-"), ("-", "A"), ("-", "B")]
    pairings += [("A", "A"), ("A", "B"), ("B", "A"), ("B", "B")]
    flops = 2 * g.elements * g.count**2 * bands

    y0, part, *sends = call(
        functools.partial(first_kernel, g=g),
        [shape(nodes, f32), shape(nodes, f32), *send_shapes],
        [],
        (orb, below_x, below_y, below_xy, mats),
        flops,
    )
    received = [pair_swap(s, *pair) for s, pair in zip(sends, pairings)]
    y1, part, *sends = call(
        functools.partial(middle_kernel, g=g),
        [shape(nodes, f32), shape(nodes, f32), *send_shapes],
        [],
        (part, *received, y0, mats),
        flops,
    )
    received = [pair_swap(s, *pair) for s, pair in zip(sends, pairings)]
    part, *sends = call(
        functools.partial(late_kernel, g=g),
        [shape(nodes, f32), x_shape, y_shape, line_shape],
        [pltpu.VMEM(nodes, f32)],
        (part, *received, y1, mats),
        flops,
    )
    received = [ring(s, *step) for s, step in zip(sends, ((-1, 0), (0, -1), (-1, -1)))]
    (y3,) = call(
        functools.partial(last_kernel, g=g),
        [shape((nx, nz, 2 * side, bands), f32)],
        [pltpu.VMEM(nodes, f32)],
        (part, *received),
        flops // 100,
    )

    columns = y3.reshape(-1, bands)
    gram = jnp.einsum("rb,rc->bc", columns, columns, precision=lax.Precision.HIGHEST)
    gram = total(gram)
    (inverse_lower,) = call(
        factor_kernel, [shape((bands, bands), f32)], [], (gram,), 2 * bands**3
    )
    basis = jnp.einsum("rb,cb->rc", columns, inverse_lower, precision=lax.Precision.HIGHEST)
    scale = math.sqrt(nx * ny * nz * lax.axis_size(AXES))
    basis = (basis * scale).reshape(nx, nz, 2 * side, bands)[:, :, :ny]
    return jnp.transpose(basis, (0, 2, 1, 3))


def solution(mesh):
    in_specs = (
        P("dx", "dy", None, None),
        P("dx", "dy", None, None, None),
        P("dx", "dy", None, None),
    )
    out_specs = P("dx", "dy", None, None)
    return jax.shard_map(shards, mesh=mesh, in_specs=in_specs, out_specs=out_specs, check_vma=False)
```

```python
import functools
import math

import jax
import jax.numpy as jnp
from jax import lax
from jax.experimental import pallas as pl
from jax.experimental.pallas import tpu as pltpu
from jax.sharding import PartitionSpec as P

filter_center = 1.5
filter_half = 4.0
FIRST = 1.0 / filter_half
LATER = 2.0 / filter_half
AXES = ("dx", "dy")
VMEM = pl.BlockSpec(memory_space=pltpu.VMEM)
LIMIT = 16 * 1024 * 1024
LANES = 128
ROWS = 8


def partner(index, size, pairing, closed):
    if pairing == "-":
        return index
    other = index ^ 1 if pairing == "A" else index - 1 if index % 2 == 0 else index + 1
    if 0 <= other < size:
        return other
    return size - 1 - index if closed and pairing == "B" and size % 2 == 0 else index


def pair_swap(value, along_x, along_y):
    size_x, size_y = lax.axis_size("dx"), lax.axis_size("dy")
    route = [
        (
            p * size_y + q,
            partner(p, size_x, along_x, False) * size_y + partner(q, size_y, along_y, True),
        )
        for p in range(size_x)
        for q in range(size_y)
    ]
    return lax.ppermute(value, AXES, route)


def ring(value, step_x, step_y):
    size_x, size_y = lax.axis_size("dx"), lax.axis_size("dy")
    route = [
        (p * size_y + q, (p + step_x) % size_x * size_y + (q + step_y) % size_y)
        for p in range(size_x)
        for q in range(size_y)
    ]
    return lax.ppermute(value, AXES, route)


def xor_swap(value, axis, bits):
    return lax.ppermute(value, axis, [(i, i ^ bits) for i in range(lax.axis_size(axis))])


def halved_total(kept, sent):
    part = kept + xor_swap(sent, "dy", 1)
    for axis, bit in (("dx", 1), ("dy", 2)):
        while bit < lax.axis_size(axis):
            if 2 * bit < lax.axis_size(axis):
                one, two, three = [xor_swap(part, axis, bit * k) for k in (1, 2, 3)]
                part = (part + one) + (two + three)
                bit *= 4
            else:
                part = part + xor_swap(part, axis, bit)
                bit *= 2
    return part, xor_swap(part, "dy", 1)


def renumber_kernel(conn_ref, mats_ref, out_ref, *, side, width, depth, layers):
    e1, e2, e3 = (pl.program_id(k) for k in range(3))
    deg = side - 1
    rows = conn_ref[0, 0]
    node = rows[0:1]
    for k in range(1, layers):
        node = jnp.where(e3 == k, rows[k : k + 1], node)
    node = node.astype(jnp.float32)
    plane = jnp.floor((node + 0.5) * (1.0 / depth))
    first = jnp.floor((plane + 0.5) * (1.0 / width))
    c = (node - plane * depth).astype(jnp.int32) - deg * e3
    b = (plane - first * width).astype(jnp.int32) - deg * e2
    a = first.astype(jnp.int32) - deg * e1
    place = (a * side + c) * side + b
    a = jnp.where((e1 == 0) & (lax.axis_index("dx") == 0), a, 1)
    b = jnp.where((e2 == 0) & (lax.axis_index("dy") == 0), b, 1)
    c_low = jnp.where(e3 == 0, c, 1)
    c_high = jnp.where(e3 == layers - 1, c, 1)
    held = (a == 0) | (b == 0) | (c_low == 0) | (c_high == deg)
    place = jnp.where(held, -1, place)
    count = mats_ref.shape[-1]
    order = lax.broadcasted_iota(jnp.int32, (count, count), 0) == place
    order = jnp.where(order, 1.0, 0.0).astype(jnp.bfloat16)
    half = jnp.dot(order, mats_ref[0, 0, 0], preferred_element_type=jnp.float32)
    whole = lax.dot_general(
        half.astype(jnp.bfloat16),
        order,
        (((1,), (1,)), ((), ())),
        preferred_element_type=jnp.float32,
    )
    out_ref[0, 0, 0] = whole.astype(jnp.bfloat16)


def renumber(conn, elem_mats, side, width, depth):
    ex, ey, layers, count, _ = elem_mats.shape
    spot = pl.BlockSpec((1, 1, 1, count, count), lambda i, j, k: (i, j, k, 0, 0))
    return pl.pallas_call(
        functools.partial(renumber_kernel, side=side, width=width, depth=depth, layers=layers),
        out_shape=jax.ShapeDtypeStruct(elem_mats.shape, jnp.bfloat16),
        grid=(ex, ey, layers),
        in_specs=[pl.BlockSpec((1, 1, layers, count), lambda i, j, k: (i, j, 0, 0)), spot],
        out_specs=spot,
        compiler_params=pltpu.CompilerParams(vmem_limit_bytes=LIMIT),
        cost_estimate=pl.CostEstimate(
            flops=4 * ex * ey * layers * count**3,
            bytes_accessed=4 * elem_mats.size,
            transcendentals=0,
        ),
        name="renumber",
    )(conn, elem_mats)


class Grid:
    def __init__(self, elem_mats, side):
        self.ex, self.ey, self.ez = elem_mats.shape[:3]
        self.count = elem_mats.shape[3]
        self.side = side
        self.deg = side - 1
        self.nz = self.ez * self.deg - 1
        self.elements = self.ex * self.ey * self.ez

    def at(self, e1, e2, e3):
        return (e1 * self.ey + e2) * self.ez + e3

    def rows(self, a, c, number):
        start = (a * self.side + c) * self.side
        return slice(start, start + number * self.side)

    def layers(self, e3):
        low = 1 if e3 == 0 else 0
        high = self.deg - 1 if e3 == self.ez - 1 else self.deg
        return low, high - low + 1, e3 * self.deg + low - 1

    def side_rows(self, b):
        return pl.ds(b, self.side * self.side, stride=self.side)

    def line_rows(self, a, b):
        return pl.ds(a * self.side * self.side + b, self.side, stride=self.side)


def lanes(h):
    return slice(h * LANES, (h + 1) * LANES)


def multiply(g, mats_ref, field_of, w_ref):
    side, deg = g.side, g.deg
    halves = range(w_ref.shape[1])
    for e in range(g.elements):
        product = jnp.dot(mats_ref[e], field_of(e), preferred_element_type=jnp.float32)
        for h in halves:
            w_ref[e, h] = product[:, lanes(h)]

    def join(one, top, two, bottom):
        for h in halves:
            both = w_ref[one, h, top] + w_ref[two, h, bottom]
            w_ref[one, h, top] = both
            w_ref[two, h, bottom] = both

    for e1 in range(g.ex):
        for e2 in range(g.ey):
            for e3 in range(g.ez - 1):
                for a in range(side):
                    one, two = g.at(e1, e2, e3), g.at(e1, e2, e3 + 1)
                    join(one, g.rows(a, deg, 1), two, g.rows(a, 0, 1))
    for e1 in range(g.ex - 1):
        for e2 in range(g.ey):
            for e3 in range(g.ez):
                one, two = g.at(e1, e2, e3), g.at(e1 + 1, e2, e3)
                join(one, g.rows(deg, 0, side), two, g.rows(0, 0, side))
    for e1 in range(g.ex):
        for e2 in range(g.ey - 1):
            for e3 in range(g.ez):
                one, two = g.at(e1, e2, e3), g.at(e1, e2 + 1, e3)
                join(one, g.side_rows(deg), two, g.side_rows(0))


def put_x_face(g, w_ref, put):
    for h in range(w_ref.shape[1]):
        for e2 in range(g.ey):
            for e3 in range(g.ez):
                low, number, start = g.layers(e3)
                if e3 > 0:
                    low, number, start = low + 1, number - 1, start + 1
                one = w_ref[g.at(0, e2, e3), h, g.rows(0, low, number)]
                two = w_ref[g.at(g.ex - 1, e2, e3), h, g.rows(g.deg, low, number)]
                where = (
                    slice(start, start + number),
                    slice(e2 * g.side, (e2 + 1) * g.side),
                    lanes(h),
                )
                shape = (number, g.side, LANES)
                put(where, one.reshape(shape), two.reshape(shape))


def put_y_face(g, w_ref, put):
    for h in range(w_ref.shape[1]):
        for e1 in range(g.ex):
            for e3 in range(g.ez):
                one = w_ref[g.at(e1, 0, e3), h, g.side_rows(0)]
                two = w_ref[g.at(e1, g.ey - 1, e3), h, g.side_rows(g.deg)]
                put((e1 * g.ez + e3, slice(None), lanes(h)), one, two)


def line(g, w_ref, high_x, high_y, e3, h):
    e1, a = (g.ex - 1, g.deg) if high_x else (0, 0)
    e2, b = (g.ey - 1, g.deg) if high_y else (0, 0)
    return w_ref[g.at(e1, e2, e3), h, g.line_rows(a, b)]


def add_x_face(g, out_ref, high, received, factor):
    e1, a = (g.ex - 1, g.deg) if high else (0, 0)
    for h in range(out_ref.shape[1]):
        for e2 in range(g.ey):
            for e3 in range(g.ez):
                low, number, start = g.layers(e3)
                columns = slice(e2 * g.side, (e2 + 1) * g.side)
                part = received((slice(start, start + number), columns, lanes(h)))
                rows = g.rows(a, low, number)
                part = part.reshape(number * g.side, LANES)
                out_ref[g.at(e1, e2, e3), h, rows] += factor * part


def add_y_face(g, out_ref, high, received, factor):
    e2, b = (g.ey - 1, g.deg) if high else (0, 0)
    for h in range(out_ref.shape[1]):
        for e1 in range(g.ex):
            for e3 in range(g.ez):
                part = received((e1 * g.ez + e3, slice(None), lanes(h)))
                out_ref[g.at(e1, e2, e3), h, g.side_rows(b)] += factor * part


def add_line(g, out_ref, high_x, high_y, received, factor):
    e1, a = (g.ex - 1, g.deg) if high_x else (0, 0)
    e2, b = (g.ey - 1, g.deg) if high_y else (0, 0)
    for h in range(out_ref.shape[1]):
        for e3 in range(g.ez):
            part = received((slice(e3 * g.side, (e3 + 1) * g.side), lanes(h)))
            out_ref[g.at(e1, e2, e3), h, g.line_rows(a, b)] += factor * part


def send_all(g, w_ref, sends):
    even_x = lax.axis_index("dx") % 2 == 0
    even_y = lax.axis_index("dy") % 2 == 0

    def by_pair(even, one_ref, two_ref):
        def put(where, low, high):
            one_ref[where] = jnp.where(even, high, low)
            two_ref[where] = jnp.where(even, low, high)

        return put

    put_x_face(g, w_ref, by_pair(even_x, sends[0], sends[1]))
    put_y_face(g, w_ref, by_pair(even_y, sends[2], sends[3]))


def corner_kernel(from_a, from_b, to_a, to_b, *, g):
    even = lax.axis_index("dy") % 2 == 0
    last = from_a.shape[1] - 1
    bands = from_a.shape[2]
    for k, source in enumerate((from_a, from_b)):
        for e3 in range(g.ez):
            low, number, start = g.layers(e3)
            for c in range(g.side):
                row = slice(e3 * g.side + c, e3 * g.side + c + 1)
                if low <= c < low + number:
                    z = start + c - low
                    bottom, top = source[z, 0:1], source[z, last : last + 1]
                    to_a[k, row] = jnp.where(even, top, bottom)
                    to_b[k, row] = jnp.where(even, bottom, top)
                else:
                    to_a[k, row] = jnp.zeros((1, bands), jnp.float32)
                    to_b[k, row] = jnp.zeros((1, bands), jnp.float32)


def add_all(g, out_ref, received, factor):
    p, q = lax.axis_index("dx"), lax.axis_index("dy")
    even_x, even_y = p % 2 == 0, q % 2 == 0
    has_x = (p > 0, p < lax.axis_size("dx") - 1)
    has_y = (q > 0, q < lax.axis_size("dy") - 1)

    def from_pair(even, high, one, two, exists):
        value = jnp.where(even, one, two) if high else jnp.where(even, two, one)
        return jnp.where(exists, value, 0.0)

    for high in (0, 1):

        def across_x(where):
            return from_pair(even_x, high, received[0][where], received[1][where], has_x[high])

        def across_y(where):
            return from_pair(even_y, high, received[2][where], received[3][where], has_y[high])

        add_x_face(g, out_ref, high, across_x, factor)
        add_y_face(g, out_ref, high, across_y, factor)
    for hx in (0, 1):
        for hy in (0, 1):

            def diagonal(where):
                one, two = [
                    from_pair(even_y, hy, received[4][k, *where], received[5][k, *where], has_y[hy])
                    for k in (0, 1)
                ]
                return from_pair(even_x, hx, one, two, has_x[hx])

            add_line(g, out_ref, hx, hy, diagonal, factor)


def field_of(y_ref, e):
    parts = [y_ref[e, h].astype(jnp.bfloat16) for h in range(y_ref.shape[1])]
    return jnp.concatenate(parts, axis=-1)


def first_kernel(*refs, g):
    orb_ref, below_x, below_y, below_xy, mats_ref, y_ref, next_ref, *sends = refs
    side = g.side
    halves = range(y_ref.shape[1])
    sub = lax.broadcasted_iota(jnp.int32, (side, LANES), 0)
    nothing = jnp.zeros((side, LANES), jnp.float32)
    rest = orb_ref.shape[2] - side
    for e1 in range(g.ex):
        for e2 in range(g.ey):
            for a in range(side):
                for h in halves:
                    y_ref[g.at(e1, e2, 0), h, g.rows(a, 0, 1)] = nothing
                    y_ref[g.at(e1, e2, g.ez - 1), h, g.rows(a, g.deg, 1)] = nothing

    def place(i, k, column, edge):
        for h in halves:
            part = column[:, lanes(h)].astype(jnp.float32)
            t0 = part[:side]
            t1 = jnp.concatenate([part[side:], nothing[: side - rest]], axis=0)
            first = jnp.broadcast_to(edge[:, lanes(h)].astype(jnp.float32), (side, LANES))
            d0 = jnp.where(sub == 0, first, pltpu.roll(t0, 1, 0))
            d1 = jnp.where(sub < 2, pltpu.roll(t0, 2, 0), pltpu.roll(t1, 2, 0))
            for e1 in range(g.ex):
                a = i - e1 * g.deg
                for e3 in range(g.ez):
                    c = k + 1 - e3 * g.deg
                    if 0 <= a <= g.deg and 0 <= c <= g.deg:
                        y_ref[g.at(e1, 0, e3), h, g.rows(a, c, 1)] = d0
                        y_ref[g.at(e1, 1, e3), h, g.rows(a, c, 1)] = d1

    for k in range(g.nz):
        place(0, k, below_x[k], below_xy[k : k + 1])
        for i in range(orb_ref.shape[0]):
            place(i + 1, k, orb_ref[i, k], below_y[i, k : k + 1])
    multiply(g, mats_ref, functools.partial(field_of, y_ref), next_ref)
    send_all(g, next_ref, sends)
    advance(next_ref, y_ref, None, FIRST)


def advance(next_ref, now_ref, older_ref, gain):
    for e in range(next_ref.shape[0]):
        for h in range(next_ref.shape[1]):
            value = gain * (next_ref[e, h] - filter_center * now_ref[e, h])
            next_ref[e, h] = value if older_ref is None else value - older_ref[e, h]


def middle_kernel(*refs, g):
    part_ref, *refs = refs
    received, refs = refs[:6], refs[6:]
    older_ref, mats_ref, y_ref, next_ref, *sends = refs
    y_ref[...] = part_ref[...]
    add_all(g, y_ref, received, FIRST)
    multiply(g, mats_ref, functools.partial(field_of, y_ref), next_ref)
    send_all(g, next_ref, sends)
    advance(next_ref, y_ref, older_ref, LATER)


def late_kernel(*refs, g):
    part_ref, *refs = refs
    received, refs = refs[:6], refs[6:]
    older_ref, mats_ref, next_ref, *sends, y_ref = refs
    y_ref[...] = part_ref[...]
    add_all(g, y_ref, received, LATER)
    multiply(g, mats_ref, functools.partial(field_of, y_ref), next_ref)

    def put_low(ref):
        def put(where, low, high):
            ref[where] = low

        return put

    put_x_face(g, next_ref, put_low(sends[0]))
    put_y_face(g, next_ref, put_low(sends[1]))
    for h in range(next_ref.shape[1]):
        for e3 in range(g.ez):
            rows = slice(e3 * g.side, (e3 + 1) * g.side)
            sends[2][rows, lanes(h)] = line(g, next_ref, 0, 0, e3, h)
    advance(next_ref, y_ref, older_ref, LATER)


def split(value):
    high = value.astype(jnp.bfloat16)
    return high, (value - high.astype(jnp.float32)).astype(jnp.bfloat16)


def packed_rows(bands):
    count = bands // LANES
    return count * bands if count != 2 else bands + 2 * ROWS


def pack(gram, put):
    count = gram.shape[0] // LANES
    block = lambda i, j: gram[lanes(i), lanes(j)]
    if count != 2:
        for i in range(count):
            for j in range(count):
                put((i * count + j) * LANES, block(i, j))
        return
    row = lax.broadcasted_iota(jnp.int32, (LANES, LANES), 0)
    lane = lax.broadcasted_iota(jnp.int32, (LANES, LANES), 1)
    put(0, jnp.where(row >= lane, block(0, 0), block(1, 1)))
    put(LANES, block(1, 0))
    diagonal = jnp.sum(jnp.where(row == lane, block(1, 1), 0.0), axis=0, keepdims=True)
    put(2 * LANES, jnp.broadcast_to(diagonal, (2 * ROWS, LANES)))


def unpack(packed, count):
    block = lambda k: packed[k * LANES : (k + 1) * LANES]
    if count != 2:
        return lambda i, j: block(i * count + j)
    row = lax.broadcasted_iota(jnp.int32, (LANES, LANES), 0)
    lane = lax.broadcasted_iota(jnp.int32, (LANES, LANES), 1)
    both = block(0)
    first = jnp.where(row > lane, both, 0.0)
    second = jnp.where(row < lane, both, 0.0)
    diagonal = jnp.broadcast_to(packed[2 * LANES : 2 * LANES + 1], (LANES, LANES))
    blocks = {
        (0, 0): first + first.T + jnp.where(row == lane, both, 0.0),
        (1, 0): block(1),
        (1, 1): second + second.T + jnp.where(row == lane, diagonal, 0.0),
    }
    return lambda i, j: blocks[i, j]


def last_kernel(part_ref, from_x, from_y, from_xy, *refs, g):
    high_ref, low_ref, kept_ref, sent_ref, y_ref, out_ref, packed_ref = refs
    side = g.side
    y_ref[...] = part_ref[...]
    p, q = lax.axis_index("dx"), lax.axis_index("dy")
    has_x, has_y = p < lax.axis_size("dx") - 1, q < lax.axis_size("dy") - 1
    add_x_face(g, y_ref, True, lambda w: jnp.where(has_x, from_x[w], 0.0), LATER)
    add_y_face(g, y_ref, True, lambda w: jnp.where(has_y, from_y[w], 0.0), LATER)
    add_line(g, y_ref, 1, 1, lambda w: jnp.where(has_x & has_y, from_xy[w], 0.0), LATER)
    sub = lax.broadcasted_iota(jnp.int32, (side, LANES), 0)
    rest = 2 * g.deg - side
    for i in range(g.ex * g.deg):
        e1 = i // g.deg
        a = i + 1 - e1 * g.deg
        for k in range(g.nz):
            e3 = k // g.deg
            rows = g.rows(a, k + 1 - e3 * g.deg, 1)
            for h in range(y_ref.shape[1]):
                d0 = pltpu.roll(y_ref[g.at(e1, 0, e3), h, rows], side - 1, 0)
                d1 = pltpu.roll(y_ref[g.at(e1, 1, e3), h, rows], side - 2, 0)
                start = (i * g.nz + k) * 2 * side
                out_ref[start : start + side, lanes(h)] = jnp.where(sub < g.deg, d0, d1)
                bottom = slice(start + side, start + 2 * side)
                out_ref[bottom, lanes(h)] = jnp.where(sub < rest, d1, 0.0)
    high, low = split(out_ref[...])
    high_ref[...] = high
    low_ref[...] = low
    inner = functools.partial(
        lax.dot_general,
        dimension_numbers=(((0,), (0,)), ((), ())),
        preferred_element_type=jnp.float32,
    )
    mixed = inner(high, low)
    gram = inner(high, high) + (mixed + mixed.T) + inner(low, low)

    def put(start, rows):
        packed_ref[start : start + rows.shape[0]] = rows

    pack(gram, put)
    half = kept_ref.shape[0]
    odd = lax.axis_index("dy") % 2 == 1
    first, second = packed_ref[:half], packed_ref[half:]
    kept_ref[...] = jnp.where(odd, second, first)
    sent_ref[...] = jnp.where(odd, first, second)


def invert_block(block):
    size = block.shape[0]
    groups = size // ROWS
    sub = lax.broadcasted_iota(jnp.int32, (ROWS, size), 0)
    lane = lax.broadcasted_iota(jnp.int32, (ROWS, size), 1)
    left = [block[ROWS * j : ROWS * (j + 1)] for j in range(groups)]
    right = [jnp.where(lane == sub + ROWS * j, 1.0, 0.0) for j in range(groups)]
    spread = lambda row: jnp.broadcast_to(row, (ROWS, size))
    result = []
    for k in range(groups):
        tile = left[k]
        cols = [spread(tile[:, ROWS * k + c : ROWS * k + c + 1]) for c in range(ROWS)]
        s = [[spread(cols[c][r : r + 1]) if c <= r else None for c in range(ROWS)] for r in range(ROWS)]
        inv, mult = [], [[None] * ROWS for _ in range(ROWS)]
        root = []
        for j in range(ROWS):
            inv.append(1.0 / s[j][j])
            root.append(lax.rsqrt(s[j][j]))
            for r in range(j + 1, ROWS):
                mult[r][j] = s[r][j] * inv[j]
            for r in range(j + 1, ROWS):
                for c in range(j + 1, r + 1):
                    s[r][c] = s[r][c] - mult[r][j] * s[c][j]
        last = k == groups - 1
        solved = []
        for source, wanted in ((right[k], True), (tile, False)):
            if last and not wanted:
                continue
            rows = [spread(source[r : r + 1]) for r in range(ROWS)]
            for j in range(ROWS):
                for r in range(j + 1, ROWS):
                    rows[r] = rows[r] - mult[r][j] * rows[j]
            if wanted:
                done = rows[0] * root[0]
                for r in range(1, ROWS):
                    done = jnp.where(sub == r, rows[r] * root[r], done)
                result.append(done)
            if last:
                continue
            rows = [row * d for row, d in zip(rows, inv)]
            for j in reversed(range(ROWS)):
                for r in range(j):
                    rows[r] = rows[r] - mult[j][r] * rows[j]
            solved.append(rows)
        for j in range(k + 1, groups):
            cols = [spread(left[j][:, ROWS * k + c : ROWS * k + c + 1]) for c in range(ROWS)]
            for c in range(ROWS):
                right[j] = right[j] - cols[c] * solved[0][c]
                left[j] = left[j] - cols[c] * solved[1][c]
    return jnp.concatenate(result, axis=0)


def dot(one, two, axis_one=1, axis_two=0):
    return lax.dot_general(
        one,
        two,
        (((axis_one,), (axis_two,)), ((), ())),
        precision=lax.Precision.HIGHEST,
        preferred_element_type=jnp.float32,
    )


def inverse_factor(block_of, count):
    low, inv = {}, {}
    for i in range(count):
        diag = block_of(i, i)
        for j in range(i):
            part = block_of(i, j)
            for k in range(j):
                part = part - dot(low[i, k], low[j, k], 1, 1)
            low[i, j] = dot(part, inv[j, j], 1, 1)
            diag = diag - dot(low[i, j], low[i, j], 1, 1)
        sums = []
        for j in range(i):
            part = dot(low[i, j], inv[j, j])
            for k in range(j + 1, i):
                part = part + dot(low[i, k], inv[k, j])
            sums.append(part)
        inv[i, i] = invert_block(diag)
        for j in range(i):
            inv[i, j] = -dot(inv[i, i], sums[j])
    return inv

def basis_kernel(mine_ref, other_ref, high_ref, low_ref, out_ref, factor_ref, *, scale):
    @pl.when(pl.program_id(0) == 0)
    def _():
        count = high_ref.shape[1] // LANES
        odd = lax.axis_index("dy") % 2 == 1
        mine, other = mine_ref[...], other_ref[...]
        packed = jnp.concatenate(
            [jnp.where(odd, other, mine), jnp.where(odd, mine, other)], axis=0
        )
        inverse = inverse_factor(unpack(packed, count), count)
        for i in range(count):
            for j in range(count):
                block = inverse[i, j] * scale if j <= i else jnp.zeros((LANES, LANES), jnp.float32)
                high, low = split(block)
                factor_ref[0, lanes(i), lanes(j)] = high
                factor_ref[1, lanes(i), lanes(j)] = low

    slab, nz, ny, bands = out_ref.shape
    rows = high_ref.shape[0] // pl.num_programs(0)
    here = pl.ds(pl.multiple_of(pl.program_id(0) * rows, rows), rows)
    times = functools.partial(
        lax.dot_general,
        dimension_numbers=(((1,), (1,)), ((), ())),
        preferred_element_type=jnp.float32,
    )
    high, low = high_ref[here], low_ref[here]
    result = times(high, factor_ref[0]) + (times(high, factor_ref[1]) + times(low, factor_ref[0]))
    result = result.reshape(slab, nz, rows // (slab * nz), bands)
    out_ref[...] = result[:, :, :ny]


def call(kernel, outs, scratch, operands, flops):
    size = sum(x.size * x.dtype.itemsize for x in (*operands, *outs))
    return pl.pallas_call(
        kernel,
        out_shape=outs,
        in_specs=[VMEM] * len(operands),
        out_specs=[VMEM] * len(outs),
        scratch_shapes=scratch,
        compiler_params=pltpu.CompilerParams(vmem_limit_bytes=LIMIT),
        cost_estimate=pl.CostEstimate(flops=flops, bytes_accessed=size, transcendentals=0),
    )(*operands)


def shards(orbitals, elem_mats, conn):
    nx, ny, nz, bands = orbitals.shape
    side = round(elem_mats.shape[-1] ** (1 / 3))
    g = Grid(elem_mats, side)
    f32 = jnp.float32
    orb = jnp.transpose(orbitals, (0, 2, 1, 3))
    below_x = ring(orb[-1], 1, 0)
    below_y = ring(orb[:, :, -1], 0, 1)
    below_xy = ring(orb[-1, :, -1], 1, 1)
    mats = renumber(conn, elem_mats, side, ny + 1, nz + 2)
    mats = mats.reshape(g.elements, g.count, g.count)

    nodes = (g.elements, bands // LANES, g.count, LANES)
    shape = jax.ShapeDtypeStruct
    x_shape = shape((nz, g.ey * side, bands), f32)
    y_shape = shape((g.ex * g.ez, side * side, bands), f32)
    line_shape = shape((g.ez * side, bands), f32)
    corner_shape = shape((2, *line_shape.shape), f32)
    send_shapes = [x_shape] * 2 + [y_shape] * 2
    pairings = [("A", "-"), ("B", "-"), ("-", "A"), ("-", "B")]
    flops = 2 * g.elements * g.count**2 * bands

    def swap(sends):
        faces = [pair_swap(s, *pair) for s, pair in zip(sends, pairings)]
        kernel = functools.partial(corner_kernel, g=g)
        lines = call(kernel, [corner_shape] * 2, [], tuple(faces[:2]), 0)
        return *faces, *[pair_swap(s, *pair) for s, pair in zip(lines, pairings[2:])]

    y0, part, *sends = call(
        functools.partial(first_kernel, g=g),
        [shape(nodes, f32), shape(nodes, f32), *send_shapes],
        [],
        (orb, below_x, below_y, below_xy, mats),
        flops,
    )
    received = swap(sends)
    y1, part, *sends = call(
        functools.partial(middle_kernel, g=g),
        [shape(nodes, f32), shape(nodes, f32), *send_shapes],
        [],
        (part, *received, y0, mats),
        flops,
    )
    received = swap(sends)
    part, *sends = call(
        functools.partial(late_kernel, g=g),
        [shape(nodes, f32), x_shape, y_shape, line_shape],
        [pltpu.VMEM(nodes, f32)],
        (part, *received, y1, mats),
        flops,
    )
    received = [ring(s, *step) for s, step in zip(sends, ((-1, 0), (0, -1), (-1, -1)))]
    rows = nx * nz * 2 * side
    packed = packed_rows(bands)
    half_shape = shape((packed // 2, LANES), f32)
    high, low, kept, sent = call(
        functools.partial(last_kernel, g=g),
        [shape((rows, bands), jnp.bfloat16)] * 2 + [half_shape] * 2,
        [pltpu.VMEM(nodes, f32), pltpu.VMEM((rows, bands), f32), pltpu.VMEM((packed, LANES), f32)],
        (part, *received),
        8 * rows * bands**2,
    )
    mine, other = halved_total(kept, sent)
    slabs = g.ex * g.deg // 2
    spot = pl.BlockSpec((nx // slabs, nz, ny, bands), lambda i: (i, 0, 0, 0))
    basis = pl.pallas_call(
        functools.partial(basis_kernel, scale=math.sqrt(nx * ny * nz * lax.axis_size(AXES))),
        out_shape=shape((nx, nz, ny, bands), f32),
        grid=(slabs,),
        in_specs=[VMEM] * 4,
        out_specs=spot,
        scratch_shapes=[pltpu.VMEM((2, bands, bands), jnp.bfloat16)],
        compiler_params=pltpu.CompilerParams(vmem_limit_bytes=LIMIT),
        name="basis",
    )(mine, other, high, low)
    return jnp.transpose(basis, (0, 2, 1, 3))


def solution(mesh):
    in_specs = (
        P("dx", "dy", None, None),
        P("dx", "dy", None, None, None),
        P("dx", "dy", None, None),
    )
    out_specs = P("dx", "dy", None, None)
    return jax.shard_map(shards, mesh=mesh, in_specs=in_specs, out_specs=out_specs, check_vma=False)
```

```python
import functools
import math

import jax
import jax.numpy as jnp
from jax import lax
from jax.experimental import pallas as pl
from jax.experimental.pallas import tpu as pltpu
from jax.sharding import PartitionSpec as P

filter_center = 1.5
filter_half = 4.0
FIRST = 1.0 / filter_half
LATER = 2.0 / filter_half
AXES = ("dx", "dy")
VMEM = pl.BlockSpec(memory_space=pltpu.VMEM)
LIMIT = 16 * 1024 * 1024
LANES = 128
ROWS = 8


def partner(index, size, pairing, closed):
    if pairing == "-":
        return index
    other = index ^ 1 if pairing == "A" else index - 1 if index % 2 == 0 else index + 1
    if 0 <= other < size:
        return other
    return size - 1 - index if closed and pairing == "B" and size % 2 == 0 else index


def pair_swap(value, along_x, along_y):
    size_x, size_y = lax.axis_size("dx"), lax.axis_size("dy")
    route = [
        (
            p * size_y + q,
            partner(p, size_x, along_x, False) * size_y + partner(q, size_y, along_y, True),
        )
        for p in range(size_x)
        for q in range(size_y)
    ]
    return lax.ppermute(value, AXES, route)


def ring(value, step_x, step_y):
    size_x, size_y = lax.axis_size("dx"), lax.axis_size("dy")
    route = [
        (p * size_y + q, (p + step_x) % size_x * size_y + (q + step_y) % size_y)
        for p in range(size_x)
        for q in range(size_y)
    ]
    return lax.ppermute(value, AXES, route)


def xor_swap(value, axis, bits):
    return lax.ppermute(value, axis, [(i, i ^ bits) for i in range(lax.axis_size(axis))])


def sum_swap(value, stage, bits):
    size_x, size_y = lax.axis_size("dx"), lax.axis_size("dy")
    route = []
    for p in range(size_x):
        for q in range(size_y):
            along_x = (q + stage) % 2 == 0
            to = (p ^ bits, q) if along_x else (p, q ^ 2 * bits)
            route.append((p * size_y + q, to[0] * size_y + to[1]))
    return lax.ppermute(value, AXES, route)


def halved_total(kept, sent):
    part = kept + xor_swap(sent, "dy", 1)
    sizes = lax.axis_size("dx"), lax.axis_size("dy") // 2
    if sizes[0] == sizes[1]:
        steps = [functools.partial(sum_swap, stage=stage) for stage in (0, 1)]
    else:
        steps = [
            lambda value, bits: xor_swap(value, "dx", bits),
            lambda value, bits: xor_swap(value, "dy", 2 * bits),
        ]
    for step, size in zip(steps, sizes):
        bit = 1
        while bit < size:
            if 2 * bit < size:
                one, two, three = [step(part, bits=bit * k) for k in (1, 2, 3)]
                part = (part + one) + (two + three)
                bit *= 4
            else:
                part = part + step(part, bits=bit)
                bit *= 2
    return part, xor_swap(part, "dy", 1)


def renumber_kernel(conn_ref, mats_ref, out_ref, *, g, width, depth):
    side, deg, layers = g.side, g.deg, g.ez
    spots = [
        (e1, e2, e3) for e1 in range(g.ex) for e2 in range(g.ey) for e3 in range(g.ez)
    ]
    for e, (e1, e2, e3) in enumerate(spots):
        node = conn_ref[e1, e2, e3 : e3 + 1].astype(jnp.float32)
        plane = jnp.floor((node + 0.5) * (1.0 / depth))
        first = jnp.floor((plane + 0.5) * (1.0 / width))
        c = (node - plane * depth).astype(jnp.int32) - deg * e3
        b = (plane - first * width).astype(jnp.int32) - deg * e2
        a = first.astype(jnp.int32) - deg * e1
        place = (a * side + c) * side + b
        if e1 == 0:
            place = jnp.where((a == 0) & (lax.axis_index("dx") == 0), -1, place)
        if e2 == 0:
            place = jnp.where((b == 0) & (lax.axis_index("dy") == 0), -1, place)
        if e3 == 0:
            place = jnp.where(c == 0, -1, place)
        if e3 == layers - 1:
            place = jnp.where(c == deg, -1, place)
        order = lax.broadcasted_iota(jnp.int32, (g.count, g.count), 0) == place
        order = jnp.where(order, 1.0, 0.0).astype(jnp.bfloat16)
        half = jnp.dot(order, mats_ref[e], preferred_element_type=jnp.float32)
        whole = lax.dot_general(
            half.astype(jnp.bfloat16),
            order,
            (((1,), (1,)), ((), ())),
            preferred_element_type=jnp.float32,
        )
        out_ref[e] = whole.astype(jnp.bfloat16)


def renumber(g, conn, elem_mats, width, depth):
    shape = (g.elements, g.count, g.count)
    return pl.pallas_call(
        functools.partial(renumber_kernel, g=g, width=width, depth=depth),
        out_shape=jax.ShapeDtypeStruct(shape, jnp.bfloat16),
        in_specs=[VMEM] * 2,
        out_specs=VMEM,
        compiler_params=pltpu.CompilerParams(vmem_limit_bytes=LIMIT),
        cost_estimate=pl.CostEstimate(
            flops=4 * g.elements * g.count**3,
            bytes_accessed=4 * elem_mats.size,
            transcendentals=0,
        ),
        name="renumber",
    )(conn, elem_mats)


class Grid:
    def __init__(self, elem_mats, side):
        self.ex, self.ey, self.ez = elem_mats.shape[:3]
        self.count = elem_mats.shape[3]
        self.side = side
        self.deg = side - 1
        self.nz = self.ez * self.deg - 1
        self.elements = self.ex * self.ey * self.ez

    def at(self, e1, e2, e3):
        return (e1 * self.ey + e2) * self.ez + e3

    def rows(self, a, c, number):
        start = (a * self.side + c) * self.side
        return slice(start, start + number * self.side)

    def layers(self, e3):
        low = 1 if e3 == 0 else 0
        high = self.deg - 1 if e3 == self.ez - 1 else self.deg
        return low, high - low + 1, e3 * self.deg + low - 1

    def side_rows(self, b):
        return pl.ds(b, self.side * self.side, stride=self.side)

    def line_rows(self, a, b):
        return pl.ds(a * self.side * self.side + b, self.side, stride=self.side)


def lanes(h):
    return slice(h * LANES, (h + 1) * LANES)


def multiply(g, mats_ref, field_of, w_ref):
    side, deg = g.side, g.deg
    halves = range(w_ref.shape[1])
    for e in range(g.elements):
        product = jnp.dot(mats_ref[e], field_of(e), preferred_element_type=jnp.float32)
        for h in halves:
            w_ref[e, h] = product[:, lanes(h)]

    def join(one, top, two, bottom):
        for h in halves:
            both = w_ref[one, h, top] + w_ref[two, h, bottom]
            w_ref[one, h, top] = both
            w_ref[two, h, bottom] = both

    for e1 in range(g.ex):
        for e2 in range(g.ey):
            for e3 in range(g.ez - 1):
                for a in range(side):
                    one, two = g.at(e1, e2, e3), g.at(e1, e2, e3 + 1)
                    join(one, g.rows(a, deg, 1), two, g.rows(a, 0, 1))
    for e1 in range(g.ex - 1):
        for e2 in range(g.ey):
            for e3 in range(g.ez):
                one, two = g.at(e1, e2, e3), g.at(e1 + 1, e2, e3)
                join(one, g.rows(deg, 0, side), two, g.rows(0, 0, side))
    for e1 in range(g.ex):
        for e2 in range(g.ey - 1):
            for e3 in range(g.ez):
                one, two = g.at(e1, e2, e3), g.at(e1, e2 + 1, e3)
                join(one, g.side_rows(deg), two, g.side_rows(0))


def put_x_face(g, w_ref, put):
    for h in range(w_ref.shape[1]):
        for e2 in range(g.ey):
            for e3 in range(g.ez):
                low, number, start = g.layers(e3)
                if e3 > 0:
                    low, number, start = low + 1, number - 1, start + 1
                one = w_ref[g.at(0, e2, e3), h, g.rows(0, low, number)]
                two = w_ref[g.at(g.ex - 1, e2, e3), h, g.rows(g.deg, low, number)]
                where = (
                    slice(start, start + number),
                    slice(e2 * g.side, (e2 + 1) * g.side),
                    lanes(h),
                )
                shape = (number, g.side, LANES)
                put(where, one.reshape(shape), two.reshape(shape))


def put_y_face(g, w_ref, put):
    for h in range(w_ref.shape[1]):
        for e1 in range(g.ex):
            for e3 in range(g.ez):
                one = w_ref[g.at(e1, 0, e3), h, g.side_rows(0)]
                two = w_ref[g.at(e1, g.ey - 1, e3), h, g.side_rows(g.deg)]
                put((e1 * g.ez + e3, slice(None), lanes(h)), one, two)


def line(g, w_ref, high_x, high_y, e3, h):
    e1, a = (g.ex - 1, g.deg) if high_x else (0, 0)
    e2, b = (g.ey - 1, g.deg) if high_y else (0, 0)
    return w_ref[g.at(e1, e2, e3), h, g.line_rows(a, b)]


def add_x_face(g, out_ref, high, received, factor):
    e1, a = (g.ex - 1, g.deg) if high else (0, 0)
    for h in range(out_ref.shape[1]):
        for e2 in range(g.ey):
            for e3 in range(g.ez):
                low, number, start = g.layers(e3)
                columns = slice(e2 * g.side, (e2 + 1) * g.side)
                part = received((slice(start, start + number), columns, lanes(h)))
                rows = g.rows(a, low, number)
                part = part.reshape(number * g.side, LANES)
                out_ref[g.at(e1, e2, e3), h, rows] += factor * part


def add_y_face(g, out_ref, high, received, factor):
    e2, b = (g.ey - 1, g.deg) if high else (0, 0)
    for h in range(out_ref.shape[1]):
        for e1 in range(g.ex):
            for e3 in range(g.ez):
                part = received((e1 * g.ez + e3, slice(None), lanes(h)))
                out_ref[g.at(e1, e2, e3), h, g.side_rows(b)] += factor * part


def add_line(g, out_ref, high_x, high_y, received, factor):
    e1, a = (g.ex - 1, g.deg) if high_x else (0, 0)
    e2, b = (g.ey - 1, g.deg) if high_y else (0, 0)
    for h in range(out_ref.shape[1]):
        for e3 in range(g.ez):
            part = received((slice(e3 * g.side, (e3 + 1) * g.side), lanes(h)))
            out_ref[g.at(e1, e2, e3), h, g.line_rows(a, b)] += factor * part


def send_all(g, w_ref, sends):
    even_x = lax.axis_index("dx") % 2 == 0
    even_y = lax.axis_index("dy") % 2 == 0

    def by_pair(even, one_ref, two_ref):
        def put(where, low, high):
            one_ref[where] = jnp.where(even, high, low)
            two_ref[where] = jnp.where(even, low, high)

        return put

    put_x_face(g, w_ref, by_pair(even_x, sends[0], sends[1]))
    put_y_face(g, w_ref, by_pair(even_y, sends[2], sends[3]))


def corner_kernel(from_a, from_b, to_a, to_b, *, g):
    even = lax.axis_index("dy") % 2 == 0
    last = from_a.shape[1] - 1
    bands = from_a.shape[2]
    for k, source in enumerate((from_a, from_b)):
        for e3 in range(g.ez):
            low, number, start = g.layers(e3)
            for c in range(g.side):
                row = slice(e3 * g.side + c, e3 * g.side + c + 1)
                if low <= c < low + number:
                    z = start + c - low
                    bottom, top = source[z, 0:1], source[z, last : last + 1]
                    to_a[k, row] = jnp.where(even, top, bottom)
                    to_b[k, row] = jnp.where(even, bottom, top)
                else:
                    to_a[k, row] = jnp.zeros((1, bands), jnp.float32)
                    to_b[k, row] = jnp.zeros((1, bands), jnp.float32)


def add_all(g, out_ref, received, factor):
    p, q = lax.axis_index("dx"), lax.axis_index("dy")
    even_x, even_y = p % 2 == 0, q % 2 == 0
    has_x = (p > 0, p < lax.axis_size("dx") - 1)
    has_y = (q > 0, q < lax.axis_size("dy") - 1)

    def from_pair(even, high, one, two, exists):
        value = jnp.where(even, one, two) if high else jnp.where(even, two, one)
        return jnp.where(exists, value, 0.0)

    for high in (0, 1):

        def across_x(where):
            return from_pair(even_x, high, received[0][where], received[1][where], has_x[high])

        def across_y(where):
            return from_pair(even_y, high, received[2][where], received[3][where], has_y[high])

        add_x_face(g, out_ref, high, across_x, factor)
        add_y_face(g, out_ref, high, across_y, factor)
    for hx in (0, 1):
        for hy in (0, 1):

            def diagonal(where):
                one, two = [
                    from_pair(even_y, hy, received[4][k, *where], received[5][k, *where], has_y[hy])
                    for k in (0, 1)
                ]
                return from_pair(even_x, hx, one, two, has_x[hx])

            add_line(g, out_ref, hx, hy, diagonal, factor)


def field_of(y_ref, e):
    parts = [y_ref[e, h].astype(jnp.bfloat16) for h in range(y_ref.shape[1])]
    return jnp.concatenate(parts, axis=-1)


def edge_kernel(orb_ref, mats_ref, conn_ref, x_ref, y_ref, line_ref, tiles_ref):
    del mats_ref, conn_ref
    nx, nz, ny, bands = orb_ref.shape
    last = (ny - 1) % ROWS
    tail = slice(ny - 1 - last, ny)
    x_ref[...] = orb_ref[nx - 1]
    for h in range(bands // LANES):
        for i in range(nx):
            part = orb_ref[i, :, tail, lanes(h)].astype(jnp.float32)
            for k in range(nz):
                start = (i * nz + k) * ROWS
                tiles_ref[h, start : start + last + 1] = part[k]
        rows = tiles_ref[h, pl.ds(last, y_ref.shape[0], stride=ROWS)]
        y_ref[:, lanes(h)] = rows.astype(jnp.bfloat16)
        line = tiles_ref[h, pl.ds((nx - 1) * nz * ROWS + last, line_ref.shape[0], stride=ROWS)]
        line_ref[:, lanes(h)] = line.astype(jnp.bfloat16)


def first_kernel(*refs, g):
    orb_ref, below_x, below_y, below_xy, mats_ref, y_ref, next_ref, *sends = refs
    side = g.side
    halves = range(y_ref.shape[1])
    sub = lax.broadcasted_iota(jnp.int32, (side, LANES), 0)
    nothing = jnp.zeros((side, LANES), jnp.float32)
    rest = orb_ref.shape[2] - side
    for e1 in range(g.ex):
        for e2 in range(g.ey):
            for a in range(side):
                for h in halves:
                    y_ref[g.at(e1, e2, 0), h, g.rows(a, 0, 1)] = nothing
                    y_ref[g.at(e1, e2, g.ez - 1), h, g.rows(a, g.deg, 1)] = nothing

    def place(i, k, column, edge):
        for h in halves:
            part = column[:, lanes(h)].astype(jnp.float32)
            t0 = part[:side]
            t1 = jnp.concatenate([part[side:], nothing[: side - rest]], axis=0)
            first = jnp.broadcast_to(edge[:, lanes(h)].astype(jnp.float32), (side, LANES))
            d0 = jnp.where(sub == 0, first, pltpu.roll(t0, 1, 0))
            d1 = jnp.where(sub < 2, pltpu.roll(t0, 2, 0), pltpu.roll(t1, 2, 0))
            for e1 in range(g.ex):
                a = i - e1 * g.deg
                for e3 in range(g.ez):
                    c = k + 1 - e3 * g.deg
                    if 0 <= a <= g.deg and 0 <= c <= g.deg:
                        y_ref[g.at(e1, 0, e3), h, g.rows(a, c, 1)] = d0
                        y_ref[g.at(e1, 1, e3), h, g.rows(a, c, 1)] = d1

    for k in range(g.nz):
        place(0, k, below_x[k], below_xy[k : k + 1])
        for i in range(orb_ref.shape[0]):
            place(i + 1, k, orb_ref[i, k], below_y[i * g.nz + k : i * g.nz + k + 1])
    multiply(g, mats_ref, functools.partial(field_of, y_ref), next_ref)
    send_all(g, next_ref, sends)
    advance(next_ref, y_ref, None, FIRST)


def advance(next_ref, now_ref, older_ref, gain):
    for e in range(next_ref.shape[0]):
        for h in range(next_ref.shape[1]):
            value = gain * (next_ref[e, h] - filter_center * now_ref[e, h])
            next_ref[e, h] = value if older_ref is None else value - older_ref[e, h]


def middle_kernel(*refs, g):
    part_ref, *refs = refs
    received, refs = refs[:6], refs[6:]
    older_ref, mats_ref, y_ref, next_ref, *sends = refs
    y_ref[...] = part_ref[...]
    add_all(g, y_ref, received, FIRST)
    multiply(g, mats_ref, functools.partial(field_of, y_ref), next_ref)
    send_all(g, next_ref, sends)
    advance(next_ref, y_ref, older_ref, LATER)


def late_kernel(*refs, g):
    part_ref, *refs = refs
    received, refs = refs[:6], refs[6:]
    older_ref, mats_ref, next_ref, *sends, y_ref = refs
    y_ref[...] = part_ref[...]
    add_all(g, y_ref, received, LATER)
    multiply(g, mats_ref, functools.partial(field_of, y_ref), next_ref)

    def put_low(ref):
        def put(where, low, high):
            ref[where] = low

        return put

    put_x_face(g, next_ref, put_low(sends[0]))
    put_y_face(g, next_ref, put_low(sends[1]))
    for h in range(next_ref.shape[1]):
        for e3 in range(g.ez):
            rows = slice(e3 * g.side, (e3 + 1) * g.side)
            sends[2][rows, lanes(h)] = line(g, next_ref, 0, 0, e3, h)
    advance(next_ref, y_ref, older_ref, LATER)


def split(value):
    high = value.astype(jnp.bfloat16)
    return high, (value - high.astype(jnp.float32)).astype(jnp.bfloat16)


def packed_rows(bands):
    count = bands // LANES
    return count * bands if count != 2 else bands + 2 * ROWS


def pack(gram, put):
    count = gram.shape[0] // LANES
    block = lambda i, j: gram[lanes(i), lanes(j)]
    if count != 2:
        for i in range(count):
            for j in range(count):
                put((i * count + j) * LANES, block(i, j))
        return
    row = lax.broadcasted_iota(jnp.int32, (LANES, LANES), 0)
    lane = lax.broadcasted_iota(jnp.int32, (LANES, LANES), 1)
    put(0, jnp.where(row >= lane, block(0, 0), block(1, 1)))
    put(LANES, block(1, 0))
    diagonal = jnp.sum(jnp.where(row == lane, block(1, 1), 0.0), axis=0, keepdims=True)
    put(2 * LANES, jnp.broadcast_to(diagonal, (2 * ROWS, LANES)))


def unpack(packed, count):
    block = lambda k: packed[k * LANES : (k + 1) * LANES]
    if count != 2:
        return lambda i, j: block(i * count + j)
    row = lax.broadcasted_iota(jnp.int32, (LANES, LANES), 0)
    lane = lax.broadcasted_iota(jnp.int32, (LANES, LANES), 1)
    both = block(0)
    first = jnp.where(row > lane, both, 0.0)
    second = jnp.where(row < lane, both, 0.0)
    diagonal = jnp.broadcast_to(packed[2 * LANES : 2 * LANES + 1], (LANES, LANES))
    blocks = {
        (0, 0): first + first.T + jnp.where(row == lane, both, 0.0),
        (1, 0): block(1),
        (1, 1): second + second.T + jnp.where(row == lane, diagonal, 0.0),
    }
    return lambda i, j: blocks[i, j]


def last_kernel(part_ref, from_x, from_y, from_xy, *refs, g):
    high_ref, low_ref, kept_ref, sent_ref, y_ref, out_ref, packed_ref = refs
    side = g.side
    y_ref[...] = part_ref[...]
    p, q = lax.axis_index("dx"), lax.axis_index("dy")
    has_x, has_y = p < lax.axis_size("dx") - 1, q < lax.axis_size("dy") - 1
    add_x_face(g, y_ref, True, lambda w: jnp.where(has_x, from_x[w], 0.0), LATER)
    add_y_face(g, y_ref, True, lambda w: jnp.where(has_y, from_y[w], 0.0), LATER)
    add_line(g, y_ref, 1, 1, lambda w: jnp.where(has_x & has_y, from_xy[w], 0.0), LATER)
    sub = lax.broadcasted_iota(jnp.int32, (side, LANES), 0)
    rest = 2 * g.deg - side
    for i in range(g.ex * g.deg):
        e1 = i // g.deg
        a = i + 1 - e1 * g.deg
        for k in range(g.nz):
            e3 = k // g.deg
            rows = g.rows(a, k + 1 - e3 * g.deg, 1)
            for h in range(y_ref.shape[1]):
                d0 = pltpu.roll(y_ref[g.at(e1, 0, e3), h, rows], side - 1, 0)
                d1 = pltpu.roll(y_ref[g.at(e1, 1, e3), h, rows], side - 2, 0)
                start = (i * g.nz + k) * 2 * side
                out_ref[start : start + side, lanes(h)] = jnp.where(sub < g.deg, d0, d1)
                bottom = slice(start + side, start + 2 * side)
                out_ref[bottom, lanes(h)] = jnp.where(sub < rest, d1, 0.0)
    high, low = split(out_ref[...])
    high_ref[...] = high
    low_ref[...] = low
    inner = functools.partial(
        lax.dot_general,
        dimension_numbers=(((0,), (0,)), ((), ())),
        preferred_element_type=jnp.float32,
    )
    mixed = inner(high, low)
    gram = inner(high, high) + (mixed + mixed.T) + inner(low, low)

    def put(start, rows):
        packed_ref[start : start + rows.shape[0]] = rows

    pack(gram, put)
    half = kept_ref.shape[0]
    odd = lax.axis_index("dy") % 2 == 1
    first, second = packed_ref[:half], packed_ref[half:]
    kept_ref[...] = jnp.where(odd, second, first)
    sent_ref[...] = jnp.where(odd, first, second)


def invert_block(block):
    size = block.shape[0]
    groups = size // ROWS
    sub = lax.broadcasted_iota(jnp.int32, (ROWS, size), 0)
    lane = lax.broadcasted_iota(jnp.int32, (ROWS, size), 1)
    left = [block[ROWS * j : ROWS * (j + 1)] for j in range(groups)]
    right = [jnp.where(lane == sub + ROWS * j, 1.0, 0.0) for j in range(groups)]
    spread = lambda row: jnp.broadcast_to(row, (ROWS, size))
    result = []
    for k in range(groups):
        tile = left[k]
        cols = [spread(tile[:, ROWS * k + c : ROWS * k + c + 1]) for c in range(ROWS)]
        s = [[spread(cols[c][r : r + 1]) if c <= r else None for c in range(ROWS)] for r in range(ROWS)]
        take = [[None] * ROWS for _ in range(ROWS)]
        pairs = {}
        for j in range(0, ROWS, 2):
            p, q, t = s[j][j], s[j + 1][j], s[j + 1][j + 1]
            over = 1.0 / (p * t - q * q)
            across = q * (1.0 / p)
            pairs[j] = (
                (t * over, q * over, p * over),
                across,
                lax.rsqrt(p),
                lax.rsqrt(t - across * q),
            )
            one, both, two = pairs[j][0]
            for r in range(j + 2, ROWS):
                take[r][j] = s[r][j] * one - s[r][j + 1] * both
                take[r][j + 1] = s[r][j + 1] * two - s[r][j] * both
                for c in range(j + 2, r + 1):
                    s[r][c] = s[r][c] - (take[r][j] * s[c][j] + take[r][j + 1] * s[c][j + 1])
        last = k == groups - 1
        solved = []
        for source, wanted in ((right[k], True), (tile, False)):
            if last and not wanted:
                continue
            rows = [spread(source[r : r + 1]) for r in range(ROWS)]
            for j in range(0, ROWS, 2):
                for r in range(j + 2, ROWS):
                    rows[r] = rows[r] - (take[r][j] * rows[j] + take[r][j + 1] * rows[j + 1])
            if wanted:
                done = jnp.zeros((ROWS, size), jnp.float32)
                for j in range(0, ROWS, 2):
                    _, across, scale, scale_next = pairs[j]
                    done = jnp.where(sub == j, rows[j] * scale, done)
                    below = (rows[j + 1] - across * rows[j]) * scale_next
                    done = jnp.where(sub == j + 1, below, done)
                result.append(done)
            if last:
                continue
            for j in range(0, ROWS, 2):
                one, both, two = pairs[j][0]
                rows[j], rows[j + 1] = (
                    one * rows[j] - both * rows[j + 1],
                    two * rows[j + 1] - both * rows[j],
                )
            for j in reversed(range(0, ROWS, 2)):
                for r in range(j):
                    rows[r] = rows[r] - (take[j][r] * rows[j] + take[j + 1][r] * rows[j + 1])
            solved.append(rows)

        def tree(terms):
            while len(terms) > 1:
                terms = [a + b for a, b in zip(terms[::2], terms[1::2])]
            return terms[0]

        for j in range(k + 1, groups):
            cols = [spread(left[j][:, ROWS * k + c : ROWS * k + c + 1]) for c in range(ROWS)]
            left[j] = left[j] - tree([cols[c] * solved[1][c] for c in range(ROWS)])
            right[j] = right[j] - tree([cols[c] * solved[0][c] for c in range(ROWS)])
    return jnp.concatenate(result, axis=0)


def dot(one, two, axis_one=1, axis_two=0):
    return lax.dot_general(
        one,
        two,
        (((axis_one,), (axis_two,)), ((), ())),
        precision=lax.Precision.HIGHEST,
        preferred_element_type=jnp.float32,
    )


def inverse_factor(block_of, count):
    low, inv = {}, {}
    for i in range(count):
        diag = block_of(i, i)
        for j in range(i):
            part = block_of(i, j)
            for k in range(j):
                part = part - dot(low[i, k], low[j, k], 1, 1)
            low[i, j] = dot(part, inv[j, j], 1, 1)
            diag = diag - dot(low[i, j], low[i, j], 1, 1)
        sums = []
        for j in range(i):
            part = dot(low[i, j], inv[j, j])
            for k in range(j + 1, i):
                part = part + dot(low[i, k], inv[k, j])
            sums.append(part)
        inv[i, i] = invert_block(diag)
        for j in range(i):
            inv[i, j] = -dot(inv[i, i], sums[j])
    return inv

def basis_kernel(mine_ref, other_ref, high_ref, low_ref, out_ref, factor_ref, *, scale):
    @pl.when(pl.program_id(0) == 0)
    def _():
        count = high_ref.shape[1] // LANES
        odd = lax.axis_index("dy") % 2 == 1
        mine, other = mine_ref[...], other_ref[...]
        packed = jnp.concatenate(
            [jnp.where(odd, other, mine), jnp.where(odd, mine, other)], axis=0
        )
        inverse = inverse_factor(unpack(packed, count), count)
        for i in range(count):
            for j in range(count):
                block = inverse[i, j] * scale if j <= i else jnp.zeros((LANES, LANES), jnp.float32)
                high, low = split(block)
                factor_ref[0, lanes(i), lanes(j)] = high
                factor_ref[1, lanes(i), lanes(j)] = low

    slab, nz, ny, bands = out_ref.shape
    rows = high_ref.shape[0] // pl.num_programs(0)
    here = pl.ds(pl.multiple_of(pl.program_id(0) * rows, rows), rows)
    times = functools.partial(
        lax.dot_general,
        dimension_numbers=(((1,), (1,)), ((), ())),
        preferred_element_type=jnp.float32,
    )
    high, low = high_ref[here], low_ref[here]
    result = times(high, factor_ref[0]) + (times(high, factor_ref[1]) + times(low, factor_ref[0]))
    result = result.reshape(slab, nz, rows // (slab * nz), bands)
    out_ref[...] = result[:, :, :ny]


def call(kernel, outs, scratch, operands, flops):
    size = sum(x.size * x.dtype.itemsize for x in (*operands, *outs))
    return pl.pallas_call(
        kernel,
        out_shape=outs,
        in_specs=[VMEM] * len(operands),
        out_specs=[VMEM] * len(outs),
        scratch_shapes=scratch,
        compiler_params=pltpu.CompilerParams(vmem_limit_bytes=LIMIT),
        cost_estimate=pl.CostEstimate(flops=flops, bytes_accessed=size, transcendentals=0),
    )(*operands)


def shards(orbitals, elem_mats, conn):
    nx, ny, nz, bands = orbitals.shape
    side = round(elem_mats.shape[-1] ** (1 / 3))
    g = Grid(elem_mats, side)
    elem_mats = elem_mats.reshape(g.elements, g.count, g.count)
    f32 = jnp.float32
    orb = jnp.transpose(orbitals, (0, 2, 1, 3))
    shape = jax.ShapeDtypeStruct
    plane = -(-nx * nz // (2 * ROWS)) * 2 * ROWS
    tall = (plane + 2 * ROWS) * ROWS
    edges = call(
        edge_kernel,
        [
            shape((nz, ny, bands), orb.dtype),
            shape((plane, bands), orb.dtype),
            shape((2 * ROWS, bands), orb.dtype),
        ],
        [pltpu.VMEM((bands // LANES, tall, LANES), f32)],
        (orb, elem_mats, conn),
        0,
    )
    below_x, below_y, below_xy = [
        ring(s, *step) for s, step in zip(edges, ((1, 0), (0, 1), (1, 1)))
    ]
    mats = renumber(g, conn, elem_mats, ny + 1, nz + 2)

    nodes = (g.elements, bands // LANES, g.count, LANES)
    x_shape = shape((nz, g.ey * side, bands), f32)
    y_shape = shape((g.ex * g.ez, side * side, bands), f32)
    line_shape = shape((g.ez * side, bands), f32)
    corner_shape = shape((2, *line_shape.shape), f32)
    send_shapes = [x_shape] * 2 + [y_shape] * 2
    pairings = [("A", "-"), ("B", "-"), ("-", "A"), ("-", "B")]
    flops = 2 * g.elements * g.count**2 * bands

    def swap(sends):
        faces = [pair_swap(s, *pair) for s, pair in zip(sends, pairings)]
        kernel = functools.partial(corner_kernel, g=g)
        lines = call(kernel, [corner_shape] * 2, [], tuple(faces[:2]), 0)
        return *faces, *[pair_swap(s, *pair) for s, pair in zip(lines, pairings[2:])]

    y0, part, *sends = call(
        functools.partial(first_kernel, g=g),
        [shape(nodes, f32), shape(nodes, f32), *send_shapes],
        [],
        (orb, below_x, below_y, below_xy, mats),
        flops,
    )
    received = swap(sends)
    y1, part, *sends = call(
        functools.partial(middle_kernel, g=g),
        [shape(nodes, f32), shape(nodes, f32), *send_shapes],
        [],
        (part, *received, y0, mats),
        flops,
    )
    received = swap(sends)
    part, *sends = call(
        functools.partial(late_kernel, g=g),
        [shape(nodes, f32), x_shape, y_shape, line_shape],
        [pltpu.VMEM(nodes, f32)],
        (part, *received, y1, mats),
        flops,
    )
    received = [ring(s, *step) for s, step in zip(sends, ((-1, 0), (0, -1), (-1, -1)))]
    rows = nx * nz * 2 * side
    packed = packed_rows(bands)
    half_shape = shape((packed // 2, LANES), f32)
    high, low, kept, sent = call(
        functools.partial(last_kernel, g=g),
        [shape((rows, bands), jnp.bfloat16)] * 2 + [half_shape] * 2,
        [pltpu.VMEM(nodes, f32), pltpu.VMEM((rows, bands), f32), pltpu.VMEM((packed, LANES), f32)],
        (part, *received),
        8 * rows * bands**2,
    )
    mine, other = halved_total(kept, sent)
    slabs = g.ex * g.deg // 2
    spot = pl.BlockSpec((nx // slabs, nz, ny, bands), lambda i: (i, 0, 0, 0))
    basis = pl.pallas_call(
        functools.partial(basis_kernel, scale=math.sqrt(nx * ny * nz * lax.axis_size(AXES))),
        out_shape=shape((nx, nz, ny, bands), f32),
        grid=(slabs,),
        in_specs=[VMEM] * 4,
        out_specs=spot,
        scratch_shapes=[pltpu.VMEM((2, bands, bands), jnp.bfloat16)],
        compiler_params=pltpu.CompilerParams(vmem_limit_bytes=LIMIT),
        name="basis",
    )(mine, other, high, low)
    return jnp.transpose(basis, (0, 2, 1, 3))


def solution(mesh):
    in_specs = (
        P("dx", "dy", None, None),
        P("dx", "dy", None, None, None),
        P("dx", "dy", None, None),
    )
    out_specs = P("dx", "dy", None, None)
    return jax.shard_map(shards, mesh=mesh, in_specs=in_specs, out_specs=out_specs, check_vma=False)
```

```python
import functools
import math

import jax
import jax.numpy as jnp
from jax import lax
from jax.experimental import pallas as pl
from jax.experimental.pallas import tpu as pltpu
from jax.sharding import PartitionSpec as P

filter_center = 1.5
filter_half = 4.0
FIRST = 1.0 / filter_half
LATER = 2.0 / filter_half
AXES = ("dx", "dy")
VMEM = pl.BlockSpec(memory_space=pltpu.VMEM)
LIMIT = 16 * 1024 * 1024
LANES = 128
ROWS = 8


def partner(index, size, pairing, closed):
    if pairing == "-":
        return index
    other = index ^ 1 if pairing == "A" else index - 1 if index % 2 == 0 else index + 1
    if 0 <= other < size:
        return other
    return size - 1 - index if closed and pairing == "B" and size % 2 == 0 else index


def pair_swap(value, along_x, along_y):
    size_x, size_y = lax.axis_size("dx"), lax.axis_size("dy")
    route = [
        (
            p * size_y + q,
            partner(p, size_x, along_x, False) * size_y + partner(q, size_y, along_y, True),
        )
        for p in range(size_x)
        for q in range(size_y)
    ]
    return lax.ppermute(value, AXES, route)


def ring(value, step_x, step_y):
    size_x, size_y = lax.axis_size("dx"), lax.axis_size("dy")
    route = [
        (p * size_y + q, (p + step_x) % size_x * size_y + (q + step_y) % size_y)
        for p in range(size_x)
        for q in range(size_y)
    ]
    return lax.ppermute(value, AXES, route)


def xor_swap(value, axis, bits):
    return lax.ppermute(value, axis, [(i, i ^ bits) for i in range(lax.axis_size(axis))])


def sum_swap(value, stage, bits):
    size_x, size_y = lax.axis_size("dx"), lax.axis_size("dy")
    route = []
    for p in range(size_x):
        for q in range(size_y):
            along_x = (q + stage) % 2 == 0
            to = (p ^ bits, q) if along_x else (p, q ^ 2 * bits)
            route.append((p * size_y + q, to[0] * size_y + to[1]))
    return lax.ppermute(value, AXES, route)


def halved_total(kept, sent):
    part = kept + xor_swap(sent, "dy", 1)
    sizes = lax.axis_size("dx"), lax.axis_size("dy") // 2
    if sizes[0] == sizes[1]:
        steps = [functools.partial(sum_swap, stage=stage) for stage in (0, 1)]
    else:
        steps = [
            lambda value, bits: xor_swap(value, "dx", bits),
            lambda value, bits: xor_swap(value, "dy", 2 * bits),
        ]
    for step, size in zip(steps, sizes):
        bit = 1
        while bit < size:
            if 2 * bit < size:
                one, two, three = [step(part, bits=bit * k) for k in (1, 2, 3)]
                part = (part + one) + (two + three)
                bit *= 4
            else:
                part = part + step(part, bits=bit)
                bit *= 2
    return part, xor_swap(part, "dy", 1)


def renumber_kernel(conn_ref, mats_ref, out_ref, *, g, width, depth):
    side, deg, layers = g.side, g.deg, g.ez
    spots = [
        (e1, e2, e3) for e1 in range(g.ex) for e2 in range(g.ey) for e3 in range(g.ez)
    ]
    for e, (e1, e2, e3) in enumerate(spots):
        node = conn_ref[e1, e2, e3 : e3 + 1].astype(jnp.float32)
        plane = jnp.floor((node + 0.5) * (1.0 / depth))
        first = jnp.floor((plane + 0.5) * (1.0 / width))
        c = (node - plane * depth).astype(jnp.int32) - deg * e3
        b = (plane - first * width).astype(jnp.int32) - deg * e2
        a = first.astype(jnp.int32) - deg * e1
        place = (a * side + c) * side + b
        if e1 == 0:
            place = jnp.where((a == 0) & (lax.axis_index("dx") == 0), -1, place)
        if e2 == 0:
            place = jnp.where((b == 0) & (lax.axis_index("dy") == 0), -1, place)
        if e3 == 0:
            place = jnp.where(c == 0, -1, place)
        if e3 == layers - 1:
            place = jnp.where(c == deg, -1, place)
        order = lax.broadcasted_iota(jnp.int32, (g.count, g.count), 0) == place
        order = jnp.where(order, 1.0, 0.0).astype(jnp.bfloat16)
        half = jnp.dot(order, mats_ref[e], preferred_element_type=jnp.float32)
        whole = lax.dot_general(
            half.astype(jnp.bfloat16),
            order,
            (((1,), (1,)), ((), ())),
            preferred_element_type=jnp.float32,
        )
        out_ref[e] = whole.astype(jnp.bfloat16)


def renumber(g, conn, elem_mats, width, depth):
    shape = (g.elements, g.count, g.count)
    return pl.pallas_call(
        functools.partial(renumber_kernel, g=g, width=width, depth=depth),
        out_shape=jax.ShapeDtypeStruct(shape, jnp.bfloat16),
        in_specs=[VMEM] * 2,
        out_specs=VMEM,
        compiler_params=pltpu.CompilerParams(vmem_limit_bytes=LIMIT),
        cost_estimate=pl.CostEstimate(
            flops=4 * g.elements * g.count**3,
            bytes_accessed=4 * elem_mats.size,
            transcendentals=0,
        ),
        name="renumber",
    )(conn, elem_mats)


class Grid:
    def __init__(self, elem_mats, side):
        self.ex, self.ey, self.ez = elem_mats.shape[:3]
        self.count = elem_mats.shape[3]
        self.side = side
        self.deg = side - 1
        self.nz = self.ez * self.deg - 1
        self.elements = self.ex * self.ey * self.ez

    def at(self, e1, e2, e3):
        return (e1 * self.ey + e2) * self.ez + e3

    def rows(self, a, c, number):
        start = (a * self.side + c) * self.side
        return slice(start, start + number * self.side)

    def layers(self, e3):
        low = 1 if e3 == 0 else 0
        high = self.deg - 1 if e3 == self.ez - 1 else self.deg
        return low, high - low + 1, e3 * self.deg + low - 1

    def side_rows(self, b):
        return pl.ds(b, self.side * self.side, stride=self.side)

    def line_rows(self, a, b):
        return pl.ds(a * self.side * self.side + b, self.side, stride=self.side)


def lanes(h):
    return slice(h * LANES, (h + 1) * LANES)


def multiply(g, mats_ref, field_of, w_ref):
    side, deg = g.side, g.deg
    halves = range(w_ref.shape[1])
    for e in range(g.elements):
        product = jnp.dot(mats_ref[e], field_of(e), preferred_element_type=jnp.float32)
        for h in halves:
            w_ref[e, h] = product[:, lanes(h)]

    def join(one, top, two, bottom):
        for h in halves:
            both = w_ref[one, h, top] + w_ref[two, h, bottom]
            w_ref[one, h, top] = both
            w_ref[two, h, bottom] = both

    for e1 in range(g.ex):
        for e2 in range(g.ey):
            for e3 in range(g.ez - 1):
                for a in range(side):
                    one, two = g.at(e1, e2, e3), g.at(e1, e2, e3 + 1)
                    join(one, g.rows(a, deg, 1), two, g.rows(a, 0, 1))
    for e1 in range(g.ex - 1):
        for e2 in range(g.ey):
            for e3 in range(g.ez):
                one, two = g.at(e1, e2, e3), g.at(e1 + 1, e2, e3)
                join(one, g.rows(deg, 0, side), two, g.rows(0, 0, side))
    for e1 in range(g.ex):
        for e2 in range(g.ey - 1):
            for e3 in range(g.ez):
                one, two = g.at(e1, e2, e3), g.at(e1, e2 + 1, e3)
                join(one, g.side_rows(deg), two, g.side_rows(0))


def rest_of(value):
    return value - value.astype(jnp.bfloat16).astype(jnp.float32)


def put_x_face(g, w_ref, put):
    for h in range(w_ref.shape[1]):
        for e2 in range(g.ey):
            for e3 in range(g.ez):
                low, number, start = g.layers(e3)
                if e3 > 0:
                    low, number, start = low + 1, number - 1, start + 1
                one = w_ref[g.at(0, e2, e3), h, g.rows(0, low, number)]
                two = w_ref[g.at(g.ex - 1, e2, e3), h, g.rows(g.deg, low, number)]
                where = (
                    slice(start, start + number),
                    slice(e2 * g.side, (e2 + 1) * g.side),
                    lanes(h),
                )
                shape = (number, g.side, LANES)
                put(where, one.reshape(shape), two.reshape(shape))
                if e3 < g.ez - 1:
                    one, two = one[-g.side :], two[-g.side :]
                    put((g.nz + e3, *where[1:]), rest_of(one), rest_of(two))


def put_y_face(g, w_ref, put):
    for h in range(w_ref.shape[1]):
        for e1 in range(g.ex):
            for e3 in range(g.ez):
                one = w_ref[g.at(e1, 0, e3), h, g.side_rows(0)]
                two = w_ref[g.at(e1, g.ey - 1, e3), h, g.side_rows(g.deg)]
                if e3 > 0:
                    layer = lax.broadcasted_iota(jnp.int32, one.shape, 0) % g.side
                    one = jnp.where(layer == 0, rest_of(one), one)
                    two = jnp.where(layer == 0, rest_of(two), two)
                put((e1 * g.ez + e3, slice(None), lanes(h)), one, two)


def line(g, w_ref, high_x, high_y, e3, h):
    e1, a = (g.ex - 1, g.deg) if high_x else (0, 0)
    e2, b = (g.ey - 1, g.deg) if high_y else (0, 0)
    return w_ref[g.at(e1, e2, e3), h, g.line_rows(a, b)]


def add_x_face(g, out_ref, high, received, factor):
    e1, a = (g.ex - 1, g.deg) if high else (0, 0)
    for h in range(out_ref.shape[1]):
        for e2 in range(g.ey):
            for e3 in range(g.ez):
                low, number, start = g.layers(e3)
                columns = slice(e2 * g.side, (e2 + 1) * g.side)
                part = received((slice(start, start + number), columns, lanes(h)))
                rows = g.rows(a, low, number)
                part = part.reshape(number * g.side, LANES)
                e = g.at(e1, e2, e3)
                out_ref[e, h, rows] += factor * part
                if e3 < g.ez - 1:
                    part = received((g.nz + e3, columns, lanes(h)))
                    out_ref[e, h, g.rows(a, g.deg, 1)] += factor * part
                if e3 > 0:
                    part = received((g.nz + e3 - 1, columns, lanes(h)))
                    out_ref[e, h, g.rows(a, 0, 1)] += factor * part


def add_y_face(g, out_ref, high, received, factor):
    e2, b = (g.ey - 1, g.deg) if high else (0, 0)
    for h in range(out_ref.shape[1]):
        for e1 in range(g.ex):
            parts = [
                received((e1 * g.ez + e3, slice(None), lanes(h))) for e3 in range(g.ez)
            ]
            count = parts[0].shape[0]
            layer = lax.broadcasted_iota(jnp.int32, parts[0].shape, 0) % g.side
            for e3 in range(g.ez):
                part = parts[e3]
                if e3 < g.ez - 1:
                    above = pltpu.roll(parts[e3 + 1], g.deg, 0)
                    part = part + jnp.where(layer == g.deg, above, 0.0)
                if e3 > 0:
                    below = pltpu.roll(parts[e3 - 1], count - g.deg, 0)
                    part = part + jnp.where(layer == 0, below, 0.0)
                out_ref[g.at(e1, e2, e3), h, g.side_rows(b)] += factor * part


def add_line(g, out_ref, high_x, high_y, received, factor):
    e1, a = (g.ex - 1, g.deg) if high_x else (0, 0)
    e2, b = (g.ey - 1, g.deg) if high_y else (0, 0)
    for h in range(out_ref.shape[1]):
        for e3 in range(g.ez):
            part = received((slice(e3 * g.side, (e3 + 1) * g.side), lanes(h)))
            out_ref[g.at(e1, e2, e3), h, g.line_rows(a, b)] += factor * part


def send_all(g, w_ref, sends):
    even_x = lax.axis_index("dx") % 2 == 0
    even_y = lax.axis_index("dy") % 2 == 0

    def by_pair(even, one_ref, two_ref):
        def put(where, low, high):
            one_ref[where] = jnp.where(even, high, low).astype(one_ref.dtype)
            two_ref[where] = jnp.where(even, low, high).astype(two_ref.dtype)

        return put

    put_x_face(g, w_ref, by_pair(even_x, sends[0], sends[1]))
    put_y_face(g, w_ref, by_pair(even_y, sends[2], sends[3]))


def corner_kernel(from_a, from_b, to_a, to_b, *, g):
    even = lax.axis_index("dy") % 2 == 0
    last = from_a.shape[1] - 1
    bands = from_a.shape[2]
    for k, source in enumerate((from_a, from_b)):
        for e3 in range(g.ez):
            low, number, start = g.layers(e3)
            for c in range(g.side):
                row = slice(e3 * g.side + c, e3 * g.side + c + 1)
                if low <= c < low + number:
                    z = start + c - low
                    both = source[z].astype(jnp.float32)
                    if (z + 1) % g.deg == 0:
                        layer = g.nz + (z + 1) // g.deg - 1
                        both = both + source[layer].astype(jnp.float32)
                    bottom, top = both[0:1], both[last : last + 1]
                    to_a[k, row] = jnp.where(even, top, bottom)
                    to_b[k, row] = jnp.where(even, bottom, top)
                else:
                    to_a[k, row] = jnp.zeros((1, bands), jnp.float32)
                    to_b[k, row] = jnp.zeros((1, bands), jnp.float32)


def add_all(g, out_ref, received, factor):
    p, q = lax.axis_index("dx"), lax.axis_index("dy")
    even_x, even_y = p % 2 == 0, q % 2 == 0
    has_x = (p > 0, p < lax.axis_size("dx") - 1)
    has_y = (q > 0, q < lax.axis_size("dy") - 1)

    def from_pair(even, high, one, two, exists):
        one, two = one.astype(jnp.float32), two.astype(jnp.float32)
        value = jnp.where(even, one, two) if high else jnp.where(even, two, one)
        return jnp.where(exists, value, 0.0)

    for high in (0, 1):

        def across_x(where):
            return from_pair(even_x, high, received[0][where], received[1][where], has_x[high])

        def across_y(where):
            return from_pair(even_y, high, received[2][where], received[3][where], has_y[high])

        add_x_face(g, out_ref, high, across_x, factor)
        add_y_face(g, out_ref, high, across_y, factor)
    for hx in (0, 1):
        for hy in (0, 1):

            def diagonal(where):
                one, two = [
                    from_pair(even_y, hy, received[4][k, *where], received[5][k, *where], has_y[hy])
                    for k in (0, 1)
                ]
                return from_pair(even_x, hx, one, two, has_x[hx])

            add_line(g, out_ref, hx, hy, diagonal, factor)


def field_of(y_ref, e):
    parts = [y_ref[e, h].astype(jnp.bfloat16) for h in range(y_ref.shape[1])]
    return jnp.concatenate(parts, axis=-1)


def edge_kernel(orb_ref, mats_ref, conn_ref, x_ref, y_ref, line_ref, tiles_ref):
    del mats_ref, conn_ref
    nx, nz, ny, bands = orb_ref.shape
    last = (ny - 1) % ROWS
    tail = slice(ny - 1 - last, ny)
    x_ref[...] = orb_ref[nx - 1]
    for h in range(bands // LANES):
        for i in range(nx):
            part = orb_ref[i, :, tail, lanes(h)].astype(jnp.float32)
            for k in range(nz):
                start = (i * nz + k) * ROWS
                tiles_ref[h, start : start + last + 1] = part[k]
        rows = tiles_ref[h, pl.ds(last, y_ref.shape[0], stride=ROWS)]
        y_ref[:, lanes(h)] = rows.astype(jnp.bfloat16)
        line = tiles_ref[h, pl.ds((nx - 1) * nz * ROWS + last, line_ref.shape[0], stride=ROWS)]
        line_ref[:, lanes(h)] = line.astype(jnp.bfloat16)


def first_kernel(*refs, g):
    orb_ref, below_x, below_y, below_xy, mats_ref, y_ref, next_ref, *sends = refs
    side = g.side
    halves = range(y_ref.shape[1])
    sub = lax.broadcasted_iota(jnp.int32, (side, LANES), 0)
    nothing = jnp.zeros((side, LANES), jnp.float32)
    rest = orb_ref.shape[2] - side
    for e1 in range(g.ex):
        for e2 in range(g.ey):
            for a in range(side):
                for h in halves:
                    y_ref[g.at(e1, e2, 0), h, g.rows(a, 0, 1)] = nothing
                    y_ref[g.at(e1, e2, g.ez - 1), h, g.rows(a, g.deg, 1)] = nothing

    def place(i, k, column, edge):
        for h in halves:
            part = column[:, lanes(h)].astype(jnp.float32)
            t0 = part[:side]
            t1 = jnp.concatenate([part[side:], nothing[: side - rest]], axis=0)
            first = jnp.broadcast_to(edge[:, lanes(h)].astype(jnp.float32), (side, LANES))
            d0 = jnp.where(sub == 0, first, pltpu.roll(t0, 1, 0))
            d1 = jnp.where(sub < 2, pltpu.roll(t0, 2, 0), pltpu.roll(t1, 2, 0))
            for e1 in range(g.ex):
                a = i - e1 * g.deg
                for e3 in range(g.ez):
                    c = k + 1 - e3 * g.deg
                    if 0 <= a <= g.deg and 0 <= c <= g.deg:
                        y_ref[g.at(e1, 0, e3), h, g.rows(a, c, 1)] = d0
                        y_ref[g.at(e1, 1, e3), h, g.rows(a, c, 1)] = d1

    for k in range(g.nz):
        place(0, k, below_x[k], below_xy[k : k + 1])
        for i in range(orb_ref.shape[0]):
            place(i + 1, k, orb_ref[i, k], below_y[i * g.nz + k : i * g.nz + k + 1])
    multiply(g, mats_ref, functools.partial(field_of, y_ref), next_ref)
    send_all(g, next_ref, sends)
    advance(next_ref, y_ref, None, FIRST)


def advance(next_ref, now_ref, older_ref, gain):
    for e in range(next_ref.shape[0]):
        for h in range(next_ref.shape[1]):
            value = gain * (next_ref[e, h] - filter_center * now_ref[e, h])
            next_ref[e, h] = value if older_ref is None else value - older_ref[e, h]


def middle_kernel(*refs, g):
    part_ref, *refs = refs
    received, refs = refs[:6], refs[6:]
    older_ref, mats_ref, y_ref, next_ref, *sends = refs
    y_ref[...] = part_ref[...]
    add_all(g, y_ref, received, FIRST)
    multiply(g, mats_ref, functools.partial(field_of, y_ref), next_ref)
    send_all(g, next_ref, sends)
    advance(next_ref, y_ref, older_ref, LATER)


def late_kernel(*refs, g):
    part_ref, *refs = refs
    received, refs = refs[:6], refs[6:]
    older_ref, mats_ref, next_ref, *sends, y_ref = refs
    y_ref[...] = part_ref[...]
    add_all(g, y_ref, received, LATER)
    multiply(g, mats_ref, functools.partial(field_of, y_ref), next_ref)

    def put_low(ref):
        def put(where, low, high):
            ref[where] = low.astype(ref.dtype)

        return put

    put_x_face(g, next_ref, put_low(sends[0]))
    put_y_face(g, next_ref, put_low(sends[1]))
    for h in range(next_ref.shape[1]):
        for e3 in range(g.ez):
            rows = slice(e3 * g.side, (e3 + 1) * g.side)
            sends[2][rows, lanes(h)] = line(g, next_ref, 0, 0, e3, h)
    advance(next_ref, y_ref, older_ref, LATER)


def split(value):
    high = value.astype(jnp.bfloat16)
    return high, (value - high.astype(jnp.float32)).astype(jnp.bfloat16)


def packed_rows(bands):
    count = bands // LANES
    return count * bands if count != 2 else bands + 2 * ROWS


def pack(gram, put):
    count = gram.shape[0] // LANES
    block = lambda i, j: gram[lanes(i), lanes(j)]
    if count != 2:
        for i in range(count):
            for j in range(count):
                put((i * count + j) * LANES, block(i, j))
        return
    row = lax.broadcasted_iota(jnp.int32, (LANES, LANES), 0)
    lane = lax.broadcasted_iota(jnp.int32, (LANES, LANES), 1)
    put(0, jnp.where(row >= lane, block(0, 0), block(1, 1)))
    put(LANES, block(1, 0))
    diagonal = jnp.sum(jnp.where(row == lane, block(1, 1), 0.0), axis=0, keepdims=True)
    put(2 * LANES, jnp.broadcast_to(diagonal, (2 * ROWS, LANES)))


def unpack(packed, count):
    block = lambda k: packed[k * LANES : (k + 1) * LANES]
    if count != 2:
        return lambda i, j: block(i * count + j)
    row = lax.broadcasted_iota(jnp.int32, (LANES, LANES), 0)
    lane = lax.broadcasted_iota(jnp.int32, (LANES, LANES), 1)
    both = block(0)
    first = jnp.where(row > lane, both, 0.0)
    second = jnp.where(row < lane, both, 0.0)
    diagonal = jnp.broadcast_to(packed[2 * LANES : 2 * LANES + 1], (LANES, LANES))
    blocks = {
        (0, 0): first + first.T + jnp.where(row == lane, both, 0.0),
        (1, 0): block(1),
        (1, 1): second + second.T + jnp.where(row == lane, diagonal, 0.0),
    }
    return lambda i, j: blocks[i, j]


def last_kernel(part_ref, from_x, from_y, from_xy, *refs, g):
    high_ref, low_ref, kept_ref, sent_ref, y_ref, out_ref, packed_ref = refs
    side = g.side
    y_ref[...] = part_ref[...]
    p, q = lax.axis_index("dx"), lax.axis_index("dy")
    has_x, has_y = p < lax.axis_size("dx") - 1, q < lax.axis_size("dy") - 1
    add_x_face(g, y_ref, True, lambda w: jnp.where(has_x, from_x[w].astype(jnp.float32), 0.0), LATER)
    add_y_face(g, y_ref, True, lambda w: jnp.where(has_y, from_y[w].astype(jnp.float32), 0.0), LATER)
    add_line(g, y_ref, 1, 1, lambda w: jnp.where(has_x & has_y, from_xy[w], 0.0), LATER)
    sub = lax.broadcasted_iota(jnp.int32, (side, LANES), 0)
    rest = 2 * g.deg - side
    for i in range(g.ex * g.deg):
        e1 = i // g.deg
        a = i + 1 - e1 * g.deg
        for k in range(g.nz):
            e3 = k // g.deg
            rows = g.rows(a, k + 1 - e3 * g.deg, 1)
            for h in range(y_ref.shape[1]):
                d0 = pltpu.roll(y_ref[g.at(e1, 0, e3), h, rows], side - 1, 0)
                d1 = pltpu.roll(y_ref[g.at(e1, 1, e3), h, rows], side - 2, 0)
                start = (i * g.nz + k) * 2 * side
                out_ref[start : start + side, lanes(h)] = jnp.where(sub < g.deg, d0, d1)
                bottom = slice(start + side, start + 2 * side)
                out_ref[bottom, lanes(h)] = jnp.where(sub < rest, d1, 0.0)
    high, low = split(out_ref[...])
    high_ref[...] = high
    low_ref[...] = low
    inner = functools.partial(
        lax.dot_general,
        dimension_numbers=(((0,), (0,)), ((), ())),
        preferred_element_type=jnp.float32,
    )
    mixed = inner(high, low)
    gram = inner(high, high) + (mixed + mixed.T) + inner(low, low)

    def put(start, rows):
        packed_ref[start : start + rows.shape[0]] = rows

    pack(gram, put)
    half = kept_ref.shape[0]
    odd = lax.axis_index("dy") % 2 == 1
    first, second = packed_ref[:half], packed_ref[half:]
    kept_ref[...] = jnp.where(odd, second, first)
    sent_ref[...] = jnp.where(odd, first, second)


def invert_block(block):
    size = block.shape[0]
    groups = size // ROWS
    sub = lax.broadcasted_iota(jnp.int32, (ROWS, size), 0)
    lane = lax.broadcasted_iota(jnp.int32, (ROWS, size), 1)
    left = [block[ROWS * j : ROWS * (j + 1)] for j in range(groups)]
    right = [jnp.where(lane == sub + ROWS * j, 1.0, 0.0) for j in range(groups)]
    spread = lambda row: jnp.broadcast_to(row, (ROWS, size))
    result = []
    for k in range(groups):
        tile = left[k]
        cols = [spread(tile[:, ROWS * k + c : ROWS * k + c + 1]) for c in range(ROWS)]
        s = [[spread(cols[c][r : r + 1]) if c <= r else None for c in range(ROWS)] for r in range(ROWS)]
        take = [[None] * ROWS for _ in range(ROWS)]
        pairs = {}
        for j in range(0, ROWS, 2):
            p, q, t = s[j][j], s[j + 1][j], s[j + 1][j + 1]
            over = 1.0 / (p * t - q * q)
            across = q * (1.0 / p)
            pairs[j] = (
                (t * over, q * over, p * over),
                across,
                lax.rsqrt(p),
                lax.rsqrt(t - across * q),
            )
            one, both, two = pairs[j][0]
            for r in range(j + 2, ROWS):
                take[r][j] = s[r][j] * one - s[r][j + 1] * both
                take[r][j + 1] = s[r][j + 1] * two - s[r][j] * both
                for c in range(j + 2, r + 1):
                    s[r][c] = s[r][c] - (take[r][j] * s[c][j] + take[r][j + 1] * s[c][j + 1])
        last = k == groups - 1
        solved = []
        for source, wanted in ((right[k], True), (tile, False)):
            if last and not wanted:
                continue
            rows = [spread(source[r : r + 1]) for r in range(ROWS)]
            for j in range(0, ROWS, 2):
                for r in range(j + 2, ROWS):
                    rows[r] = rows[r] - (take[r][j] * rows[j] + take[r][j + 1] * rows[j + 1])
            if wanted:
                done = jnp.zeros((ROWS, size), jnp.float32)
                for j in range(0, ROWS, 2):
                    _, across, scale, scale_next = pairs[j]
                    done = jnp.where(sub == j, rows[j] * scale, done)
                    below = (rows[j + 1] - across * rows[j]) * scale_next
                    done = jnp.where(sub == j + 1, below, done)
                result.append(done)
            if last:
                continue
            for j in range(0, ROWS, 2):
                one, both, two = pairs[j][0]
                rows[j], rows[j + 1] = (
                    one * rows[j] - both * rows[j + 1],
                    two * rows[j + 1] - both * rows[j],
                )
            for j in reversed(range(0, ROWS, 2)):
                for r in range(j):
                    rows[r] = rows[r] - (take[j][r] * rows[j] + take[j + 1][r] * rows[j + 1])
            solved.append(rows)

        def tree(terms):
            while len(terms) > 1:
                terms = [a + b for a, b in zip(terms[::2], terms[1::2])]
            return terms[0]

        for j in range(k + 1, groups):
            cols = [spread(left[j][:, ROWS * k + c : ROWS * k + c + 1]) for c in range(ROWS)]
            left[j] = left[j] - tree([cols[c] * solved[1][c] for c in range(ROWS)])
            right[j] = right[j] - tree([cols[c] * solved[0][c] for c in range(ROWS)])
    return jnp.concatenate(result, axis=0)


def dot(one, two, axis_one=1, axis_two=0):
    return lax.dot_general(
        one,
        two,
        (((axis_one,), (axis_two,)), ((), ())),
        precision=lax.Precision.HIGHEST,
        preferred_element_type=jnp.float32,
    )


def inverse_factor(block_of, count):
    low, inv = {}, {}
    for i in range(count):
        diag = block_of(i, i)
        for j in range(i):
            part = block_of(i, j)
            for k in range(j):
                part = part - dot(low[i, k], low[j, k], 1, 1)
            low[i, j] = dot(part, inv[j, j], 1, 1)
            diag = diag - dot(low[i, j], low[i, j], 1, 1)
        sums = []
        for j in range(i):
            part = dot(low[i, j], inv[j, j])
            for k in range(j + 1, i):
                part = part + dot(low[i, k], inv[k, j])
            sums.append(part)
        inv[i, i] = invert_block(diag)
        for j in range(i):
            inv[i, j] = -dot(inv[i, i], sums[j])
    return inv

def basis_kernel(mine_ref, other_ref, high_ref, low_ref, out_ref, factor_ref, *, scale):
    @pl.when(pl.program_id(0) == 0)
    def _():
        count = high_ref.shape[1] // LANES
        odd = lax.axis_index("dy") % 2 == 1
        mine, other = mine_ref[...], other_ref[...]
        packed = jnp.concatenate(
            [jnp.where(odd, other, mine), jnp.where(odd, mine, other)], axis=0
        )
        inverse = inverse_factor(unpack(packed, count), count)
        for i in range(count):
            for j in range(count):
                block = inverse[i, j] * scale if j <= i else jnp.zeros((LANES, LANES), jnp.float32)
                high, low = split(block)
                factor_ref[0, lanes(i), lanes(j)] = high
                factor_ref[1, lanes(i), lanes(j)] = low

    slab, nz, ny, bands = out_ref.shape
    rows = high_ref.shape[0] // pl.num_programs(0)
    here = pl.ds(pl.multiple_of(pl.program_id(0) * rows, rows), rows)
    times = functools.partial(
        lax.dot_general,
        dimension_numbers=(((1,), (1,)), ((), ())),
        preferred_element_type=jnp.float32,
    )
    high, low = high_ref[here], low_ref[here]
    result = times(high, factor_ref[0]) + (times(high, factor_ref[1]) + times(low, factor_ref[0]))
    result = result.reshape(slab, nz, rows // (slab * nz), bands)
    out_ref[...] = result[:, :, :ny]


def call(kernel, outs, scratch, operands, flops):
    size = sum(x.size * x.dtype.itemsize for x in (*operands, *outs))
    return pl.pallas_call(
        kernel,
        out_shape=outs,
        in_specs=[VMEM] * len(operands),
        out_specs=[VMEM] * len(outs),
        scratch_shapes=scratch,
        compiler_params=pltpu.CompilerParams(vmem_limit_bytes=LIMIT),
        cost_estimate=pl.CostEstimate(flops=flops, bytes_accessed=size, transcendentals=0),
    )(*operands)


def shards(orbitals, elem_mats, conn):
    nx, ny, nz, bands = orbitals.shape
    side = round(elem_mats.shape[-1] ** (1 / 3))
    g = Grid(elem_mats, side)
    elem_mats = elem_mats.reshape(g.elements, g.count, g.count)
    f32 = jnp.float32
    orb = jnp.transpose(orbitals, (0, 2, 1, 3))
    shape = jax.ShapeDtypeStruct
    plane = -(-nx * nz // (2 * ROWS)) * 2 * ROWS
    tall = (plane + 2 * ROWS) * ROWS
    edges = call(
        edge_kernel,
        [
            shape((nz, ny, bands), orb.dtype),
            shape((plane, bands), orb.dtype),
            shape((2 * ROWS, bands), orb.dtype),
        ],
        [pltpu.VMEM((bands // LANES, tall, LANES), f32)],
        (orb, elem_mats, conn),
        0,
    )
    below_x, below_y, below_xy = [
        ring(s, *step) for s, step in zip(edges, ((1, 0), (0, 1), (1, 1)))
    ]
    mats = renumber(g, conn, elem_mats, ny + 1, nz + 2)

    nodes = (g.elements, bands // LANES, g.count, LANES)
    x_shape = shape((nz + g.ez - 1, g.ey * side, bands), jnp.bfloat16)
    y_shape = shape((g.ex * g.ez, side * side, bands), jnp.bfloat16)
    line_shape = shape((g.ez * side, bands), f32)
    corner_shape = shape((2, *line_shape.shape), f32)
    send_shapes = [x_shape] * 2 + [y_shape] * 2
    pairings = [("A", "-"), ("B", "-"), ("-", "A"), ("-", "B")]
    flops = 2 * g.elements * g.count**2 * bands

    def swap(sends):
        faces = [pair_swap(s, *pair) for s, pair in zip(sends, pairings)]
        kernel = functools.partial(corner_kernel, g=g)
        lines = call(kernel, [corner_shape] * 2, [], tuple(faces[:2]), 0)
        return *faces, *[pair_swap(s, *pair) for s, pair in zip(lines, pairings[2:])]

    y0, part, *sends = call(
        functools.partial(first_kernel, g=g),
        [shape(nodes, f32), shape(nodes, f32), *send_shapes],
        [],
        (orb, below_x, below_y, below_xy, mats),
        flops,
    )
    received = swap(sends)
    y1, part, *sends = call(
        functools.partial(middle_kernel, g=g),
        [shape(nodes, f32), shape(nodes, f32), *send_shapes],
        [],
        (part, *received, y0, mats),
        flops,
    )
    received = swap(sends)
    part, *sends = call(
        functools.partial(late_kernel, g=g),
        [shape(nodes, f32), x_shape, y_shape, line_shape],
        [pltpu.VMEM(nodes, f32)],
        (part, *received, y1, mats),
        flops,
    )
    received = [ring(s, *step) for s, step in zip(sends, ((-1, 0), (0, -1), (-1, -1)))]
    rows = nx * nz * 2 * side
    packed = packed_rows(bands)
    half_shape = shape((packed // 2, LANES), f32)
    high, low, kept, sent = call(
        functools.partial(last_kernel, g=g),
        [shape((rows, bands), jnp.bfloat16)] * 2 + [half_shape] * 2,
        [pltpu.VMEM(nodes, f32), pltpu.VMEM((rows, bands), f32), pltpu.VMEM((packed, LANES), f32)],
        (part, *received),
        8 * rows * bands**2,
    )
    mine, other = halved_total(kept, sent)
    slabs = g.ex * g.deg // 2
    spot = pl.BlockSpec((nx // slabs, nz, ny, bands), lambda i: (i, 0, 0, 0))
    basis = pl.pallas_call(
        functools.partial(basis_kernel, scale=math.sqrt(nx * ny * nz * lax.axis_size(AXES))),
        out_shape=shape((nx, nz, ny, bands), f32),
        grid=(slabs,),
        in_specs=[VMEM] * 4,
        out_specs=spot,
        scratch_shapes=[pltpu.VMEM((2, bands, bands), jnp.bfloat16)],
        compiler_params=pltpu.CompilerParams(vmem_limit_bytes=LIMIT),
        name="basis",
    )(mine, other, high, low)
    return jnp.transpose(basis, (0, 2, 1, 3))


def solution(mesh):
    in_specs = (
        P("dx", "dy", None, None),
        P("dx", "dy", None, None, None),
        P("dx", "dy", None, None),
    )
    out_specs = P("dx", "dy", None, None)
    return jax.shard_map(shards, mesh=mesh, in_specs=in_specs, out_specs=out_specs, check_vma=False)
```

```python
import functools
import math

import jax
import jax.numpy as jnp
from jax import lax
from jax.experimental import pallas as pl
from jax.experimental.pallas import tpu as pltpu
from jax.sharding import PartitionSpec as P

filter_center = 1.5
filter_half = 4.0
FIRST = 1.0 / filter_half
LATER = 2.0 / filter_half
AXES = ("dx", "dy")
VMEM = pl.BlockSpec(memory_space=pltpu.VMEM)
LIMIT = 16 * 1024 * 1024
LANES = 128
ROWS = 8


def partner(index, size, pairing, closed):
    if pairing == "-":
        return index
    other = index ^ 1 if pairing == "A" else index - 1 if index % 2 == 0 else index + 1
    if 0 <= other < size:
        return other
    return size - 1 - index if closed and pairing == "B" and size % 2 == 0 else index


def pair_swap(value, along_x, along_y):
    size_x, size_y = lax.axis_size("dx"), lax.axis_size("dy")
    route = [
        (
            p * size_y + q,
            partner(p, size_x, along_x, False) * size_y + partner(q, size_y, along_y, True),
        )
        for p in range(size_x)
        for q in range(size_y)
    ]
    return lax.ppermute(value, AXES, route)


def ring(value, step_x, step_y):
    size_x, size_y = lax.axis_size("dx"), lax.axis_size("dy")
    route = [
        (p * size_y + q, (p + step_x) % size_x * size_y + (q + step_y) % size_y)
        for p in range(size_x)
        for q in range(size_y)
    ]
    return lax.ppermute(value, AXES, route)


def xor_swap(value, axis, bits):
    return lax.ppermute(value, axis, [(i, i ^ bits) for i in range(lax.axis_size(axis))])


def sum_swap(value, stage, bits):
    size_x, size_y = lax.axis_size("dx"), lax.axis_size("dy")
    route = []
    for p in range(size_x):
        for q in range(size_y):
            along_x = (q + stage) % 2 == 0
            to = (p ^ bits, q) if along_x else (p, q ^ 2 * bits)
            route.append((p * size_y + q, to[0] * size_y + to[1]))
    return lax.ppermute(value, AXES, route)


def halved_total(kept, sent):
    part = kept + xor_swap(sent, "dy", 1)
    sizes = lax.axis_size("dx"), lax.axis_size("dy") // 2
    if sizes[0] == sizes[1]:
        steps = [functools.partial(sum_swap, stage=stage) for stage in (0, 1)]
    else:
        steps = [
            lambda value, bits: xor_swap(value, "dx", bits),
            lambda value, bits: xor_swap(value, "dy", 2 * bits),
        ]
    for step, size in zip(steps, sizes):
        bit = 1
        while bit < size:
            if 2 * bit < size:
                one, two, three = [step(part, bits=bit * k) for k in (1, 2, 3)]
                part = (part + one) + (two + three)
                bit *= 4
            else:
                part = part + step(part, bits=bit)
                bit *= 2
    return part, xor_swap(part, "dy", 1)


def renumber_kernel(conn_ref, mats_ref, out_ref, *, g, width, depth):
    side, deg, layers = g.side, g.deg, g.ez
    spots = [
        (e1, e2, e3) for e1 in range(g.ex) for e2 in range(g.ey) for e3 in range(g.ez)
    ]
    for e, (e1, e2, e3) in enumerate(spots):
        node = conn_ref[e1, e2, e3 : e3 + 1].astype(jnp.float32)
        plane = jnp.floor((node + 0.5) * (1.0 / depth))
        first = jnp.floor((plane + 0.5) * (1.0 / width))
        c = (node - plane * depth).astype(jnp.int32) - deg * e3
        b = (plane - first * width).astype(jnp.int32) - deg * e2
        a = first.astype(jnp.int32) - deg * e1
        place = (a * side + c) * side + b
        if e1 == 0:
            place = jnp.where((a == 0) & (lax.axis_index("dx") == 0), -1, place)
        if e2 == 0:
            place = jnp.where((b == 0) & (lax.axis_index("dy") == 0), -1, place)
        if e3 == 0:
            place = jnp.where(c == 0, -1, place)
        if e3 == layers - 1:
            place = jnp.where(c == deg, -1, place)
        order = lax.broadcasted_iota(jnp.int32, (g.count, g.count), 0) == place
        order = jnp.where(order, 1.0, 0.0).astype(jnp.bfloat16)
        half = jnp.dot(order, mats_ref[e], preferred_element_type=jnp.float32)
        whole = lax.dot_general(
            half.astype(jnp.bfloat16),
            order,
            (((1,), (1,)), ((), ())),
            preferred_element_type=jnp.float32,
        )
        out_ref[e] = whole.astype(jnp.bfloat16)


def renumber(g, conn, elem_mats, width, depth):
    shape = (g.elements, g.count, g.count)
    return pl.pallas_call(
        functools.partial(renumber_kernel, g=g, width=width, depth=depth),
        out_shape=jax.ShapeDtypeStruct(shape, jnp.bfloat16),
        in_specs=[VMEM] * 2,
        out_specs=VMEM,
        compiler_params=pltpu.CompilerParams(vmem_limit_bytes=LIMIT),
        cost_estimate=pl.CostEstimate(
            flops=4 * g.elements * g.count**3,
            bytes_accessed=4 * elem_mats.size,
            transcendentals=0,
        ),
        name="renumber",
    )(conn, elem_mats)


class Grid:
    def __init__(self, elem_mats, side):
        self.ex, self.ey, self.ez = elem_mats.shape[:3]
        self.count = elem_mats.shape[3]
        self.side = side
        self.deg = side - 1
        self.nz = self.ez * self.deg - 1
        self.elements = self.ex * self.ey * self.ez

    def at(self, e1, e2, e3):
        return (e1 * self.ey + e2) * self.ez + e3

    def rows(self, a, c, number):
        start = (a * self.side + c) * self.side
        return slice(start, start + number * self.side)

    def layers(self, e3):
        low = 1 if e3 == 0 else 0
        high = self.deg - 1 if e3 == self.ez - 1 else self.deg
        return low, high - low + 1, e3 * self.deg + low - 1

    def side_rows(self, b):
        return pl.ds(b, self.side * self.side, stride=self.side)

    def line_rows(self, a, b):
        return pl.ds(a * self.side * self.side + b, self.side, stride=self.side)


def lanes(h):
    return slice(h * LANES, (h + 1) * LANES)


def multiply(g, mats_ref, field_of, w_ref):
    side, deg = g.side, g.deg
    halves = range(w_ref.shape[1])
    for e in range(g.elements):
        product = jnp.dot(mats_ref[e], field_of(e), preferred_element_type=jnp.float32)
        for h in halves:
            w_ref[e, h] = product[:, lanes(h)]

    def join(one, top, two, bottom):
        for h in halves:
            both = w_ref[one, h, top] + w_ref[two, h, bottom]
            w_ref[one, h, top] = both
            w_ref[two, h, bottom] = both

    for e1 in range(g.ex):
        for e2 in range(g.ey):
            for e3 in range(g.ez - 1):
                for a in range(side):
                    one, two = g.at(e1, e2, e3), g.at(e1, e2, e3 + 1)
                    join(one, g.rows(a, deg, 1), two, g.rows(a, 0, 1))
    for e1 in range(g.ex - 1):
        for e2 in range(g.ey):
            for e3 in range(g.ez):
                one, two = g.at(e1, e2, e3), g.at(e1 + 1, e2, e3)
                join(one, g.rows(deg, 0, side), two, g.rows(0, 0, side))
    for e1 in range(g.ex):
        for e2 in range(g.ey - 1):
            for e3 in range(g.ez):
                one, two = g.at(e1, e2, e3), g.at(e1, e2 + 1, e3)
                join(one, g.side_rows(deg), two, g.side_rows(0))


def rest_of(value):
    return value - value.astype(jnp.bfloat16).astype(jnp.float32)


def put_x_face(g, w_ref, put):
    for h in range(w_ref.shape[1]):
        for e2 in range(g.ey):
            for e3 in range(g.ez):
                low, number, start = g.layers(e3)
                if e3 > 0:
                    low, number, start = low + 1, number - 1, start + 1
                one = w_ref[g.at(0, e2, e3), h, g.rows(0, low, number)]
                two = w_ref[g.at(g.ex - 1, e2, e3), h, g.rows(g.deg, low, number)]
                where = (
                    slice(start, start + number),
                    slice(e2 * g.side, (e2 + 1) * g.side),
                    lanes(h),
                )
                shape = (number, g.side, LANES)
                put(where, one.reshape(shape), two.reshape(shape))
                if e3 < g.ez - 1:
                    one, two = one[-g.side :], two[-g.side :]
                    put((g.nz + e3, *where[1:]), rest_of(one), rest_of(two))


def put_y_face(g, w_ref, put):
    for h in range(w_ref.shape[1]):
        for e1 in range(g.ex):
            for e3 in range(g.ez):
                one = w_ref[g.at(e1, 0, e3), h, g.side_rows(0)]
                two = w_ref[g.at(e1, g.ey - 1, e3), h, g.side_rows(g.deg)]
                if e3 > 0:
                    layer = lax.broadcasted_iota(jnp.int32, one.shape, 0) % g.side
                    one = jnp.where(layer == 0, rest_of(one), one)
                    two = jnp.where(layer == 0, rest_of(two), two)
                put((e1 * g.ez + e3, slice(None), lanes(h)), one, two)


def line(g, w_ref, high_x, high_y, e3, h):
    e1, a = (g.ex - 1, g.deg) if high_x else (0, 0)
    e2, b = (g.ey - 1, g.deg) if high_y else (0, 0)
    return w_ref[g.at(e1, e2, e3), h, g.line_rows(a, b)]


def add_x_face(g, out_ref, high, received, factor):
    e1, a = (g.ex - 1, g.deg) if high else (0, 0)
    for h in range(out_ref.shape[1]):
        for e2 in range(g.ey):
            for e3 in range(g.ez):
                low, number, start = g.layers(e3)
                columns = slice(e2 * g.side, (e2 + 1) * g.side)
                part = received((slice(start, start + number), columns, lanes(h)))
                rows = g.rows(a, low, number)
                part = part.reshape(number * g.side, LANES)
                e = g.at(e1, e2, e3)
                out_ref[e, h, rows] += factor * part
                if e3 < g.ez - 1:
                    part = received((g.nz + e3, columns, lanes(h)))
                    out_ref[e, h, g.rows(a, g.deg, 1)] += factor * part
                if e3 > 0:
                    part = received((g.nz + e3 - 1, columns, lanes(h)))
                    out_ref[e, h, g.rows(a, 0, 1)] += factor * part


def add_y_face(g, out_ref, high, received, factor):
    e2, b = (g.ey - 1, g.deg) if high else (0, 0)
    for h in range(out_ref.shape[1]):
        for e1 in range(g.ex):
            parts = [
                received((e1 * g.ez + e3, slice(None), lanes(h))) for e3 in range(g.ez)
            ]
            count = parts[0].shape[0]
            layer = lax.broadcasted_iota(jnp.int32, parts[0].shape, 0) % g.side
            for e3 in range(g.ez):
                part = parts[e3]
                if e3 < g.ez - 1:
                    above = pltpu.roll(parts[e3 + 1], g.deg, 0)
                    part = part + jnp.where(layer == g.deg, above, 0.0)
                if e3 > 0:
                    below = pltpu.roll(parts[e3 - 1], count - g.deg, 0)
                    part = part + jnp.where(layer == 0, below, 0.0)
                out_ref[g.at(e1, e2, e3), h, g.side_rows(b)] += factor * part


def add_line(g, out_ref, high_x, high_y, received, factor):
    e1, a = (g.ex - 1, g.deg) if high_x else (0, 0)
    e2, b = (g.ey - 1, g.deg) if high_y else (0, 0)
    for h in range(out_ref.shape[1]):
        for e3 in range(g.ez):
            part = received((slice(e3 * g.side, (e3 + 1) * g.side), lanes(h)))
            out_ref[g.at(e1, e2, e3), h, g.line_rows(a, b)] += factor * part


def send_all(g, w_ref, sends):
    even_x = lax.axis_index("dx") % 2 == 0
    even_y = lax.axis_index("dy") % 2 == 0

    def by_pair(even, one_ref, two_ref):
        def put(where, low, high):
            one_ref[where] = jnp.where(even, high, low).astype(one_ref.dtype)
            two_ref[where] = jnp.where(even, low, high).astype(two_ref.dtype)

        return put

    put_x_face(g, w_ref, by_pair(even_x, sends[0], sends[1]))
    put_y_face(g, w_ref, by_pair(even_y, sends[2], sends[3]))


def corner_kernel(from_a, from_b, to_a, to_b, *, g):
    even = lax.axis_index("dy") % 2 == 0
    last = from_a.shape[1] - 1
    bands = from_a.shape[2]
    for k, source in enumerate((from_a, from_b)):
        for e3 in range(g.ez):
            low, number, start = g.layers(e3)
            for c in range(g.side):
                row = slice(e3 * g.side + c, e3 * g.side + c + 1)
                if low <= c < low + number:
                    z = start + c - low
                    both = source[z].astype(jnp.float32)
                    if (z + 1) % g.deg == 0:
                        layer = g.nz + (z + 1) // g.deg - 1
                        both = both + source[layer].astype(jnp.float32)
                    bottom, top = both[0:1], both[last : last + 1]
                    to_a[k, row] = jnp.where(even, top, bottom)
                    to_b[k, row] = jnp.where(even, bottom, top)
                else:
                    to_a[k, row] = jnp.zeros((1, bands), jnp.float32)
                    to_b[k, row] = jnp.zeros((1, bands), jnp.float32)


def add_all(g, out_ref, received, factor):
    p, q = lax.axis_index("dx"), lax.axis_index("dy")
    even_x, even_y = p % 2 == 0, q % 2 == 0
    has_x = (p > 0, p < lax.axis_size("dx") - 1)
    has_y = (q > 0, q < lax.axis_size("dy") - 1)

    def from_pair(even, high, one, two, exists):
        one, two = one.astype(jnp.float32), two.astype(jnp.float32)
        value = jnp.where(even, one, two) if high else jnp.where(even, two, one)
        return jnp.where(exists, value, 0.0)

    for high in (0, 1):

        def across_x(where):
            return from_pair(even_x, high, received[0][where], received[1][where], has_x[high])

        def across_y(where):
            return from_pair(even_y, high, received[2][where], received[3][where], has_y[high])

        add_x_face(g, out_ref, high, across_x, factor)
        add_y_face(g, out_ref, high, across_y, factor)
    for hx in (0, 1):
        for hy in (0, 1):

            def diagonal(where):
                one, two = [
                    from_pair(even_y, hy, received[4][k, *where], received[5][k, *where], has_y[hy])
                    for k in (0, 1)
                ]
                return from_pair(even_x, hx, one, two, has_x[hx])

            add_line(g, out_ref, hx, hy, diagonal, factor)


def field_of(y_ref, e):
    parts = [y_ref[e, h].astype(jnp.bfloat16) for h in range(y_ref.shape[1])]
    return jnp.concatenate(parts, axis=-1)


def edge_kernel(orb_ref, x_ref, y_ref, line_ref, tiles_ref):
    nx, nz, ny, bands = orb_ref.shape
    last = (ny - 1) % ROWS
    tail = slice(ny - 1 - last, ny)
    x_ref[...] = orb_ref[nx - 1]
    for h in range(bands // LANES):
        for i in range(nx):
            part = orb_ref[i, :, tail, lanes(h)].astype(jnp.float32)
            for k in range(nz):
                start = (i * nz + k) * ROWS
                tiles_ref[h, start : start + last + 1] = part[k]
        rows = tiles_ref[h, pl.ds(last, y_ref.shape[0], stride=ROWS)]
        y_ref[:, lanes(h)] = rows.astype(jnp.bfloat16)
        line = tiles_ref[h, pl.ds((nx - 1) * nz * ROWS + last, line_ref.shape[0], stride=ROWS)]
        line_ref[:, lanes(h)] = line.astype(jnp.bfloat16)


def first_kernel(*refs, g):
    orb_ref, below_x, below_y, below_xy, mats_ref, y_ref, next_ref, *sends = refs
    side = g.side
    halves = range(y_ref.shape[1])
    sub = lax.broadcasted_iota(jnp.int32, (side, LANES), 0)
    nothing = jnp.zeros((side, LANES), jnp.float32)
    rest = orb_ref.shape[2] - side
    for e1 in range(g.ex):
        for e2 in range(g.ey):
            for a in range(side):
                for h in halves:
                    y_ref[g.at(e1, e2, 0), h, g.rows(a, 0, 1)] = nothing
                    y_ref[g.at(e1, e2, g.ez - 1), h, g.rows(a, g.deg, 1)] = nothing

    def place(i, k, column, edge):
        for h in halves:
            part = column[:, lanes(h)].astype(jnp.float32)
            t0 = part[:side]
            t1 = jnp.concatenate([part[side:], nothing[: side - rest]], axis=0)
            first = jnp.broadcast_to(edge[:, lanes(h)].astype(jnp.float32), (side, LANES))
            d0 = jnp.where(sub == 0, first, pltpu.roll(t0, 1, 0))
            d1 = jnp.where(sub < 2, pltpu.roll(t0, 2, 0), pltpu.roll(t1, 2, 0))
            for e1 in range(g.ex):
                a = i - e1 * g.deg
                for e3 in range(g.ez):
                    c = k + 1 - e3 * g.deg
                    if 0 <= a <= g.deg and 0 <= c <= g.deg:
                        y_ref[g.at(e1, 0, e3), h, g.rows(a, c, 1)] = d0
                        y_ref[g.at(e1, 1, e3), h, g.rows(a, c, 1)] = d1

    for k in range(g.nz):
        place(0, k, below_x[k], below_xy[k : k + 1])
        for i in range(orb_ref.shape[0]):
            place(i + 1, k, orb_ref[i, k], below_y[i * g.nz + k : i * g.nz + k + 1])
    multiply(g, mats_ref, functools.partial(field_of, y_ref), next_ref)
    send_all(g, next_ref, sends)
    advance(next_ref, y_ref, None, FIRST)


def advance(next_ref, now_ref, older_ref, gain):
    for e in range(next_ref.shape[0]):
        for h in range(next_ref.shape[1]):
            value = gain * (next_ref[e, h] - filter_center * now_ref[e, h])
            next_ref[e, h] = value if older_ref is None else value - older_ref[e, h]


def middle_kernel(*refs, g):
    part_ref, *refs = refs
    received, refs = refs[:6], refs[6:]
    older_ref, mats_ref, y_ref, next_ref, *sends = refs
    y_ref[...] = part_ref[...]
    add_all(g, y_ref, received, FIRST)
    multiply(g, mats_ref, functools.partial(field_of, y_ref), next_ref)
    send_all(g, next_ref, sends)
    advance(next_ref, y_ref, older_ref, LATER)


def late_kernel(*refs, g):
    part_ref, *refs = refs
    received, refs = refs[:6], refs[6:]
    older_ref, mats_ref, next_ref, *sends, y_ref = refs
    y_ref[...] = part_ref[...]
    add_all(g, y_ref, received, LATER)
    multiply(g, mats_ref, functools.partial(field_of, y_ref), next_ref)

    def put_low(ref):
        def put(where, low, high):
            ref[where] = low.astype(ref.dtype)

        return put

    put_x_face(g, next_ref, put_low(sends[0]))
    put_y_face(g, next_ref, put_low(sends[1]))
    for h in range(next_ref.shape[1]):
        for e3 in range(g.ez):
            rows = slice(e3 * g.side, (e3 + 1) * g.side)
            sends[2][rows, lanes(h)] = line(g, next_ref, 0, 0, e3, h)
    advance(next_ref, y_ref, older_ref, LATER)


def split(value):
    high = value.astype(jnp.bfloat16)
    return high, (value - high.astype(jnp.float32)).astype(jnp.bfloat16)


def packed_rows(bands):
    count = bands // LANES
    return count * bands if count != 2 else bands + 2 * ROWS


def pack(gram, put):
    count = gram.shape[0] // LANES
    block = lambda i, j: gram[lanes(i), lanes(j)]
    if count != 2:
        for i in range(count):
            for j in range(count):
                put((i * count + j) * LANES, block(i, j))
        return
    row = lax.broadcasted_iota(jnp.int32, (LANES, LANES), 0)
    lane = lax.broadcasted_iota(jnp.int32, (LANES, LANES), 1)
    put(0, jnp.where(row >= lane, block(0, 0), block(1, 1)))
    put(LANES, block(1, 0))
    diagonal = jnp.sum(jnp.where(row == lane, block(1, 1), 0.0), axis=0, keepdims=True)
    put(2 * LANES, jnp.broadcast_to(diagonal, (2 * ROWS, LANES)))


def unpack(packed, count):
    block = lambda k: packed[k * LANES : (k + 1) * LANES]
    if count != 2:
        return lambda i, j: block(i * count + j)
    row = lax.broadcasted_iota(jnp.int32, (LANES, LANES), 0)
    lane = lax.broadcasted_iota(jnp.int32, (LANES, LANES), 1)
    both = block(0)
    first = jnp.where(row > lane, both, 0.0)
    second = jnp.where(row < lane, both, 0.0)
    diagonal = jnp.broadcast_to(packed[2 * LANES : 2 * LANES + 1], (LANES, LANES))
    blocks = {
        (0, 0): first + first.T + jnp.where(row == lane, both, 0.0),
        (1, 0): block(1),
        (1, 1): second + second.T + jnp.where(row == lane, diagonal, 0.0),
    }
    return lambda i, j: blocks[i, j]


def last_kernel(part_ref, from_x, from_y, from_xy, *refs, g):
    high_ref, low_ref, kept_ref, sent_ref, y_ref, out_ref, packed_ref = refs
    side = g.side
    y_ref[...] = part_ref[...]
    p, q = lax.axis_index("dx"), lax.axis_index("dy")
    has_x, has_y = p < lax.axis_size("dx") - 1, q < lax.axis_size("dy") - 1
    add_x_face(g, y_ref, True, lambda w: jnp.where(has_x, from_x[w].astype(jnp.float32), 0.0), LATER)
    add_y_face(g, y_ref, True, lambda w: jnp.where(has_y, from_y[w].astype(jnp.float32), 0.0), LATER)
    add_line(g, y_ref, 1, 1, lambda w: jnp.where(has_x & has_y, from_xy[w], 0.0), LATER)
    sub = lax.broadcasted_iota(jnp.int32, (side, LANES), 0)
    rest = 2 * g.deg - side
    for i in range(g.ex * g.deg):
        e1 = i // g.deg
        a = i + 1 - e1 * g.deg
        for k in range(g.nz):
            e3 = k // g.deg
            rows = g.rows(a, k + 1 - e3 * g.deg, 1)
            for h in range(y_ref.shape[1]):
                d0 = pltpu.roll(y_ref[g.at(e1, 0, e3), h, rows], side - 1, 0)
                d1 = pltpu.roll(y_ref[g.at(e1, 1, e3), h, rows], side - 2, 0)
                start = (i * g.nz + k) * 2 * side
                out_ref[start : start + side, lanes(h)] = jnp.where(sub < g.deg, d0, d1)
                bottom = slice(start + side, start + 2 * side)
                out_ref[bottom, lanes(h)] = jnp.where(sub < rest, d1, 0.0)
    high, low = split(out_ref[...])
    high_ref[...] = high
    low_ref[...] = low
    inner = functools.partial(
        lax.dot_general,
        dimension_numbers=(((0,), (0,)), ((), ())),
        preferred_element_type=jnp.float32,
    )
    mixed = inner(high, low)
    gram = inner(high, high) + (mixed + mixed.T) + inner(low, low)

    def put(start, rows):
        packed_ref[start : start + rows.shape[0]] = rows

    pack(gram, put)
    half = kept_ref.shape[0]
    odd = lax.axis_index("dy") % 2 == 1
    first, second = packed_ref[:half], packed_ref[half:]
    kept_ref[...] = jnp.where(odd, second, first)
    sent_ref[...] = jnp.where(odd, first, second)


def invert_block(block):
    size = block.shape[0]
    groups = size // ROWS
    sub = lax.broadcasted_iota(jnp.int32, (ROWS, size), 0)
    lane = lax.broadcasted_iota(jnp.int32, (ROWS, size), 1)
    left = [block[ROWS * j : ROWS * (j + 1)] for j in range(groups)]
    right = [jnp.where(lane == sub + ROWS * j, 1.0, 0.0) for j in range(groups)]
    spread = lambda row: jnp.broadcast_to(row, (ROWS, size))
    result = []
    for k in range(groups):
        tile = left[k]
        cols = [spread(tile[:, ROWS * k + c : ROWS * k + c + 1]) for c in range(ROWS)]
        s = [[spread(cols[c][r : r + 1]) if c <= r else None for c in range(ROWS)] for r in range(ROWS)]
        take = [[None] * ROWS for _ in range(ROWS)]
        pairs = {}
        for j in range(0, ROWS, 2):
            p, q, t = s[j][j], s[j + 1][j], s[j + 1][j + 1]
            over = 1.0 / (p * t - q * q)
            across = q * (1.0 / p)
            pairs[j] = (
                (t * over, q * over, p * over),
                across,
                lax.rsqrt(p),
                lax.rsqrt(t - across * q),
            )
            one, both, two = pairs[j][0]
            for r in range(j + 2, ROWS):
                take[r][j] = s[r][j] * one - s[r][j + 1] * both
                take[r][j + 1] = s[r][j + 1] * two - s[r][j] * both
                for c in range(j + 2, r + 1):
                    s[r][c] = s[r][c] - (take[r][j] * s[c][j] + take[r][j + 1] * s[c][j + 1])
        last = k == groups - 1
        solved = []
        for source, wanted in ((right[k], True), (tile, False)):
            if last and not wanted:
                continue
            rows = [spread(source[r : r + 1]) for r in range(ROWS)]
            for j in range(0, ROWS, 2):
                for r in range(j + 2, ROWS):
                    rows[r] = rows[r] - (take[r][j] * rows[j] + take[r][j + 1] * rows[j + 1])
            if wanted:
                done = jnp.zeros((ROWS, size), jnp.float32)
                for j in range(0, ROWS, 2):
                    _, across, scale, scale_next = pairs[j]
                    done = jnp.where(sub == j, rows[j] * scale, done)
                    below = (rows[j + 1] - across * rows[j]) * scale_next
                    done = jnp.where(sub == j + 1, below, done)
                result.append(done)
            if last:
                continue
            for j in range(0, ROWS, 2):
                one, both, two = pairs[j][0]
                rows[j], rows[j + 1] = (
                    one * rows[j] - both * rows[j + 1],
                    two * rows[j + 1] - both * rows[j],
                )
            for j in reversed(range(0, ROWS, 2)):
                for r in range(j):
                    rows[r] = rows[r] - (take[j][r] * rows[j] + take[j + 1][r] * rows[j + 1])
            solved.append(rows)

        def tree(terms):
            while len(terms) > 1:
                terms = [a + b for a, b in zip(terms[::2], terms[1::2])]
            return terms[0]

        for j in range(k + 1, groups):
            cols = [spread(left[j][:, ROWS * k + c : ROWS * k + c + 1]) for c in range(ROWS)]
            left[j] = left[j] - tree([cols[c] * solved[1][c] for c in range(ROWS)])
            right[j] = right[j] - tree([cols[c] * solved[0][c] for c in range(ROWS)])
    return jnp.concatenate(result, axis=0)


def dot(one, two, axis_one=1, axis_two=0):
    return lax.dot_general(
        one,
        two,
        (((axis_one,), (axis_two,)), ((), ())),
        precision=lax.Precision.HIGHEST,
        preferred_element_type=jnp.float32,
    )


def inverse_factor(block_of, count):
    low, inv = {}, {}
    for i in range(count):
        diag = block_of(i, i)
        for j in range(i):
            part = block_of(i, j)
            for k in range(j):
                part = part - dot(low[i, k], low[j, k], 1, 1)
            low[i, j] = dot(part, inv[j, j], 1, 1)
            diag = diag - dot(low[i, j], low[i, j], 1, 1)
        sums = []
        for j in range(i):
            part = dot(low[i, j], inv[j, j])
            for k in range(j + 1, i):
                part = part + dot(low[i, k], inv[k, j])
            sums.append(part)
        inv[i, i] = invert_block(diag)
        for j in range(i):
            inv[i, j] = -dot(inv[i, i], sums[j])
    return inv

def basis_kernel(mine_ref, other_ref, high_ref, low_ref, out_ref, factor_ref, *, scale):
    @pl.when(pl.program_id(0) == 0)
    def _():
        count = high_ref.shape[1] // LANES
        odd = lax.axis_index("dy") % 2 == 1
        mine, other = mine_ref[...], other_ref[...]
        packed = jnp.concatenate(
            [jnp.where(odd, other, mine), jnp.where(odd, mine, other)], axis=0
        )
        inverse = inverse_factor(unpack(packed, count), count)
        for i in range(count):
            for j in range(count):
                block = inverse[i, j] * scale if j <= i else jnp.zeros((LANES, LANES), jnp.float32)
                high, low = split(block)
                factor_ref[0, lanes(i), lanes(j)] = high
                factor_ref[1, lanes(i), lanes(j)] = low

    slab, nz, ny, bands = out_ref.shape
    rows = high_ref.shape[0] // pl.num_programs(0)
    here = pl.ds(pl.multiple_of(pl.program_id(0) * rows, rows), rows)
    times = functools.partial(
        lax.dot_general,
        dimension_numbers=(((1,), (1,)), ((), ())),
        preferred_element_type=jnp.float32,
    )
    high, low = high_ref[here], low_ref[here]
    result = times(high, factor_ref[0]) + (times(high, factor_ref[1]) + times(low, factor_ref[0]))
    result = result.reshape(slab, nz, rows // (slab * nz), bands)
    out_ref[...] = result[:, :, :ny]


def call(kernel, outs, scratch, operands, flops):
    size = sum(x.size * x.dtype.itemsize for x in (*operands, *outs))
    return pl.pallas_call(
        kernel,
        out_shape=outs,
        in_specs=[VMEM] * len(operands),
        out_specs=[VMEM] * len(outs),
        scratch_shapes=scratch,
        compiler_params=pltpu.CompilerParams(vmem_limit_bytes=LIMIT),
        cost_estimate=pl.CostEstimate(flops=flops, bytes_accessed=size, transcendentals=0),
    )(*operands)


def shards(orbitals, elem_mats, conn):
    nx, ny, nz, bands = orbitals.shape
    side = round(elem_mats.shape[-1] ** (1 / 3))
    g = Grid(elem_mats, side)
    elem_mats = elem_mats.reshape(g.elements, g.count, g.count)
    f32 = jnp.float32
    orb = jnp.transpose(orbitals, (0, 2, 1, 3))
    shape = jax.ShapeDtypeStruct
    plane = -(-nx * nz // (2 * ROWS)) * 2 * ROWS
    tall = (plane + 2 * ROWS) * ROWS
    edges = call(
        edge_kernel,
        [
            shape((nz, ny, bands), orb.dtype),
            shape((plane, bands), orb.dtype),
            shape((2 * ROWS, bands), orb.dtype),
        ],
        [pltpu.VMEM((bands // LANES, tall, LANES), f32)],
        (orb,),
        0,
    )
    below_x, below_y, below_xy = [
        ring(s, *step) for s, step in zip(edges, ((1, 0), (0, 1), (1, 1)))
    ]
    mats = renumber(g, conn, elem_mats, ny + 1, nz + 2)

    nodes = (g.elements, bands // LANES, g.count, LANES)
    x_shape = shape((nz + g.ez - 1, g.ey * side, bands), jnp.bfloat16)
    y_shape = shape((g.ex * g.ez, side * side, bands), jnp.bfloat16)
    line_shape = shape((g.ez * side, bands), f32)
    corner_shape = shape((2, *line_shape.shape), f32)
    send_shapes = [x_shape] * 2 + [y_shape] * 2
    pairings = [("A", "-"), ("B", "-"), ("-", "A"), ("-", "B")]
    flops = 2 * g.elements * g.count**2 * bands

    def swap(sends):
        faces = [pair_swap(s, *pair) for s, pair in zip(sends, pairings)]
        kernel = functools.partial(corner_kernel, g=g)
        lines = call(kernel, [corner_shape] * 2, [], tuple(faces[:2]), 0)
        return *faces, *[pair_swap(s, *pair) for s, pair in zip(lines, pairings[2:])]

    y0, part, *sends = call(
        functools.partial(first_kernel, g=g),
        [shape(nodes, f32), shape(nodes, f32), *send_shapes],
        [],
        (orb, below_x, below_y, below_xy, mats),
        flops,
    )
    received = swap(sends)
    y1, part, *sends = call(
        functools.partial(middle_kernel, g=g),
        [shape(nodes, f32), shape(nodes, f32), *send_shapes],
        [],
        (part, *received, y0, mats),
        flops,
    )
    received = swap(sends)
    part, *sends = call(
        functools.partial(late_kernel, g=g),
        [shape(nodes, f32), x_shape, y_shape, line_shape],
        [pltpu.VMEM(nodes, f32)],
        (part, *received, y1, mats),
        flops,
    )
    received = [ring(s, *step) for s, step in zip(sends, ((-1, 0), (0, -1), (-1, -1)))]
    rows = nx * nz * 2 * side
    packed = packed_rows(bands)
    half_shape = shape((packed // 2, LANES), f32)
    high, low, kept, sent = call(
        functools.partial(last_kernel, g=g),
        [shape((rows, bands), jnp.bfloat16)] * 2 + [half_shape] * 2,
        [pltpu.VMEM(nodes, f32), pltpu.VMEM((rows, bands), f32), pltpu.VMEM((packed, LANES), f32)],
        (part, *received),
        8 * rows * bands**2,
    )
    mine, other = halved_total(kept, sent)
    slabs = g.ex
    spot = pl.BlockSpec((nx // slabs, nz, ny, bands), lambda i: (i, 0, 0, 0))
    basis = pl.pallas_call(
        functools.partial(basis_kernel, scale=math.sqrt(nx * ny * nz * lax.axis_size(AXES))),
        out_shape=shape((nx, nz, ny, bands), f32),
        grid=(slabs,),
        in_specs=[VMEM] * 4,
        out_specs=spot,
        scratch_shapes=[pltpu.VMEM((2, bands, bands), jnp.bfloat16)],
        compiler_params=pltpu.CompilerParams(vmem_limit_bytes=LIMIT),
        name="basis",
    )(mine, other, high, low)
    return jnp.transpose(basis, (0, 2, 1, 3))


def solution(mesh):
    in_specs = (
        P("dx", "dy", None, None),
        P("dx", "dy", None, None, None),
        P("dx", "dy", None, None),
    )
    out_specs = P("dx", "dy", None, None)
    return jax.shard_map(shards, mesh=mesh, in_specs=in_specs, out_specs=out_specs, check_vma=False)
```

```python
import functools
import math

import jax
import jax.numpy as jnp
from jax import lax
from jax.experimental import pallas as pl
from jax.experimental.pallas import tpu as pltpu
from jax.sharding import PartitionSpec as P

filter_center = 1.5
filter_half = 4.0
FIRST = 1.0 / filter_half
LATER = 2.0 / filter_half
AXES = ("dx", "dy")
VMEM = pl.BlockSpec(memory_space=pltpu.VMEM)
LIMIT = 16 * 1024 * 1024
LANES = 128
ROWS = 8


def partner(index, size, pairing, closed):
    if pairing == "-":
        return index
    other = index ^ 1 if pairing == "A" else index - 1 if index % 2 == 0 else index + 1
    if 0 <= other < size:
        return other
    return size - 1 - index if closed and pairing == "B" and size % 2 == 0 else index


def pair_swap(value, along_x, along_y):
    size_x, size_y = lax.axis_size("dx"), lax.axis_size("dy")
    route = [
        (
            p * size_y + q,
            partner(p, size_x, along_x, False) * size_y + partner(q, size_y, along_y, True),
        )
        for p in range(size_x)
        for q in range(size_y)
    ]
    return lax.ppermute(value, AXES, route)


def ring(value, step_x, step_y):
    size_x, size_y = lax.axis_size("dx"), lax.axis_size("dy")
    route = [
        (p * size_y + q, (p + step_x) % size_x * size_y + (q + step_y) % size_y)
        for p in range(size_x)
        for q in range(size_y)
    ]
    return lax.ppermute(value, AXES, route)


def xor_swap(value, axis, bits):
    return lax.ppermute(value, axis, [(i, i ^ bits) for i in range(lax.axis_size(axis))])


def sum_swap(value, stage, bits):
    size_x, size_y = lax.axis_size("dx"), lax.axis_size("dy")
    route = []
    for p in range(size_x):
        for q in range(size_y):
            along_x = (q + stage) % 2 == 0
            to = (p ^ bits, q) if along_x else (p, q ^ 2 * bits)
            route.append((p * size_y + q, to[0] * size_y + to[1]))
    return lax.ppermute(value, AXES, route)


def halved_total(kept, sent):
    part = kept + xor_swap(sent, "dy", 1)
    sizes = lax.axis_size("dx"), lax.axis_size("dy") // 2
    if sizes[0] == sizes[1]:
        steps = [functools.partial(sum_swap, stage=stage) for stage in (0, 1)]
    else:
        steps = [
            lambda value, bits: xor_swap(value, "dx", bits),
            lambda value, bits: xor_swap(value, "dy", 2 * bits),
        ]
    for step, size in zip(steps, sizes):
        bit = 1
        while bit < size:
            if 2 * bit < size:
                one, two, three = [step(part, bits=bit * k) for k in (1, 2, 3)]
                part = (part + one) + (two + three)
                bit *= 4
            else:
                part = part + step(part, bits=bit)
                bit *= 2
    return part, xor_swap(part, "dy", 1)


def renumber_kernel(conn_ref, mats_ref, out_ref, *, g, width, depth):
    side, deg, layers = g.side, g.deg, g.ez
    spots = [
        (e1, e2, e3) for e1 in range(g.ex) for e2 in range(g.ey) for e3 in range(g.ez)
    ]
    for e, (e1, e2, e3) in enumerate(spots):
        node = conn_ref[e1, e2, e3 : e3 + 1].astype(jnp.float32)
        plane = jnp.floor((node + 0.5) * (1.0 / depth))
        first = jnp.floor((plane + 0.5) * (1.0 / width))
        c = (node - plane * depth).astype(jnp.int32) - deg * e3
        b = (plane - first * width).astype(jnp.int32) - deg * e2
        a = first.astype(jnp.int32) - deg * e1
        place = (a * side + c) * side + b
        if e1 == 0:
            place = jnp.where((a == 0) & (lax.axis_index("dx") == 0), -1, place)
        if e2 == 0:
            place = jnp.where((b == 0) & (lax.axis_index("dy") == 0), -1, place)
        if e3 == 0:
            place = jnp.where(c == 0, -1, place)
        if e3 == layers - 1:
            place = jnp.where(c == deg, -1, place)
        order = lax.broadcasted_iota(jnp.int32, (g.count, g.count), 0) == place
        order = jnp.where(order, 1.0, 0.0).astype(jnp.bfloat16)
        half = jnp.dot(order, mats_ref[e], preferred_element_type=jnp.float32)
        whole = lax.dot_general(
            half.astype(jnp.bfloat16),
            order,
            (((1,), (1,)), ((), ())),
            preferred_element_type=jnp.float32,
        )
        out_ref[e] = whole.astype(jnp.bfloat16)


def renumber(g, conn, elem_mats, width, depth):
    shape = (g.elements, g.count, g.count)
    return pl.pallas_call(
        functools.partial(renumber_kernel, g=g, width=width, depth=depth),
        out_shape=jax.ShapeDtypeStruct(shape, jnp.bfloat16),
        in_specs=[VMEM] * 2,
        out_specs=VMEM,
        compiler_params=pltpu.CompilerParams(vmem_limit_bytes=LIMIT),
        cost_estimate=pl.CostEstimate(
            flops=4 * g.elements * g.count**3,
            bytes_accessed=4 * elem_mats.size,
            transcendentals=0,
        ),
        name="renumber",
    )(conn, elem_mats)


class Grid:
    def __init__(self, elem_mats, side):
        self.ex, self.ey, self.ez = elem_mats.shape[:3]
        self.count = elem_mats.shape[3]
        self.side = side
        self.deg = side - 1
        self.nz = self.ez * self.deg - 1
        self.elements = self.ex * self.ey * self.ez

    def at(self, e1, e2, e3):
        return (e1 * self.ey + e2) * self.ez + e3

    def rows(self, a, c, number):
        start = (a * self.side + c) * self.side
        return slice(start, start + number * self.side)

    def layers(self, e3):
        low = 1 if e3 == 0 else 0
        high = self.deg - 1 if e3 == self.ez - 1 else self.deg
        return low, high - low + 1, e3 * self.deg + low - 1

    def side_rows(self, b):
        return pl.ds(b, self.side * self.side, stride=self.side)

    def line_rows(self, a, b):
        return pl.ds(a * self.side * self.side + b, self.side, stride=self.side)


def lanes(h):
    return slice(h * LANES, (h + 1) * LANES)


def multiply(g, mats_ref, field_of, w_ref):
    side, deg = g.side, g.deg
    halves = range(w_ref.shape[1])
    for e in range(g.elements):
        product = jnp.dot(mats_ref[e], field_of(e), preferred_element_type=jnp.float32)
        for h in halves:
            w_ref[e, h] = product[:, lanes(h)]

    def join(one, top, two, bottom):
        for h in halves:
            both = w_ref[one, h, top] + w_ref[two, h, bottom]
            w_ref[one, h, top] = both
            w_ref[two, h, bottom] = both

    for e1 in range(g.ex):
        for e2 in range(g.ey):
            for e3 in range(g.ez - 1):
                for a in range(side):
                    one, two = g.at(e1, e2, e3), g.at(e1, e2, e3 + 1)
                    join(one, g.rows(a, deg, 1), two, g.rows(a, 0, 1))
    for e1 in range(g.ex - 1):
        for e2 in range(g.ey):
            for e3 in range(g.ez):
                one, two = g.at(e1, e2, e3), g.at(e1 + 1, e2, e3)
                join(one, g.rows(deg, 0, side), two, g.rows(0, 0, side))
    for e1 in range(g.ex):
        for e2 in range(g.ey - 1):
            for e3 in range(g.ez):
                one, two = g.at(e1, e2, e3), g.at(e1, e2 + 1, e3)
                join(one, g.side_rows(deg), two, g.side_rows(0))


def rest_of(value):
    return value - value.astype(jnp.bfloat16).astype(jnp.float32)


def put_x_face(g, w_ref, put):
    for h in range(w_ref.shape[1]):
        for e2 in range(g.ey):
            for e3 in range(g.ez):
                low, number, start = g.layers(e3)
                if e3 > 0:
                    low, number, start = low + 1, number - 1, start + 1
                one = w_ref[g.at(0, e2, e3), h, g.rows(0, low, number)]
                two = w_ref[g.at(g.ex - 1, e2, e3), h, g.rows(g.deg, low, number)]
                where = (
                    slice(start, start + number),
                    slice(e2 * g.side, (e2 + 1) * g.side),
                    lanes(h),
                )
                shape = (number, g.side, LANES)
                put(where, one.reshape(shape), two.reshape(shape))
                if e3 < g.ez - 1:
                    one, two = one[-g.side :], two[-g.side :]
                    put((g.nz + e3, *where[1:]), rest_of(one), rest_of(two))


def put_y_face(g, w_ref, put):
    for h in range(w_ref.shape[1]):
        for e1 in range(g.ex):
            for e3 in range(g.ez):
                one = w_ref[g.at(e1, 0, e3), h, g.side_rows(0)]
                two = w_ref[g.at(e1, g.ey - 1, e3), h, g.side_rows(g.deg)]
                if e3 > 0:
                    layer = lax.broadcasted_iota(jnp.int32, one.shape, 0) % g.side
                    one = jnp.where(layer == 0, rest_of(one), one)
                    two = jnp.where(layer == 0, rest_of(two), two)
                put((e1 * g.ez + e3, slice(None), lanes(h)), one, two)


def line(g, w_ref, high_x, high_y, e3, h):
    e1, a = (g.ex - 1, g.deg) if high_x else (0, 0)
    e2, b = (g.ey - 1, g.deg) if high_y else (0, 0)
    return w_ref[g.at(e1, e2, e3), h, g.line_rows(a, b)]


def add_x_face(g, out_ref, high, received, factor):
    e1, a = (g.ex - 1, g.deg) if high else (0, 0)
    for h in range(out_ref.shape[1]):
        for e2 in range(g.ey):
            for e3 in range(g.ez):
                low, number, start = g.layers(e3)
                columns = slice(e2 * g.side, (e2 + 1) * g.side)
                part = received((slice(start, start + number), columns, lanes(h)))
                rows = g.rows(a, low, number)
                part = part.reshape(number * g.side, LANES)
                e = g.at(e1, e2, e3)
                out_ref[e, h, rows] += factor * part
                if e3 < g.ez - 1:
                    part = received((g.nz + e3, columns, lanes(h)))
                    out_ref[e, h, g.rows(a, g.deg, 1)] += factor * part
                if e3 > 0:
                    part = received((g.nz + e3 - 1, columns, lanes(h)))
                    out_ref[e, h, g.rows(a, 0, 1)] += factor * part


def add_y_face(g, out_ref, high, received, factor):
    e2, b = (g.ey - 1, g.deg) if high else (0, 0)
    for h in range(out_ref.shape[1]):
        for e1 in range(g.ex):
            parts = [
                received((e1 * g.ez + e3, slice(None), lanes(h))) for e3 in range(g.ez)
            ]
            count = parts[0].shape[0]
            layer = lax.broadcasted_iota(jnp.int32, parts[0].shape, 0) % g.side
            for e3 in range(g.ez):
                part = parts[e3]
                if e3 < g.ez - 1:
                    above = pltpu.roll(parts[e3 + 1], g.deg, 0)
                    part = part + jnp.where(layer == g.deg, above, 0.0)
                if e3 > 0:
                    below = pltpu.roll(parts[e3 - 1], count - g.deg, 0)
                    part = part + jnp.where(layer == 0, below, 0.0)
                out_ref[g.at(e1, e2, e3), h, g.side_rows(b)] += factor * part


def add_line(g, out_ref, high_x, high_y, received, factor):
    e1, a = (g.ex - 1, g.deg) if high_x else (0, 0)
    e2, b = (g.ey - 1, g.deg) if high_y else (0, 0)
    for h in range(out_ref.shape[1]):
        for e3 in range(g.ez):
            part = received((slice(e3 * g.side, (e3 + 1) * g.side), lanes(h)))
            out_ref[g.at(e1, e2, e3), h, g.line_rows(a, b)] += factor * part


def send_all(g, w_ref, sends):
    even_x = lax.axis_index("dx") % 2 == 0
    even_y = lax.axis_index("dy") % 2 == 0

    def by_pair(even, one_ref, two_ref):
        def put(where, low, high):
            one_ref[where] = jnp.where(even, high, low).astype(one_ref.dtype)
            two_ref[where] = jnp.where(even, low, high).astype(two_ref.dtype)

        return put

    put_x_face(g, w_ref, by_pair(even_x, sends[0], sends[1]))
    put_y_face(g, w_ref, by_pair(even_y, sends[2], sends[3]))


def corner_kernel(from_a, from_b, to_a, to_b, *, g):
    even = lax.axis_index("dy") % 2 == 0
    last = from_a.shape[1] - 1
    bands = from_a.shape[2]
    for k, source in enumerate((from_a, from_b)):
        for e3 in range(g.ez):
            low, number, start = g.layers(e3)
            for c in range(g.side):
                row = slice(e3 * g.side + c, e3 * g.side + c + 1)
                if low <= c < low + number:
                    z = start + c - low
                    both = source[z].astype(jnp.float32)
                    if (z + 1) % g.deg == 0:
                        layer = g.nz + (z + 1) // g.deg - 1
                        both = both + source[layer].astype(jnp.float32)
                    bottom, top = both[0:1], both[last : last + 1]
                    to_a[k, row] = jnp.where(even, top, bottom)
                    to_b[k, row] = jnp.where(even, bottom, top)
                else:
                    to_a[k, row] = jnp.zeros((1, bands), jnp.float32)
                    to_b[k, row] = jnp.zeros((1, bands), jnp.float32)


def add_all(g, out_ref, received, factor):
    p, q = lax.axis_index("dx"), lax.axis_index("dy")
    even_x, even_y = p % 2 == 0, q % 2 == 0
    has_x = (p > 0, p < lax.axis_size("dx") - 1)
    has_y = (q > 0, q < lax.axis_size("dy") - 1)

    def from_pair(even, high, one, two, exists):
        one, two = one.astype(jnp.float32), two.astype(jnp.float32)
        value = jnp.where(even, one, two) if high else jnp.where(even, two, one)
        return jnp.where(exists, value, 0.0)

    for high in (0, 1):

        def across_x(where):
            return from_pair(even_x, high, received[0][where], received[1][where], has_x[high])

        def across_y(where):
            return from_pair(even_y, high, received[2][where], received[3][where], has_y[high])

        add_x_face(g, out_ref, high, across_x, factor)
        add_y_face(g, out_ref, high, across_y, factor)
    for hx in (0, 1):
        for hy in (0, 1):

            def diagonal(where):
                one, two = [
                    from_pair(even_y, hy, received[4][k, *where], received[5][k, *where], has_y[hy])
                    for k in (0, 1)
                ]
                return from_pair(even_x, hx, one, two, has_x[hx])

            add_line(g, out_ref, hx, hy, diagonal, factor)


def field_of(y_ref, e):
    parts = [y_ref[e, h].astype(jnp.bfloat16) for h in range(y_ref.shape[1])]
    return jnp.concatenate(parts, axis=-1)


def edge_kernel(orb_ref, x_ref, y_ref, line_ref, tiles_ref):
    nx, nz, ny, bands = orb_ref.shape
    last = (ny - 1) % ROWS
    tail = slice(ny - 1 - last, ny)
    x_ref[...] = orb_ref[nx - 1]
    for h in range(bands // LANES):
        for i in range(nx):
            part = orb_ref[i, :, tail, lanes(h)].astype(jnp.float32)
            for k in range(nz):
                start = (i * nz + k) * ROWS
                tiles_ref[h, start : start + last + 1] = part[k]
        rows = tiles_ref[h, pl.ds(last, y_ref.shape[0], stride=ROWS)]
        y_ref[:, lanes(h)] = rows.astype(jnp.bfloat16)
        line = tiles_ref[h, pl.ds((nx - 1) * nz * ROWS + last, line_ref.shape[0], stride=ROWS)]
        line_ref[:, lanes(h)] = line.astype(jnp.bfloat16)


def first_kernel(*refs, g):
    orb_ref, below_x, below_y, below_xy, mats_ref, y_ref, next_ref, *sends = refs
    side = g.side
    halves = range(y_ref.shape[1])
    sub = lax.broadcasted_iota(jnp.int32, (side, LANES), 0)
    nothing = jnp.zeros((side, LANES), jnp.float32)
    rest = orb_ref.shape[2] - side
    for e1 in range(g.ex):
        for e2 in range(g.ey):
            for a in range(side):
                for h in halves:
                    y_ref[g.at(e1, e2, 0), h, g.rows(a, 0, 1)] = nothing
                    y_ref[g.at(e1, e2, g.ez - 1), h, g.rows(a, g.deg, 1)] = nothing

    def place(i, k, column, edge):
        for h in halves:
            part = column[:, lanes(h)].astype(jnp.float32)
            t0 = part[:side]
            t1 = jnp.concatenate([part[side:], nothing[: side - rest]], axis=0)
            first = jnp.broadcast_to(edge[:, lanes(h)].astype(jnp.float32), (side, LANES))
            d0 = jnp.where(sub == 0, first, pltpu.roll(t0, 1, 0))
            d1 = jnp.where(sub < 2, pltpu.roll(t0, 2, 0), pltpu.roll(t1, 2, 0))
            for e1 in range(g.ex):
                a = i - e1 * g.deg
                for e3 in range(g.ez):
                    c = k + 1 - e3 * g.deg
                    if 0 <= a <= g.deg and 0 <= c <= g.deg:
                        y_ref[g.at(e1, 0, e3), h, g.rows(a, c, 1)] = d0
                        y_ref[g.at(e1, 1, e3), h, g.rows(a, c, 1)] = d1

    for k in range(g.nz):
        place(0, k, below_x[k], below_xy[k : k + 1])
        for i in range(orb_ref.shape[0]):
            place(i + 1, k, orb_ref[i, k], below_y[i * g.nz + k : i * g.nz + k + 1])
    multiply(g, mats_ref, functools.partial(field_of, y_ref), next_ref)
    send_all(g, next_ref, sends)
    advance(next_ref, y_ref, None, FIRST)


def advance(next_ref, now_ref, older_ref, gain):
    for e in range(next_ref.shape[0]):
        for h in range(next_ref.shape[1]):
            value = gain * (next_ref[e, h] - filter_center * now_ref[e, h])
            next_ref[e, h] = value if older_ref is None else value - older_ref[e, h]


def middle_kernel(*refs, g):
    part_ref, *refs = refs
    received, refs = refs[:6], refs[6:]
    older_ref, mats_ref, y_ref, next_ref, *sends = refs
    y_ref[...] = part_ref[...]
    add_all(g, y_ref, received, FIRST)
    multiply(g, mats_ref, functools.partial(field_of, y_ref), next_ref)
    send_all(g, next_ref, sends)
    advance(next_ref, y_ref, older_ref, LATER)


def late_kernel(*refs, g):
    part_ref, *refs = refs
    received, refs = refs[:6], refs[6:]
    older_ref, mats_ref, next_ref, *sends, y_ref = refs
    y_ref[...] = part_ref[...]
    add_all(g, y_ref, received, LATER)
    multiply(g, mats_ref, functools.partial(field_of, y_ref), next_ref)

    def put_low(ref):
        def put(where, low, high):
            ref[where] = low.astype(ref.dtype)

        return put

    put_x_face(g, next_ref, put_low(sends[0]))
    put_y_face(g, next_ref, put_low(sends[1]))
    for h in range(next_ref.shape[1]):
        for e3 in range(g.ez):
            rows = slice(e3 * g.side, (e3 + 1) * g.side)
            sends[2][rows, lanes(h)] = line(g, next_ref, 0, 0, e3, h)
    advance(next_ref, y_ref, older_ref, LATER)


def split(value):
    high = value.astype(jnp.bfloat16)
    return high, (value - high.astype(jnp.float32)).astype(jnp.bfloat16)


def packed_rows(bands):
    count = bands // LANES
    return count * bands if count != 2 else bands + 2 * ROWS


def pack(gram, put):
    count = gram.shape[0] // LANES
    block = lambda i, j: gram[lanes(i), lanes(j)]
    if count != 2:
        for i in range(count):
            for j in range(count):
                put((i * count + j) * LANES, block(i, j))
        return
    row = lax.broadcasted_iota(jnp.int32, (LANES, LANES), 0)
    lane = lax.broadcasted_iota(jnp.int32, (LANES, LANES), 1)
    put(0, jnp.where(row >= lane, block(0, 0), block(1, 1)))
    put(LANES, block(1, 0))
    diagonal = jnp.sum(jnp.where(row == lane, block(1, 1), 0.0), axis=0, keepdims=True)
    put(2 * LANES, jnp.broadcast_to(diagonal, (2 * ROWS, LANES)))


def unpack(packed, count):
    block = lambda k: packed[k * LANES : (k + 1) * LANES]
    if count != 2:
        return lambda i, j: block(i * count + j)
    row = lax.broadcasted_iota(jnp.int32, (LANES, LANES), 0)
    lane = lax.broadcasted_iota(jnp.int32, (LANES, LANES), 1)
    both = block(0)
    first = jnp.where(row > lane, both, 0.0)
    second = jnp.where(row < lane, both, 0.0)
    diagonal = jnp.broadcast_to(packed[2 * LANES : 2 * LANES + 1], (LANES, LANES))
    blocks = {
        (0, 0): first + first.T + jnp.where(row == lane, both, 0.0),
        (1, 0): block(1),
        (1, 1): second + second.T + jnp.where(row == lane, diagonal, 0.0),
    }
    return lambda i, j: blocks[i, j]


def last_kernel(part_ref, from_x, from_y, from_xy, *refs, g):
    high_ref, low_ref, kept_ref, sent_ref, y_ref, out_ref, packed_ref = refs
    side = g.side
    y_ref[...] = part_ref[...]
    p, q = lax.axis_index("dx"), lax.axis_index("dy")
    has_x, has_y = p < lax.axis_size("dx") - 1, q < lax.axis_size("dy") - 1
    add_x_face(g, y_ref, True, lambda w: jnp.where(has_x, from_x[w].astype(jnp.float32), 0.0), LATER)
    add_y_face(g, y_ref, True, lambda w: jnp.where(has_y, from_y[w].astype(jnp.float32), 0.0), LATER)
    add_line(g, y_ref, 1, 1, lambda w: jnp.where(has_x & has_y, from_xy[w], 0.0), LATER)
    sub = lax.broadcasted_iota(jnp.int32, (side, LANES), 0)
    rest = 2 * g.deg - side
    for i in range(g.ex * g.deg):
        e1 = i // g.deg
        a = i + 1 - e1 * g.deg
        for k in range(g.nz):
            e3 = k // g.deg
            rows = g.rows(a, k + 1 - e3 * g.deg, 1)
            for h in range(y_ref.shape[1]):
                d0 = pltpu.roll(y_ref[g.at(e1, 0, e3), h, rows], side - 1, 0)
                d1 = pltpu.roll(y_ref[g.at(e1, 1, e3), h, rows], side - 2, 0)
                start = (i * g.nz + k) * 2 * side
                out_ref[start : start + side, lanes(h)] = jnp.where(sub < g.deg, d0, d1)
                bottom = slice(start + side, start + 2 * side)
                out_ref[bottom, lanes(h)] = jnp.where(sub < rest, d1, 0.0)
    high, low = split(out_ref[...])
    high_ref[...] = high
    low_ref[...] = low
    inner = functools.partial(
        lax.dot_general,
        dimension_numbers=(((0,), (0,)), ((), ())),
        preferred_element_type=jnp.float32,
    )
    mixed = inner(high, low)
    gram = inner(high, high) + (mixed + mixed.T) + inner(low, low)

    def put(start, rows):
        packed_ref[start : start + rows.shape[0]] = rows

    pack(gram, put)
    half = kept_ref.shape[0]
    odd = lax.axis_index("dy") % 2 == 1
    first, second = packed_ref[:half], packed_ref[half:]
    kept_ref[...] = jnp.where(odd, second, first)
    sent_ref[...] = jnp.where(odd, first, second)


def invert_block(block):
    size = block.shape[0]
    groups = size // ROWS
    sub = lax.broadcasted_iota(jnp.int32, (ROWS, size), 0)
    lane = lax.broadcasted_iota(jnp.int32, (ROWS, size), 1)
    left = [block[ROWS * j : ROWS * (j + 1)] for j in range(groups)]
    right = [jnp.where(lane == sub + ROWS * j, 1.0, 0.0) for j in range(groups)]
    spread = lambda row: jnp.broadcast_to(row, (ROWS, size))
    result = []
    for k in range(groups):
        tile = left[k]
        cols = [spread(tile[:, ROWS * k + c : ROWS * k + c + 1]) for c in range(ROWS)]
        s = [[spread(cols[c][r : r + 1]) if c <= r else None for c in range(ROWS)] for r in range(ROWS)]
        take = [[None] * ROWS for _ in range(ROWS)]
        pairs = {}
        for j in range(0, ROWS, 2):
            p, q, t = s[j][j], s[j + 1][j], s[j + 1][j + 1]
            over = 1.0 / (p * t - q * q)
            across = q * (1.0 / p)
            pairs[j] = (
                (t * over, q * over, p * over),
                across,
                lax.rsqrt(p),
                lax.rsqrt(t - across * q),
            )
            one, both, two = pairs[j][0]
            for r in range(j + 2, ROWS):
                take[r][j] = s[r][j] * one - s[r][j + 1] * both
                take[r][j + 1] = s[r][j + 1] * two - s[r][j] * both
                for c in range(j + 2, r + 1):
                    s[r][c] = s[r][c] - (take[r][j] * s[c][j] + take[r][j + 1] * s[c][j + 1])
        last = k == groups - 1
        solved = []
        for source, wanted in ((right[k], True), (tile, False)):
            if last and not wanted:
                continue
            rows = [spread(source[r : r + 1]) for r in range(ROWS)]
            for j in range(0, ROWS, 2):
                for r in range(j + 2, ROWS):
                    rows[r] = rows[r] - (take[r][j] * rows[j] + take[r][j + 1] * rows[j + 1])
            if wanted:
                done = jnp.zeros((ROWS, size), jnp.float32)
                for j in range(0, ROWS, 2):
                    _, across, scale, scale_next = pairs[j]
                    done = jnp.where(sub == j, rows[j] * scale, done)
                    below = (rows[j + 1] - across * rows[j]) * scale_next
                    done = jnp.where(sub == j + 1, below, done)
                result.append(done)
            if last:
                continue
            for j in range(0, ROWS, 2):
                one, both, two = pairs[j][0]
                rows[j], rows[j + 1] = (
                    one * rows[j] - both * rows[j + 1],
                    two * rows[j + 1] - both * rows[j],
                )
            for j in reversed(range(0, ROWS, 2)):
                for r in range(j):
                    rows[r] = rows[r] - (take[j][r] * rows[j] + take[j + 1][r] * rows[j + 1])
            solved.append(rows)

        def tree(terms):
            while len(terms) > 1:
                terms = [a + b for a, b in zip(terms[::2], terms[1::2])]
            return terms[0]

        for j in range(k + 1, groups):
            cols = [spread(left[j][:, ROWS * k + c : ROWS * k + c + 1]) for c in range(ROWS)]
            left[j] = left[j] - tree([cols[c] * solved[1][c] for c in range(ROWS)])
            right[j] = right[j] - tree([cols[c] * solved[0][c] for c in range(ROWS)])
    return jnp.concatenate(result, axis=0)


def dot(one, two, axis_one=1, axis_two=0):
    return lax.dot_general(
        one,
        two,
        (((axis_one,), (axis_two,)), ((), ())),
        precision=lax.Precision.HIGHEST,
        preferred_element_type=jnp.float32,
    )


def inverse_factor(block_of, count):
    low, inv = {}, {}
    for i in range(count):
        diag = block_of(i, i)
        for j in range(i):
            part = block_of(i, j)
            for k in range(j):
                part = part - dot(low[i, k], low[j, k], 1, 1)
            low[i, j] = dot(part, inv[j, j], 1, 1)
            diag = diag - dot(low[i, j], low[i, j], 1, 1)
        sums = []
        for j in range(i):
            part = dot(low[i, j], inv[j, j])
            for k in range(j + 1, i):
                part = part + dot(low[i, k], inv[k, j])
            sums.append(part)
        inv[i, i] = invert_block(diag)
        for j in range(i):
            inv[i, j] = -dot(inv[i, i], sums[j])
    return inv

def basis_kernel(mine_ref, other_ref, high_ref, low_ref, out_ref, factor_ref, *, scale):
    @pl.when(pl.program_id(0) == 0)
    def _():
        count = high_ref.shape[1] // LANES
        odd = lax.axis_index("dy") % 2 == 1
        mine, other = mine_ref[...], other_ref[...]
        packed = jnp.concatenate(
            [jnp.where(odd, other, mine), jnp.where(odd, mine, other)], axis=0
        )
        inverse = inverse_factor(unpack(packed, count), count)
        for i in range(count):
            for j in range(count):
                block = inverse[i, j] * scale if j <= i else jnp.zeros((LANES, LANES), jnp.float32)
                high, low = split(block)
                factor_ref[0, lanes(i), lanes(j)] = high
                factor_ref[1, lanes(i), lanes(j)] = low

    slab, nz, ny, bands = out_ref.shape
    rows = high_ref.shape[0] // pl.num_programs(0)
    here = pl.ds(pl.multiple_of(pl.program_id(0) * rows, rows), rows)
    times = functools.partial(
        lax.dot_general,
        dimension_numbers=(((1,), (1,)), ((), ())),
        preferred_element_type=jnp.float32,
    )
    high, low = high_ref[here], low_ref[here]
    result = times(high, factor_ref[0]) + (times(high, factor_ref[1]) + times(low, factor_ref[0]))
    result = result.reshape(slab, nz, rows // (slab * nz), bands)
    out_ref[...] = result[:, :, :ny]


def call(kernel, outs, scratch, operands, flops):
    size = sum(x.size * x.dtype.itemsize for x in (*operands, *outs))
    return pl.pallas_call(
        kernel,
        out_shape=outs,
        in_specs=[VMEM] * len(operands),
        out_specs=[VMEM] * len(outs),
        scratch_shapes=scratch,
        compiler_params=pltpu.CompilerParams(vmem_limit_bytes=LIMIT),
        cost_estimate=pl.CostEstimate(flops=flops, bytes_accessed=size, transcendentals=0),
    )(*operands)


def shards(orbitals, elem_mats, conn):
    nx, ny, nz, bands = orbitals.shape
    side = round(elem_mats.shape[-1] ** (1 / 3))
    g = Grid(elem_mats, side)
    elem_mats = elem_mats.reshape(g.elements, g.count, g.count)
    f32 = jnp.float32
    orb = jnp.transpose(orbitals, (0, 2, 1, 3))
    shape = jax.ShapeDtypeStruct
    plane = -(-nx * nz // (2 * ROWS)) * 2 * ROWS
    tall = (plane + 2 * ROWS) * ROWS
    edges = call(
        edge_kernel,
        [
            shape((nz, ny, bands), orb.dtype),
            shape((plane, bands), orb.dtype),
            shape((2 * ROWS, bands), orb.dtype),
        ],
        [pltpu.VMEM((bands // LANES, tall, LANES), f32)],
        (orb,),
        0,
    )
    below_x, below_y, below_xy = [
        ring(s, *step) for s, step in zip(edges, ((1, 0), (0, 1), (1, 1)))
    ]
    mats = renumber(g, conn, elem_mats, ny + 1, nz + 2)

    nodes = (g.elements, bands // LANES, g.count, LANES)
    x_shape = shape((nz + g.ez - 1, g.ey * side, bands), jnp.bfloat16)
    y_shape = shape((g.ex * g.ez, side * side, bands), jnp.bfloat16)
    line_shape = shape((g.ez * side, bands), f32)
    corner_shape = shape((2, *line_shape.shape), f32)
    send_shapes = [x_shape] * 2 + [y_shape] * 2
    pairings = [("A", "-"), ("B", "-"), ("-", "A"), ("-", "B")]
    flops = 2 * g.elements * g.count**2 * bands

    def swap(sends):
        faces = [pair_swap(s, *pair) for s, pair in zip(sends, pairings)]
        kernel = functools.partial(corner_kernel, g=g)
        lines = call(kernel, [corner_shape] * 2, [], tuple(faces[:2]), 0)
        return *faces, *[pair_swap(s, *pair) for s, pair in zip(lines, pairings[2:])]

    y0, part, *sends = call(
        functools.partial(first_kernel, g=g),
        [shape(nodes, f32), shape(nodes, f32), *send_shapes],
        [],
        (orb, below_x, below_y, below_xy, mats),
        flops,
    )
    received = swap(sends)
    y1, part, *sends = call(
        functools.partial(middle_kernel, g=g),
        [shape(nodes, f32), shape(nodes, f32), *send_shapes],
        [],
        (part, *received, y0, mats),
        flops,
    )
    received = swap(sends)
    part, *sends = call(
        functools.partial(late_kernel, g=g),
        [shape(nodes, f32), x_shape, y_shape, line_shape],
        [pltpu.VMEM(nodes, f32)],
        (part, *received, y1, mats),
        flops,
    )
    received = [ring(s, *step) for s, step in zip(sends, ((-1, 0), (0, -1), (-1, -1)))]
    rows = nx * nz * 2 * side
    packed = packed_rows(bands)
    half_shape = shape((packed // 2, LANES), f32)
    high, low, kept, sent = call(
        functools.partial(last_kernel, g=g),
        [shape((rows, bands), jnp.bfloat16)] * 2 + [half_shape] * 2,
        [pltpu.VMEM(nodes, f32), pltpu.VMEM((rows, bands), f32), pltpu.VMEM((packed, LANES), f32)],
        (part, *received),
        8 * rows * bands**2,
    )
    mine, other = halved_total(kept, sent)
    slabs = 1
    spot = pl.BlockSpec((nx // slabs, nz, ny, bands), lambda i: (i, 0, 0, 0))
    basis = pl.pallas_call(
        functools.partial(basis_kernel, scale=math.sqrt(nx * ny * nz * lax.axis_size(AXES))),
        out_shape=shape((nx, nz, ny, bands), f32),
        grid=(slabs,),
        in_specs=[VMEM] * 4,
        out_specs=spot,
        scratch_shapes=[pltpu.VMEM((2, bands, bands), jnp.bfloat16)],
        compiler_params=pltpu.CompilerParams(vmem_limit_bytes=LIMIT),
        name="basis",
    )(mine, other, high, low)
    return jnp.transpose(basis, (0, 2, 1, 3))


def solution(mesh):
    in_specs = (
        P("dx", "dy", None, None),
        P("dx", "dy", None, None, None),
        P("dx", "dy", None, None),
    )
    out_specs = P("dx", "dy", None, None)
    return jax.shard_map(shards, mesh=mesh, in_specs=in_specs, out_specs=out_specs, check_vma=False)
```
